32 devices in a mesh: member: 2 (over core), space: 16 (over z, y, x).
Axes of the slice: x: 2, y: 2, z: 4, core: 2. Of those that a mesh axis runs over, the one named last changes fastest.
Arguments:
- state: float32 [64, 2, 1024, 512], P('member', None, 'space'), may hold values from -6 to 6
- courant: float32 [2, 1024, 512], P(None, 'space'), may hold values from -0.3 to 0.3
- diffusion: float32 [2, 1024, 512], P(None, 'space'), may hold values from 0.02 to 0.1
- obs_cells: int32 [8, 512], replicated, may hold values from 0 to 32767
- obs_owner: int32 [8], replicated, may hold values from 0 to 15
- batch_order: int32 [8], replicated, may hold values from 0 to 7, each once
- obs_values: float32 [8, 64, 512], replicated, may hold values from -8 to 8
- obs_error: float32 [8, 512], replicated, may hold values from 0.5 to 2
Outputs:
- analysis: float32 [64, 2, 1024, 512], P(None, None, 'space', 'member')
The draws below stay inside these ranges and needn't reach their ends.
All inputs are finite; a program needn't handle non-finite values.
Results may differ from the reference program's by a relative error of at most 0.0003.
Values sent between devices are 32-bit elements; how exact they have to be, the bound alone decides.
No kernel may reach another device: no remote copies, remote signals or barrier semaphores. Data moves between devices by JAX's collectives and lax.ppermute only.
A program may use at most 128 MiB of HBM per device.

```python
import math
import jax
import jax.numpy as jnp
from jax import lax

M = 64
NOBS = 512
BATCHES = 8
CX = 64
NX = 1024
NY = 512
N_SPACE = 16


def draw_obs_owner(key, part):
    key = jax.random.fold_in(key, 11)
    return jax.random.randint(key, (BATCHES,), 0, N_SPACE).astype(jnp.int32)


def draw_obs_cells(key, part):
    key = jax.random.fold_in(key, 3)
    key_rows, key_cols = jax.random.split(key)
    rows_in = jax.random.randint(key_rows, (BATCHES, NOBS), 0, CX).astype(jnp.int32)
    columns = jax.random.randint(key_cols, (BATCHES, NOBS), 0, NY).astype(jnp.int32)
    return (rows_in * NY + columns).astype(jnp.int32)


def block_scale(own_key, shape, shards, least, top_value):
    gain = 1.0
    for axis_at, blocks in shards:
        steps = jax.random.uniform(jax.random.fold_in(jax.random.fold_in(own_key, 6), axis_at), (blocks,), jnp.float32, least / len(shards), top_value / len(shards))
        gain = gain * jnp.repeat(jnp.exp(steps), shape[axis_at] // blocks).reshape((-1,) + (1,) * (len(shape) - 1 - axis_at))
    return gain


def centred(rng, dims, width, bound, shards=(), kind=jnp.bfloat16):
    drawn = jax.random.normal(rng, dims, jnp.float32) * width
    if len(shards) > 0:
        drawn = block_scale(rng, dims, shards, -0.22, 0.18) * drawn
    return jnp.clip(drawn, min=-bound, max=bound).astype(kind)


def setup_inputs(seed: int = 0) -> dict:
    keys = jax.random.split(jax.random.key(seed), 9)
    return {
        "state": centred(keys[0], (M, 2, NX, NY), 1.0, 6.0, ((0, 2), (2, 16)), jnp.float32),
        "courant": jnp.clip(jax.random.uniform(keys[1], (2, NX, NY), jnp.float32, -0.3, 0.3) * block_scale(keys[1], (2, NX, NY), ((1, 16),), -0.4, 0.0), -0.3, 0.3),
        "diffusion": jnp.clip(jnp.exp(math.log(0.1) - 1.609438 * jax.random.uniform(keys[2], (2, NX, NY), jnp.float32) ** block_scale(keys[2], (2, NX, NY), ((1, 16),), -0.2, 0.2)), 0.02, 0.1),
        "obs_cells": draw_obs_cells(jax.random.fold_in(keys[8], 71), 0),
        "obs_owner": draw_obs_owner(jax.random.fold_in(keys[8], 71), 0),
        "batch_order": jax.random.permutation(keys[5], BATCHES).astype(jnp.int32),
        "obs_values": centred(keys[6], (BATCHES, M, NOBS), 1.5, 8.0, (), jnp.float32),
        "obs_error": jnp.clip(jnp.exp(jax.random.uniform(keys[7], (BATCHES, NOBS), jnp.float32, math.log(0.5), math.log(2.0))), 0.5, 2.0),
    }


HIGH = lax.Precision.HIGHEST

def advance(padded, flow_x, flow_y, diffuse):
    center = padded[..., 1:-1, 1:-1]
    western = padded[..., :-2, 1:-1]
    eastern = padded[..., 2:, 1:-1]
    southern = padded[..., 1:-1, :-2]
    northern = padded[..., 1:-1, 2:]
    upwind = jnp.maximum(flow_x, 0.0) * (center - western) + jnp.minimum(flow_x, 0.0) * (eastern - center)
    upwind = upwind + jnp.maximum(flow_y, 0.0) * (center - southern) + jnp.minimum(flow_y, 0.0) * (northern - center)
    return center - upwind + diffuse * (eastern + western + northern + southern - 4.0 * center)

def batch_transform(prior_ens, observed, obs_var):
    members = prior_ens.shape[0]
    anomaly = prior_ens - jnp.mean(prior_ens, axis=0, keepdims=True)
    inverse_var = 1.0 / obs_var
    scaled_misfit = (observed - prior_ens).T * inverse_var[:, None]
    scaled_anom = anomaly * inverse_var[None, :]
    inner = jnp.dot(scaled_anom, anomaly.T, precision=HIGH) + (members - 1) * jnp.eye(members, dtype=jnp.float32)
    lower_factor = jnp.linalg.cholesky(inner)
    projected = jnp.dot(anomaly, scaled_misfit, precision=HIGH)
    half_solved = lax.linalg.triangular_solve(lower_factor, projected, left_side=True, lower=True)
    inner_solved = lax.linalg.triangular_solve(lower_factor, half_solved, left_side=True, lower=True, transpose_a=True)
    solved = scaled_misfit - jnp.dot(scaled_anom.T, inner_solved, precision=HIGH)
    weights = jnp.dot(anomaly, solved, precision=HIGH) / (members - 1)
    return jnp.eye(members, dtype=jnp.float32) + weights - jnp.mean(weights, axis=0, keepdims=True)

def reference(state, courant, diffusion, obs_cells, obs_owner, batch_order, obs_values, obs_error):
    fields = state
    for turn in range(2):
        padded = jnp.pad(fields, ((0, 0), (0, 0), (1, 1), (1, 1)))
        fields = advance(padded, courant[0], courant[1], diffusion)
    members = fields.shape[0]
    for position in range(BATCHES):
        batch_id = batch_order[position]
        cells = (obs_owner[batch_id] * (CX * NY) + obs_cells[batch_id]).astype(jnp.int32)
        flat = fields[:, 0].reshape(members, -1)
        prior_ens = jnp.take(flat, cells, axis=1)
        transform = batch_transform(prior_ens, obs_values[batch_id], obs_error[batch_id])
        whole = fields.reshape(members, -1)
        fields = jnp.dot(transform.T, whole, precision=HIGH).reshape(state.shape)
    return fields
```

```python
import functools

import jax
import jax.numpy as jnp
from jax import lax
from jax.experimental import pallas as pl
from jax.experimental.pallas import tpu as pltpu
from jax.sharding import PartitionSpec as P

HIGH = lax.Precision.HIGHEST
F32 = jnp.float32
BF16 = jnp.bfloat16
LANES = 128
SUB = 8
PACK = 8
VMEM_LIMIT = 56 * 1024 * 1024


def params(**kw):
    return pltpu.CompilerParams(vmem_limit_bytes=VMEM_LIMIT, **kw)


def tiled(array):
    *lead, rows, cols = array.shape
    n = len(lead)
    split = array.reshape(*lead, rows // SUB, SUB, cols // LANES, LANES)
    return jnp.transpose(split, (*range(n), n, n + 2, n + 1, n + 3))


def untiled(array):
    *lead, r8, ct, sub, lanes = array.shape
    n = len(lead)
    back = jnp.transpose(array, (*range(n), n, n + 2, n + 1, n + 3))
    return back.reshape(*lead, r8 * sub, ct * lanes)


def pack_kernel(first, last, flow_first, flow_last, nu_first, nu_last, *outs):
    members = first.shape[0]
    fields = first.shape[1]
    nct = first.shape[3]
    up, down = outs[:fields], outs[fields:]
    for field in range(fields):
        for msg, src, flow, nu, rows, edge in (
            (up[field], last, flow_last, nu_last, (SUB - 2, SUB - 1), SUB - 1),
            (down[field], first, flow_first, nu_first, (0, 1), 0),
        ):
            flat = src.reshape(members * fields * nct * SUB, LANES)
            for ct in range(nct):
                for at, row in enumerate(rows):
                    start = (field * nct + ct) * SUB + row
                    msg[ct, pl.ds(at * members, members), :] = flat[
                        pl.ds(start, members, stride=fields * nct * SUB), :
                    ]
                extra = jnp.concatenate(
                    [
                        flow[0, 0, ct, edge : edge + 1, :],
                        flow[1, 0, ct, edge : edge + 1, :],
                        nu[field, 0, ct, edge : edge + 1, :],
                        jnp.zeros((PACK - 3, LANES), F32),
                    ],
                    axis=0,
                )
                msg[ct, pl.ds(2 * members, PACK), :] = extra


def pack_edges(state6, flow5, nu5):
    members, fields, r8, nct = state6.shape[:4]
    msg = jax.ShapeDtypeStruct((nct, 2 * members + PACK, LANES), F32)
    last = r8 - 1

    def state_block(at):
        return pl.BlockSpec((members, fields, 1, nct, SUB, LANES), lambda i: (0, 0, at, 0, 0, 0))

    def row_block(at):
        return pl.BlockSpec((2, 1, nct, SUB, LANES), lambda i: (0, at, 0, 0, 0))

    return pl.pallas_call(
        pack_kernel,
        grid=(1,),
        out_shape=[msg] * (2 * fields),
        in_specs=[
            state_block(0), state_block(last), row_block(0), row_block(last),
            row_block(0), row_block(last),
        ],
        out_specs=[pl.BlockSpec(msg.shape, lambda i: (0, 0, 0))] * (2 * fields),
        compiler_params=params(),
        name="pack_edges",
    )(state6, state6, flow5, flow5, nu5, nu5)


def stencil_coefs(flow_x, flow_y, nu, col, width):
    east = nu - jnp.minimum(flow_x, 0.0)
    west = nu + jnp.maximum(flow_x, 0.0)
    north = nu - jnp.minimum(flow_y, 0.0)
    south = nu + jnp.maximum(flow_y, 0.0)
    centre = 1.0 - (east + west + north + south)
    south = jnp.where(col == 0, 0.0, south)
    north = jnp.where(col == width - 1, 0.0, north)
    return centre, west, east, south, north


def stencil_row(src, row, dst, coef, members):
    nct = src.shape[1]
    lane = lax.broadcasted_iota(jnp.int32, (SUB, LANES), 1)
    first, last = lane == 0, lane == LANES - 1
    weights = [
        [jnp.broadcast_to(coef[k, ct, pl.ds(row, 1), :], (SUB, LANES)) for k in range(5)]
        for ct in range(nct)
    ]
    for group in range(members // SUB):
        rows = pl.ds(group * SUB, SUB)
        mid = [src[row + 1, ct, rows, :] for ct in range(nct)]
        right = [pltpu.roll(x, 1, 1) for x in mid]
        left = [pltpu.roll(x, LANES - 1, 1) for x in mid]
        for ct in range(nct):
            south = jnp.where(first, right[(ct - 1) % nct], right[ct])
            north = jnp.where(last, left[(ct + 1) % nct], left[ct])
            centre, west, east, w_s, w_n = weights[ct]
            value = (
                centre * mid[ct]
                + west * src[row, ct, rows, :]
                + east * src[row + 2, ct, rows, :]
                + (w_s * south + w_n * north)
            )
            dst(ct, rows, value)


def forecast_kernel(
    gather, ids, cells, owner, order, state, flow, nu, before, after, *rest
):
    if gather:
        own, send, keep, away, q0, q1, coef = rest
    else:
        own, send, q0, q1, coef = rest
    members, _, r8, nct = state.shape[:4]
    rows = r8 * SUB
    half = nct // 2
    width = nct * LANES
    slab, member = ids[0], ids[1]
    flat = state.reshape(members * r8 * nct * SUB, LANES)

    def phys(ct):
        return lax.rem(ct + member * half, nct)

    for ct in range(nct):
        at = phys(ct)
        col = lax.broadcasted_iota(jnp.int32, (rows, LANES), 1) + at * LANES
        flow_x = flow[0, :, at, :, :].reshape(rows, LANES)
        flow_y = flow[1, :, at, :, :].reshape(rows, LANES)
        diffuse = nu[0, :, at, :, :].reshape(rows, LANES)
        for k, value in enumerate(stencil_coefs(flow_x, flow_y, diffuse, col, width)):
            coef[k, ct, pl.ds(SUB, rows), :] = value
        for msg, row in ((before, SUB - 1), (after, SUB + rows)):
            base = 2 * members
            edge = [msg[at, pl.ds(base + k, 1), :] for k in range(3)]
            for k, value in enumerate(stencil_coefs(*edge, col[0:1], width)):
                coef[k, ct, pl.ds(row, 1), :] = value

    for ct in range(nct):
        at = phys(ct)
        for k in range(2):
            q0[k, ct] = before[at, pl.ds(k * members, members), :]
            q0[rows + 2 + k, ct] = after[at, pl.ds(k * members, members), :]

    def load(r, carry):
        for ct in range(nct):
            start = (lax.div(r, SUB) * nct + phys(ct)) * SUB + lax.rem(r, SUB)
            q0[r + 2, ct] = flat[pl.ds(start, members, stride=r8 * nct * SUB), :]
        return carry

    lax.fori_loop(0, rows, load, 0)

    def first_step(r, carry):
        def put(ct, at, value):
            q1[r, ct, at, :] = value

        stencil_row(q0, r, put, coef.at[:, :, pl.ds(SUB - 1, rows + 2)], members)
        return carry

    lax.fori_loop(0, rows + 2, first_step, 0)

    def second_step(r, carry):
        def put(ct, at, value):
            if ct < half:
                own[r, ct, at, :] = value
            else:
                send[r, ct - half, at, :] = value
            if gather:
                q0[r, ct, at, :] = value

        stencil_row(q1, r, put, coef.at[:, :, pl.ds(SUB, rows)], members)
        return carry

    lax.fori_loop(0, rows, second_step, 0)

    if not gather:
        return
    nobs = cells.shape[1]
    lane = lax.broadcasted_iota(jnp.int32, (members, LANES), 1)
    for position in range(order.shape[0]):
        batch = order[position]
        mine = owner[batch] == slab
        kept = lax.rem(position, 2) == member

        def pick(tile, carry, batch=batch, mine=mine, kept=kept, position=position):
            def one(o, acc):
                cell = cells[batch, tile * LANES + o]
                r = lax.div(cell, width)
                c = lax.rem(cell, width)
                at = lax.rem(lax.div(c, LANES) + member * half, nct)
                shift = lax.rem(o - lax.rem(c, LANES) + LANES, LANES)
                moved = pltpu.roll(q0[r, at], shift, 1)
                return jnp.where(lane == o, moved, acc)

            count = jnp.where(mine, LANES, 0)
            acc = lax.fori_loop(0, count // 8, lambda g, a: functools.reduce(
                lambda v, u: one(g * 8 + u, v), range(8), a), jnp.zeros((members, LANES), F32))

            @pl.when(kept)
            def _():
                keep[position // 2, tile] = acc

            @pl.when(jnp.logical_not(kept))
            def _():
                away[position // 2, tile] = acc

            return carry

        lax.fori_loop(0, nobs // LANES, pick, 0)


def forecast(field, gather, ids, cells, owner, order, state6, flow5, nu5, before, after):
    members, fields, r8, nct = state6.shape[:4]
    rows = r8 * SUB
    half = nct // 2
    part = jax.ShapeDtypeStruct((rows, half, members, LANES), F32)
    out_shape = [part, part]
    if gather:
        nb, nobs = cells.shape
        picks = jax.ShapeDtypeStruct((nb // 2, nobs // LANES, members, LANES), F32)
        out_shape += [picks, picks]
    msg = pl.BlockSpec(before.shape, lambda i, *s: (0, 0, 0))
    cells_n = rows * nct * members * LANES
    return pl.pallas_call(
        functools.partial(forecast_kernel, gather),
        out_shape=out_shape,
        grid_spec=pltpu.PrefetchScalarGridSpec(
            num_scalar_prefetch=4,
            grid=(1,),
            in_specs=[
                pl.BlockSpec((members, 1, r8, nct, SUB, LANES), lambda i, *s: (0, field, 0, 0, 0, 0)),
                pl.BlockSpec((2, r8, nct, SUB, LANES), lambda i, *s: (0, 0, 0, 0, 0)),
                pl.BlockSpec((1, r8, nct, SUB, LANES), lambda i, *s: (field, 0, 0, 0, 0)),
                msg,
                msg,
            ],
            out_specs=[
                pl.BlockSpec(o.shape, lambda i, *s: (0, 0, 0, 0)) for o in out_shape
            ],
            scratch_shapes=[
                pltpu.VMEM((rows + 4, nct, members, LANES), F32),
                pltpu.VMEM((rows + 2, nct, members, LANES), F32),
                pltpu.VMEM((5, nct, rows + 2 * SUB, LANES), F32),
            ],
        ),
        compiler_params=params(),
        cost_estimate=pl.CostEstimate(
            flops=40 * cells_n, bytes_accessed=8 * cells_n, transcendentals=0
        ),
        name="forecast_gather" if gather else "forecast",
    )(ids, cells, owner, order, state6, flow5, nu5, before, after)


def gram_kernel(ids, owner, order, keep, other, observed, variance, out):
    slab, member = ids[0], ids[1]
    count, tiles, members = keep.shape[:3]
    for k in range(count):
        batch = order[2 * k + member]
        mine = owner[batch] == slab

        @pl.when(jnp.logical_not(mine))
        def _():
            out[k] = jnp.zeros(out.shape[1:], F32)

        @pl.when(mine)
        def _():
            total = jnp.zeros(out.shape[1:], F32)
            for t in range(tiles):
                a, b = keep[k, t], other[k, t]
                prior = jnp.concatenate(
                    [jnp.where(member == 0, a, b), jnp.where(member == 0, b, a)], axis=0
                )
                mean = jnp.sum(prior, axis=0, keepdims=True) / (2 * members)
                anomaly = prior - mean
                scaled = anomaly / variance[batch, :, pl.ds(t * LANES, LANES)]
                misfit = observed[batch, :, pl.ds(t * LANES, LANES)] - mean
                total += lax.dot_general(
                    scaled,
                    jnp.concatenate([anomaly, misfit], axis=0),
                    (((1,), (1,)), ((), ())),
                    precision=HIGH,
                    preferred_element_type=F32,
                )
            out[k] = total


def gram(ids, owner, order, keep, other, observed, variance):
    count, _, members, _ = keep.shape
    total = 2 * members
    smem = pl.BlockSpec(memory_space=pltpu.SMEM)
    vmem = pl.BlockSpec(memory_space=pltpu.VMEM)
    return pl.pallas_call(
        gram_kernel,
        out_shape=jax.ShapeDtypeStruct((count, total, 2 * total), F32),
        in_specs=[smem] * 3 + [vmem] * 4,
        out_specs=vmem,
        compiler_params=params(),
        name="gram",
    )(ids, owner, order, keep, other, observed, variance[:, None, :])


def solve(inner, rhs):
    size = inner.shape[0]
    groups = size // SUB
    wide = (SUB, LANES)
    sub = lax.broadcasted_iota(jnp.int32, wide, 0)
    a = [inner[g * SUB : (g + 1) * SUB] for g in range(groups)]
    b = [rhs[g * SUB : (g + 1) * SUB] for g in range(groups)]

    def column(x, k):
        return jnp.broadcast_to(x[:, k : k + 1], wide)

    def row(x, k):
        return jnp.broadcast_to(x[k : k + 1, :], wide)

    for p in range(groups):
        cols = [[column(a[g], p * SUB + k) for k in range(SUB)] for g in range(groups)]
        c, pa, pb = cols[p], a[p], b[p]
        for k in range(SUB):
            here = sub == k
            scale = 1.0 / row(c[k], k)
            for j in range(k + 1, SUB):
                t = row(c[j], k) * scale
                c[j] = jnp.where(here, t, c[j] - c[k] * t)
            ra, rb = row(pa, k) * scale, row(pb, k) * scale
            pa = jnp.where(here, ra, pa - c[k] * ra)
            pb = jnp.where(here, rb, pb - c[k] * rb)
        a[p], b[p] = pa, pb
        ra = [row(pa, k) for k in range(SUB)]
        rb = [row(pb, k) for k in range(SUB)]
        for g in range(groups):
            if g == p:
                continue
            for k in range(SUB):
                if p + 1 < groups:
                    a[g] = a[g] - cols[g][k] * ra[k]
                b[g] = b[g] - cols[g][k] * rb[k]
    return jnp.concatenate(b, axis=0)


def chain_kernel(ids, mine, other, out):
    member = ids[1]
    count, size, _ = mine.shape
    eye = (
        lax.broadcasted_iota(jnp.int32, (size, 2 * size), 0)
        == lax.broadcasted_iota(jnp.int32, (size, 2 * size), 1)
    ).astype(F32)
    unit = eye[:, :size]

    def dot(x, y, lhs=1):
        return lax.dot_general(
            x, y, (((lhs,), (0,)), ((), ())), precision=HIGH, preferred_element_type=F32
        )

    def step(position, v):
        k = lax.div(position, 2)
        gh = jnp.where(lax.rem(position, 2) == member, mine[k], other[k])
        g, h = gh[:, :size], gh[:, size:]
        centred = h - jnp.sum(h, axis=1, keepdims=True) / size
        z = v[:, :size]
        gv = dot(g, v)
        both = dot(z, jnp.concatenate([gv, centred, h], axis=1), lhs=0)
        inner = both[:, : 2 * size] + (size - 1) * eye
        rhs = both[:, 2 * size :] - both[:, : 2 * size]
        return v + dot(z, solve(inner, rhs))

    start = jnp.concatenate([unit - 1.0 / size, unit], axis=1)
    v = lax.fori_loop(0, 2 * count, step, start)
    w = v[:, size:].T
    half = size // 2
    first, second = w[:, :half], w[:, half:]
    w = jnp.concatenate(
        [jnp.where(member == 0, first, second), jnp.where(member == 0, second, first)], axis=1
    )
    high = w.astype(BF16).astype(F32)
    low = w - high
    out[...] = jnp.concatenate([high, high, low], axis=1)


def chain(ids, mine, other):
    count, size, _ = mine.shape
    smem = pl.BlockSpec(memory_space=pltpu.SMEM)
    vmem = pl.BlockSpec(memory_space=pltpu.VMEM)
    return pl.pallas_call(
        chain_kernel,
        out_shape=jax.ShapeDtypeStruct((size, 3 * size), F32),
        in_specs=[smem, vmem, vmem],
        out_specs=vmem,
        compiler_params=params(),
        name="chain",
    )(ids, mine, other)


def apply_kernel(w_ref, own0, other0, own1, other1, out):
    field = pl.program_id(0)
    size = w_ref.shape[0]
    rows, half = own0.shape[:2]
    weights = w_ref[...].astype(BF16)
    flat = out.reshape(size * half * rows, LANES)

    def run(own, other):
        for r in range(rows):
            parts = [
                jnp.concatenate([src[r, ct] for ct in range(half)], axis=1) for src in (own, other)
            ]
            high = [x.astype(BF16) for x in parts]
            low = [(x - y.astype(F32)).astype(BF16) for x, y in zip(parts, high)]
            stacked = jnp.concatenate([*high, *low, *high], axis=0)
            result = jnp.dot(weights, stacked, preferred_element_type=F32)
            for ct in range(half):
                flat[pl.ds(ct * rows + r, size, stride=half * rows), :] = result[
                    :, ct * LANES : (ct + 1) * LANES
                ]

    @pl.when(field == 0)
    def _():
        run(own0, other0)

    @pl.when(field == 1)
    def _():
        run(own1, other1)


def apply(weights, own0, other0, own1, other1):
    rows, half, members, _ = own0.shape
    size = 2 * members
    r8 = rows // SUB
    block = (SUB, half, members, LANES)
    zero = pl.BlockSpec(block, lambda f, r: (jnp.where(f == 0, r, r8 - 1), 0, 0, 0))
    one = pl.BlockSpec(block, lambda f, r: (jnp.where(f == 1, r, 0), 0, 0, 0))
    return pl.pallas_call(
        apply_kernel,
        grid=(2, r8),
        out_shape=jax.ShapeDtypeStruct((size, 2, r8, half, SUB, LANES), F32),
        in_specs=[
            pl.BlockSpec(weights.shape, lambda f, r: (0, 0)), zero, zero, one, one,
        ],
        out_specs=pl.BlockSpec((size, 1, 1, half, SUB, LANES), lambda f, r: (0, f, r, 0, 0, 0)),
        compiler_params=params(),
        name="apply",
    )(weights, own0, other0, own1, other1)


def body(state, courant, diffusion, obs_cells, obs_owner, batch_order, obs_values, obs_error):
    slab = lax.axis_index("space")
    member = lax.axis_index("member")
    space = lax.axis_size("space")
    ids = jnp.stack([slab, member]).astype(jnp.int32)
    up = [(i, i + 1) for i in range(space - 1)]
    down = [(i + 1, i) for i in range(space - 1)]
    swap = [(0, 1), (1, 0)]

    state6, flow5, nu5 = tiled(state), tiled(courant), tiled(diffusion)
    up0, up1, down0, down1 = pack_edges(state6, flow5, nu5)
    before0 = lax.ppermute(up0, "space", up)
    after0 = lax.ppermute(down0, "space", down)
    before1 = lax.ppermute(up1, "space", up)
    after1 = lax.ppermute(down1, "space", down)

    scalars = (ids, obs_cells, obs_owner, batch_order)
    own0, send0, keep, away = forecast(0, True, *scalars, state6, flow5, nu5, before0, after0)
    other = lax.ppermute(away, "member", swap)
    gh = gram(ids, obs_owner, batch_order, keep, other, obs_values, obs_error)
    own1, send1 = forecast(1, False, *scalars, state6, flow5, nu5, before1, after1)
    other0 = lax.ppermute(send0, "member", swap)
    other1 = lax.ppermute(send1, "member", swap)
    bit = 1
    while bit < space:
        gh = gh + lax.ppermute(gh, "space", [(i, i ^ bit) for i in range(space)])
        bit *= 2
    theirs = lax.ppermute(gh, "member", swap)
    weights = chain(ids, gh, theirs)
    return untiled(apply(weights, own0, other0, own1, other1))


def solution(mesh):
    placed = (
        P("member", None, "space", None),
        P(None, "space", None),
        P(None, "space", None),
        P(),
        P(),
        P(),
        P(),
        P(),
    )
    return jax.shard_map(
        body,
        mesh=mesh,
        in_specs=placed,
        out_specs=P(None, None, "space", "member"),
        check_vma=False,
    )
```

```python
import functools

import jax
import jax.numpy as jnp
from jax import lax
from jax.experimental import pallas as pl
from jax.experimental.pallas import tpu as pltpu
from jax.sharding import PartitionSpec as P

HIGH = lax.Precision.HIGHEST
F32 = jnp.float32
BF16 = jnp.bfloat16
LANES = 128
SUB = 8
GATHER = 32
PACK = 8


def params(mib):
    return pltpu.CompilerParams(vmem_limit_bytes=mib * 1024 * 1024)


def unrolled(count, most):
    return max(d for d in range(1, most + 1) if count % d == 0)


def rows_loop(count, most, fn):
    step = unrolled(count, most)

    def run(i, carry):
        for u in range(step):
            fn(i * step + u)
        return carry

    lax.fori_loop(0, count // step, run, 0)


def tiled(array):
    *lead, rows, cols = array.shape
    n = len(lead)
    split = array.reshape(*lead, rows // SUB, SUB, cols // LANES, LANES)
    return jnp.transpose(split, (*range(n), n, n + 2, n + 1, n + 3))


def untiled(array):
    *lead, r8, ct, sub, lanes = array.shape
    n = len(lead)
    back = jnp.transpose(array, (*range(n), n, n + 2, n + 1, n + 3))
    return back.reshape(*lead, r8 * sub, ct * lanes)


def pack_kernel(first, last, flow_first, flow_last, nu_first, nu_last, *outs):
    members = first.shape[0]
    fields = first.shape[1]
    nct = first.shape[3]
    up, down = outs[:fields], outs[fields:]
    for field in range(fields):
        for msg, src, flow, nu, rows, edge in (
            (up[field], last, flow_last, nu_last, (SUB - 2, SUB - 1), SUB - 1),
            (down[field], first, flow_first, nu_first, (0, 1), 0),
        ):
            flat = src.reshape(members * fields * nct * SUB, LANES)
            for ct in range(nct):
                for at, row in enumerate(rows):
                    start = (field * nct + ct) * SUB + row
                    msg[ct, pl.ds(at * members, members), :] = flat[
                        pl.ds(start, members, stride=fields * nct * SUB), :
                    ]
                extra = jnp.concatenate(
                    [
                        flow[0, 0, ct, edge : edge + 1, :],
                        flow[1, 0, ct, edge : edge + 1, :],
                        nu[field, 0, ct, edge : edge + 1, :],
                        jnp.zeros((PACK - 3, LANES), F32),
                    ],
                    axis=0,
                )
                msg[ct, pl.ds(2 * members, PACK), :] = extra


def pack_edges(state6, flow5, nu5):
    members, fields, r8, nct = state6.shape[:4]
    msg = jax.ShapeDtypeStruct((nct, 2 * members + PACK, LANES), F32)
    last = r8 - 1

    def state_block(at):
        return pl.BlockSpec((members, fields, 1, nct, SUB, LANES), lambda i: (0, 0, at, 0, 0, 0))

    def row_block(at):
        return pl.BlockSpec((2, 1, nct, SUB, LANES), lambda i: (0, at, 0, 0, 0))

    return pl.pallas_call(
        pack_kernel,
        grid=(1,),
        out_shape=[msg] * (2 * fields),
        in_specs=[
            state_block(0), state_block(last), row_block(0), row_block(last),
            row_block(0), row_block(last),
        ],
        out_specs=[pl.BlockSpec(msg.shape, lambda i: (0, 0, 0))] * (2 * fields),
        compiler_params=params(60),
        name="pack_edges",
    )(state6, state6, flow5, flow5, nu5, nu5)


def stencil_coefs(flow_x, flow_y, nu, col, width):
    east = nu - jnp.minimum(flow_x, 0.0)
    west = nu + jnp.maximum(flow_x, 0.0)
    north = nu - jnp.minimum(flow_y, 0.0)
    south = nu + jnp.maximum(flow_y, 0.0)
    centre = 1.0 - (east + west + north + south)
    south = jnp.where(col == 0, 0.0, south)
    north = jnp.where(col == width - 1, 0.0, north)
    return centre, west, east, south, north


def stencil_row(src, row, dst, coef, members):
    nct = src.shape[1]
    lane = lax.broadcasted_iota(jnp.int32, (SUB, LANES), 1)
    first, last = lane == 0, lane == LANES - 1
    weights = [
        [jnp.broadcast_to(coef[k, ct, pl.ds(row, 1), :], (SUB, LANES)) for k in range(5)]
        for ct in range(nct)
    ]
    for group in range(members // SUB):
        rows = pl.ds(group * SUB, SUB)
        mid = [src[row + 1, ct, rows, :] for ct in range(nct)]
        right = [pltpu.roll(x, 1, 1) for x in mid]
        left = [pltpu.roll(x, LANES - 1, 1) for x in mid]
        for ct in range(nct):
            south = jnp.where(first, right[(ct - 1) % nct], right[ct])
            north = jnp.where(last, left[(ct + 1) % nct], left[ct])
            centre, west, east, w_s, w_n = weights[ct]
            value = (
                centre * mid[ct]
                + west * src[row, ct, rows, :]
                + east * src[row + 2, ct, rows, :]
                + (w_s * south + w_n * north)
            )
            dst(ct, rows, value)


def forecast_kernel(
    gather, ids, cells, owner, order, state, flow, nu, before, after, *rest
):
    if gather:
        own, send, keep, away, q0, q1, coef = rest
    else:
        own, send, q0, q1, coef = rest
    members, _, r8, nct = state.shape[:4]
    rows = r8 * SUB
    half = nct // 2
    width = nct * LANES
    slab, member = ids[0], ids[1]
    flat = state.reshape(members * r8 * nct * SUB, LANES)

    def phys(ct):
        return lax.rem(ct + member * half, nct)

    for ct in range(nct):
        at = phys(ct)
        col = lax.broadcasted_iota(jnp.int32, (rows, LANES), 1) + at * LANES
        flow_x = flow[0, :, at, :, :].reshape(rows, LANES)
        flow_y = flow[1, :, at, :, :].reshape(rows, LANES)
        diffuse = nu[0, :, at, :, :].reshape(rows, LANES)
        for k, value in enumerate(stencil_coefs(flow_x, flow_y, diffuse, col, width)):
            coef[k, ct, pl.ds(SUB, rows), :] = value
        for msg, row in ((before, SUB - 1), (after, SUB + rows)):
            base = 2 * members
            edge = [msg[at, pl.ds(base + k, 1), :] for k in range(3)]
            for k, value in enumerate(stencil_coefs(*edge, col[0:1], width)):
                coef[k, ct, pl.ds(row, 1), :] = value

    for ct in range(nct):
        at = phys(ct)
        for k in range(2):
            q0[k, ct] = before[at, pl.ds(k * members, members), :]
            q0[rows + 2 + k, ct] = after[at, pl.ds(k * members, members), :]

    def load(block, carry):
        for sub in range(SUB):
            for ct in range(nct):
                start = (block * nct + phys(ct)) * SUB + sub
                q0[block * SUB + sub + 2, ct] = flat[
                    pl.ds(start, members, stride=r8 * nct * SUB), :
                ]
        return carry

    lax.fori_loop(0, r8, load, 0)

    def first_step(r):
        def put(ct, at, value):
            q1[r, ct, at, :] = value

        stencil_row(q0, r, put, coef.at[:, :, pl.ds(SUB - 1, rows + 2)], members)

    rows_loop(rows + 2, 6, first_step)

    def second_step(r):
        def put(ct, at, value):
            if ct < half:
                own[r, ct, at, :] = value
            else:
                send[r, ct - half, at, :] = value
            if gather:
                q0[r, ct, at, :] = value

        stencil_row(q1, r, put, coef.at[:, :, pl.ds(SUB, rows)], members)

    rows_loop(rows, 4, second_step)

    if not gather:
        return
    nobs = cells.shape[1]
    bits = width.bit_length() - 1
    assert width == 1 << bits
    lane = lax.broadcasted_iota(jnp.int32, (members, LANES), 1)
    for position in range(order.shape[0]):
        batch = order[position]
        mine = owner[batch] == slab
        kept = lax.rem(position, 2) == member

        def pick(tile, carry, batch=batch, mine=mine, kept=kept, position=position):
            def some(group, acc):
                for u in range(GATHER):
                    o = group * GATHER + u
                    cell = cells[batch, tile * LANES + o]
                    r = lax.shift_right_logical(cell, bits)
                    c = cell & (width - 1)
                    at = (lax.shift_right_logical(c, 7) + member * half) & (nct - 1)
                    moved = pltpu.roll(q0[r, at], (o - c) & (LANES - 1), 1)
                    acc = jnp.where(lane == o, moved, acc)
                return acc

            acc = lax.fori_loop(
                0, jnp.where(mine, LANES // GATHER, 0), some, jnp.zeros((members, LANES), F32)
            )

            @pl.when(kept)
            def _():
                keep[position // 2, tile] = acc

            @pl.when(jnp.logical_not(kept))
            def _():
                away[position // 2, tile] = acc

            return carry

        lax.fori_loop(0, nobs // LANES, pick, 0)


def forecast(field, gather, ids, cells, owner, order, state6, flow5, nu5, before, after):
    members, fields, r8, nct = state6.shape[:4]
    rows = r8 * SUB
    half = nct // 2
    part = jax.ShapeDtypeStruct((rows, half, members, LANES), F32)
    out_shape = [part, part]
    if gather:
        nb, nobs = cells.shape
        picks = jax.ShapeDtypeStruct((nb // 2, nobs // LANES, members, LANES), F32)
        out_shape += [picks, picks]
    msg = pl.BlockSpec(before.shape, lambda i, *s: (0, 0, 0))
    cells_n = rows * nct * members * LANES
    return pl.pallas_call(
        functools.partial(forecast_kernel, gather),
        out_shape=out_shape,
        grid_spec=pltpu.PrefetchScalarGridSpec(
            num_scalar_prefetch=4,
            grid=(1,),
            in_specs=[
                pl.BlockSpec((members, 1, r8, nct, SUB, LANES), lambda i, *s: (0, field, 0, 0, 0, 0)),
                pl.BlockSpec((2, r8, nct, SUB, LANES), lambda i, *s: (0, 0, 0, 0, 0)),
                pl.BlockSpec((1, r8, nct, SUB, LANES), lambda i, *s: (field, 0, 0, 0, 0)),
                msg,
                msg,
            ],
            out_specs=[
                pl.BlockSpec(o.shape, lambda i, *s: (0, 0, 0, 0)) for o in out_shape
            ],
            scratch_shapes=[
                pltpu.VMEM((rows + 4, nct, members, LANES), F32),
                pltpu.VMEM((rows + 2, nct, members, LANES), F32),
                pltpu.VMEM((5, nct, rows + 2 * SUB, LANES), F32),
            ],
        ),
        compiler_params=params(32),
        cost_estimate=pl.CostEstimate(
            flops=40 * cells_n, bytes_accessed=8 * cells_n, transcendentals=0
        ),
        name="forecast_gather" if gather else "forecast",
    )(ids, cells, owner, order, state6, flow5, nu5, before, after)


def gram_kernel(ids, owner, order, keep, other, observed, variance, out):
    slab, member = ids[0], ids[1]
    count, tiles, members = keep.shape[:3]
    for k in range(count):
        batch = order[2 * k + member]
        mine = owner[batch] == slab

        @pl.when(jnp.logical_not(mine))
        def _():
            out[k] = jnp.zeros(out.shape[1:], F32)

        @pl.when(mine)
        def _():
            total = jnp.zeros(out.shape[1:], F32)
            for t in range(tiles):
                a, b = keep[k, t], other[k, t]
                prior = jnp.concatenate(
                    [jnp.where(member == 0, a, b), jnp.where(member == 0, b, a)], axis=0
                )
                mean = jnp.sum(prior, axis=0, keepdims=True) / (2 * members)
                anomaly = prior - mean
                scaled = anomaly / variance[batch, :, pl.ds(t * LANES, LANES)]
                misfit = observed[batch, :, pl.ds(t * LANES, LANES)] - mean
                total += lax.dot_general(
                    scaled,
                    jnp.concatenate([anomaly, misfit], axis=0),
                    (((1,), (1,)), ((), ())),
                    precision=HIGH,
                    preferred_element_type=F32,
                )
            out[k] = total


def gram(ids, owner, order, keep, other, observed, variance):
    count, _, members, _ = keep.shape
    total = 2 * members
    smem = pl.BlockSpec(memory_space=pltpu.SMEM)
    vmem = pl.BlockSpec(memory_space=pltpu.VMEM)
    return pl.pallas_call(
        gram_kernel,
        out_shape=jax.ShapeDtypeStruct((count, total, 2 * total), F32),
        in_specs=[smem] * 3 + [vmem] * 4,
        out_specs=vmem,
        compiler_params=params(12),
        name="gram",
    )(ids, owner, order, keep, other, observed, variance[:, None, :])


def solve(inner, rhs):
    size = inner.shape[0]
    groups = size // SUB
    wide = (SUB, LANES)
    sub = lax.broadcasted_iota(jnp.int32, wide, 0)
    a = [inner[g * SUB : (g + 1) * SUB] for g in range(groups)]
    b = [rhs[g * SUB : (g + 1) * SUB] for g in range(groups)]

    def column(x, k):
        return jnp.broadcast_to(x[:, k : k + 1], wide)

    def row(x, k):
        return jnp.broadcast_to(x[k : k + 1, :], wide)

    for p in range(groups):
        cols = [[column(a[g], p * SUB + k) for k in range(SUB)] for g in range(groups)]
        c, pa, pb = cols[p], a[p], b[p]
        for k in range(SUB):
            here = sub == k
            scale = 1.0 / row(c[k], k)
            for j in range(k + 1, SUB):
                t = row(c[j], k) * scale
                c[j] = jnp.where(here, t, c[j] - c[k] * t)
            ra, rb = row(pa, k) * scale, row(pb, k) * scale
            pa = jnp.where(here, ra, pa - c[k] * ra)
            pb = jnp.where(here, rb, pb - c[k] * rb)
        a[p], b[p] = pa, pb
        ra = [row(pa, k) for k in range(SUB)]
        rb = [row(pb, k) for k in range(SUB)]
        for g in range(groups):
            if g == p:
                continue
            for k in range(SUB):
                if p + 1 < groups:
                    a[g] = a[g] - cols[g][k] * ra[k]
                b[g] = b[g] - cols[g][k] * rb[k]
    return jnp.concatenate(b, axis=0)


def chain_kernel(ids, mine, other, out):
    member = ids[1]
    count, size, _ = mine.shape
    eye = (
        lax.broadcasted_iota(jnp.int32, (size, 2 * size), 0)
        == lax.broadcasted_iota(jnp.int32, (size, 2 * size), 1)
    ).astype(F32)
    unit = eye[:, :size]

    def dot(x, y, lhs=1):
        return lax.dot_general(
            x, y, (((lhs,), (0,)), ((), ())), precision=HIGH, preferred_element_type=F32
        )

    def step(position, v):
        k = lax.div(position, 2)
        gh = jnp.where(lax.rem(position, 2) == member, mine[k], other[k])
        g, h = gh[:, :size], gh[:, size:]
        centred = h - jnp.sum(h, axis=1, keepdims=True) / size
        z = v[:, :size]
        gv = dot(g, v)
        both = dot(z, jnp.concatenate([gv, centred, h], axis=1), lhs=0)
        inner = both[:, : 2 * size] + (size - 1) * eye
        rhs = both[:, 2 * size :] - both[:, : 2 * size]
        return v + dot(z, solve(inner, rhs))

    start = jnp.concatenate([unit - 1.0 / size, unit], axis=1)
    v = lax.fori_loop(0, 2 * count, step, start)
    w = v[:, size:].T
    half = size // 2
    first, second = w[:, :half], w[:, half:]
    w = jnp.concatenate(
        [jnp.where(member == 0, first, second), jnp.where(member == 0, second, first)], axis=1
    )
    high = w.astype(BF16).astype(F32)
    low = w - high
    out[...] = jnp.concatenate(
        [jnp.concatenate([high, high], axis=1), jnp.concatenate([low, jnp.zeros_like(low)], axis=1)],
        axis=0,
    )


def chain(ids, mine, other):
    count, size, _ = mine.shape
    smem = pl.BlockSpec(memory_space=pltpu.SMEM)
    vmem = pl.BlockSpec(memory_space=pltpu.VMEM)
    return pl.pallas_call(
        chain_kernel,
        out_shape=jax.ShapeDtypeStruct((2 * size, 2 * size), F32),
        in_specs=[smem, vmem, vmem],
        out_specs=vmem,
        compiler_params=params(12),
        name="chain",
    )(ids, mine, other)


def apply_kernel(w_ref, own0, other0, own1, other1, out):
    field = pl.program_id(0)
    size = w_ref.shape[0] // 2
    rows, half = own0.shape[:2]
    weights = w_ref[...].astype(BF16)
    flat = out.reshape(size * half * rows, LANES)

    def run(own, other):
        for r in range(rows):
            parts = [
                jnp.concatenate([src[r, ct] for ct in range(half)], axis=1) for src in (own, other)
            ]
            high = [x.astype(BF16) for x in parts]
            low = [(x - y.astype(F32)).astype(BF16) for x, y in zip(parts, high)]
            stacked = jnp.concatenate([*high, *low], axis=0)
            result = jnp.dot(weights, stacked, preferred_element_type=F32)
            result = result[:size] + result[size:]
            for ct in range(half):
                flat[pl.ds(ct * rows + r, size, stride=half * rows), :] = result[
                    :, ct * LANES : (ct + 1) * LANES
                ]

    @pl.when(field == 0)
    def _():
        run(own0, other0)

    @pl.when(field == 1)
    def _():
        run(own1, other1)


def apply(weights, own0, other0, own1, other1):
    rows, half, members, _ = own0.shape
    size = 2 * members
    r8 = rows // SUB
    block = (SUB, half, members, LANES)
    zero = pl.BlockSpec(block, lambda f, r: (jnp.where(f == 0, r, r8 - 1), 0, 0, 0))
    one = pl.BlockSpec(block, lambda f, r: (jnp.where(f == 1, r, 0), 0, 0, 0))
    return pl.pallas_call(
        apply_kernel,
        grid=(2, r8),
        out_shape=jax.ShapeDtypeStruct((size, 2, r8, half, SUB, LANES), F32),
        in_specs=[
            pl.BlockSpec(weights.shape, lambda f, r: (0, 0)), zero, zero, one, one,
        ],
        out_specs=pl.BlockSpec((size, 1, 1, half, SUB, LANES), lambda f, r: (0, f, r, 0, 0, 0)),
        compiler_params=params(12),
        name="apply",
    )(weights, own0, other0, own1, other1)


def body(state, courant, diffusion, obs_cells, obs_owner, batch_order, obs_values, obs_error):
    slab = lax.axis_index("space")
    member = lax.axis_index("member")
    space = lax.axis_size("space")
    ids = jnp.stack([slab, member]).astype(jnp.int32)
    up = [(i, i + 1) for i in range(space - 1)]
    down = [(i + 1, i) for i in range(space - 1)]
    swap = [(0, 1), (1, 0)]

    state6, flow5, nu5 = tiled(state), tiled(courant), tiled(diffusion)
    up0, up1, down0, down1 = pack_edges(state6, flow5, nu5)
    before0 = lax.ppermute(up0, "space", up)
    after0 = lax.ppermute(down0, "space", down)
    scalars = (ids, obs_cells, obs_owner, batch_order)
    own0, send0, keep, away = forecast(0, True, *scalars, state6, flow5, nu5, before0, after0)
    other = lax.ppermute(away, "member", swap)
    gh = gram(ids, obs_owner, batch_order, keep, other, obs_values, obs_error)
    up1, down1, _ = lax.optimization_barrier((up1, down1, keep))
    before1 = lax.ppermute(up1, "space", up)
    after1 = lax.ppermute(down1, "space", down)
    before1, after1, gh = lax.optimization_barrier((before1, after1, gh))
    own1, send1 = forecast(1, False, *scalars, state6, flow5, nu5, before1, after1)
    other0 = lax.ppermute(send0, "member", swap)
    other1 = lax.ppermute(send1, "member", swap)
    bit = 1
    while bit < space:
        gh = gh + lax.ppermute(gh, "space", [(i, i ^ bit) for i in range(space)])
        bit *= 2
    theirs = lax.ppermute(gh, "member", swap)
    weights = chain(ids, gh, theirs)
    return untiled(apply(weights, own0, other0, own1, other1))


def solution(mesh):
    placed = (
        P("member", None, "space", None),
        P(None, "space", None),
        P(None, "space", None),
        P(),
        P(),
        P(),
        P(),
        P(),
    )
    return jax.shard_map(
        body,
        mesh=mesh,
        in_specs=placed,
        out_specs=P(None, None, "space", "member"),
        check_vma=False,
    )
```

```python
import functools

import jax
import jax.numpy as jnp
from jax import lax
from jax.experimental import pallas as pl
from jax.experimental.pallas import tpu as pltpu
from jax.sharding import PartitionSpec as P

HIGH = lax.Precision.HIGHEST
F32 = jnp.float32
BF16 = jnp.bfloat16
LANES = 128
SUB = 8
GATHER = 32
PACK = 8


def params(mib):
    return pltpu.CompilerParams(vmem_limit_bytes=mib * 1024 * 1024)


def unrolled(count, most):
    return max(d for d in range(1, most + 1) if count % d == 0)


def rows_loop(count, most, fn):
    step = unrolled(count, most)

    def run(i, carry):
        for u in range(step):
            fn(i * step + u)
        return carry

    lax.fori_loop(0, count // step, run, 0)


def tiled(array):
    *lead, rows, cols = array.shape
    n = len(lead)
    split = array.reshape(*lead, rows // SUB, SUB, cols // LANES, LANES)
    return jnp.transpose(split, (*range(n), n, n + 2, n + 1, n + 3))


def untiled(array):
    *lead, r8, ct, sub, lanes = array.shape
    n = len(lead)
    back = jnp.transpose(array, (*range(n), n, n + 2, n + 1, n + 3))
    return back.reshape(*lead, r8 * sub, ct * lanes)


def pack_kernel(state, flow, nu, *rest):
    fields = state.shape[1]
    members, _, r8, nct = state.shape[:4]
    outs, (edge_flow, edge_nu, sems) = rest[: 2 * fields], rest[2 * fields :]
    sides = ((r8 - 1, (SUB - 2, SUB - 1)), (0, (0, 1)))
    copies = []
    for side, (block, rows) in enumerate(sides):
        copies.append(pltpu.make_async_copy(flow.at[:, block], edge_flow.at[side], sems.at[len(copies)]))
        copies.append(pltpu.make_async_copy(nu.at[:, block], edge_nu.at[side], sems.at[len(copies)]))
    for field in range(fields):
        for side, (block, rows) in enumerate(sides):
            msg = outs[side * fields + field]
            for ct in range(nct):
                for at, row in enumerate(rows):
                    copies.append(
                        pltpu.make_async_copy(
                            state.at[:, field, block, ct, row, :],
                            msg.at[ct, pl.ds(at * members, members), :],
                            sems.at[len(copies)],
                        )
                    )
    for copy in copies:
        copy.start()
    for copy in copies[:4]:
        copy.wait()
    for field in range(fields):
        for side in range(2):
            msg = outs[side * fields + field]
            edge = (SUB - 1, 0)[side]
            for ct in range(nct):
                msg[ct, pl.ds(2 * members, PACK), :] = jnp.concatenate(
                    [
                        edge_flow[side, 0, ct, edge : edge + 1, :],
                        edge_flow[side, 1, ct, edge : edge + 1, :],
                        edge_nu[side, field, ct, edge : edge + 1, :],
                        jnp.zeros((PACK - 3, LANES), F32),
                    ],
                    axis=0,
                )
    for copy in copies[4:]:
        copy.wait()


def pack_edges(state6, flow5, nu5):
    members, fields, r8, nct = state6.shape[:4]
    msg = jax.ShapeDtypeStruct((nct, 2 * members + PACK, LANES), F32)
    edge = pltpu.VMEM((2, 2, nct, SUB, LANES), F32)
    return pl.pallas_call(
        pack_kernel,
        out_shape=[msg] * (2 * fields),
        in_specs=[pl.BlockSpec(memory_space=pltpu.HBM)] * 3,
        out_specs=[pl.BlockSpec(memory_space=pltpu.VMEM)] * (2 * fields),
        scratch_shapes=[edge, edge, pltpu.SemaphoreType.DMA((4 + 4 * fields * nct,))],
        compiler_params=params(56),
        name="pack_edges",
    )(state6, flow5, nu5)


def stencil_coefs(flow_x, flow_y, nu, col, width):
    east = nu - jnp.minimum(flow_x, 0.0)
    west = nu + jnp.maximum(flow_x, 0.0)
    north = nu - jnp.minimum(flow_y, 0.0)
    south = nu + jnp.maximum(flow_y, 0.0)
    centre = 1.0 - (east + west + north + south)
    south = jnp.where(col == 0, 0.0, south)
    north = jnp.where(col == width - 1, 0.0, north)
    return centre, west, east, south, north


def stencil_row(src, row, dst, coef, members):
    nct = src.shape[1]
    lane = lax.broadcasted_iota(jnp.int32, (SUB, LANES), 1)
    first, last = lane == 0, lane == LANES - 1
    weights = [
        [jnp.broadcast_to(coef(k, ct, row), (SUB, LANES)) for k in range(5)] for ct in range(nct)
    ]
    for group in range(members // SUB):
        rows = pl.ds(group * SUB, SUB)
        mid = [src[row + 1, ct, rows, :] for ct in range(nct)]
        right = [pltpu.roll(x, 1, 1) for x in mid]
        left = [pltpu.roll(x, LANES - 1, 1) for x in mid]
        for ct in range(nct):
            south = jnp.where(first, right[(ct - 1) % nct], right[ct])
            north = jnp.where(last, left[(ct + 1) % nct], left[ct])
            centre, west, east, w_s, w_n = weights[ct]
            value = (
                centre * mid[ct]
                + west * src[row, ct, rows, :]
                + east * src[row + 2, ct, rows, :]
                + (w_s * south + w_n * north)
            )
            dst(ct, rows, value)


def forecast_rows(lo, hi, field, member, state, flow, nu, before, after, q0, q1, coef, put):
    members, fields, r8, nct = state.shape[:4]
    rows = r8 * SUB
    half = nct // 2
    width = nct * LANES
    flat = state.reshape(members * fields * r8 * nct * SUB, LANES)
    stride = fields * r8 * nct * SUB

    def phys(ct):
        return lax.rem(ct + member * half, nct)

    first = max(lo - 1, 0) // SUB
    count = min(hi, rows - 1) // SUB + 1 - first
    base = first * SUB - SUB
    for ct in range(nct):
        at = phys(ct)
        col = lax.broadcasted_iota(jnp.int32, (count * SUB, LANES), 1) + at * LANES
        block = pl.ds(first, count)
        flow_x = flow[0, block, at, :, :].reshape(count * SUB, LANES)
        flow_y = flow[1, block, at, :, :].reshape(count * SUB, LANES)
        diffuse = nu[field, block, at, :, :].reshape(count * SUB, LANES)
        for k, value in enumerate(stencil_coefs(flow_x, flow_y, diffuse, col, width)):
            coef[k, ct, pl.ds(SUB, count * SUB), :] = value
        for msg, row, needed in ((before, -1, lo == 0), (after, rows, hi == rows)):
            if needed:
                edge = [msg[at, pl.ds(2 * members + k, 1), :] for k in range(3)]
                for k, value in enumerate(stencil_coefs(*edge, col[0:1], width)):
                    coef[k, ct, pl.ds(row - base, 1), :] = value
        if lo == 0:
            for k in range(2):
                q0[k, ct] = before[at, pl.ds(k * members, members), :]
        if hi == rows:
            for k in range(2):
                q0[rows - lo + 2 + k, ct] = after[at, pl.ds(k * members, members), :]

    start = max(lo - 2, 0)
    stop = min(hi + 2, rows)

    def load(i):
        r = start + i
        for ct in range(nct):
            at = (lax.div(r, SUB) * nct + phys(ct)) * SUB + lax.rem(r, SUB) + field * r8 * nct * SUB
            q0[r - lo + 2, ct] = flat[pl.ds(at, members, stride=stride), :]

    rows_loop(stop - start, 8, load)

    def first_step(i):
        def keep(ct, at, value):
            q1[i, ct, at, :] = value

        stencil_row(
            q0, i, keep, lambda k, ct, r: coef[k, ct, pl.ds(r + (lo - 1 - base), 1), :], members
        )

    rows_loop(hi - lo + 2, 6, first_step)

    def second_step(i):
        def keep(ct, at, value):
            put(lo + i, ct, at, value)

        stencil_row(
            q1, i, keep, lambda k, ct, r: coef[k, ct, pl.ds(r + (lo - base), 1), :], members
        )

    rows_loop(hi - lo, 4, second_step)


def row_scratch(count, nct, members):
    return [
        pltpu.VMEM((count + 4, nct, members, LANES), F32),
        pltpu.VMEM((count + 2, nct, members, LANES), F32),
        pltpu.VMEM((5, nct, -(-count // SUB) * SUB + 4 * SUB, LANES), F32),
    ]


def cost(count, nct, members):
    cells = count * nct * members * LANES
    return pl.CostEstimate(flops=40 * cells, bytes_accessed=8 * cells, transcendentals=0)


SMEM = pl.BlockSpec(memory_space=pltpu.SMEM)
VMEM = pl.BlockSpec(memory_space=pltpu.VMEM)


def inner_kernel(lo, hi, ids, state, flow, nu, full, send, *scratch):
    half = full.shape[1] // 2

    def put(r, ct, at, value):
        full[r, ct, at, :] = value
        if ct >= half:
            send[r, ct - half, at, :] = value

    forecast_rows(lo, hi, 0, ids[1], state, flow, nu, None, None, *scratch, put)


def forecast_inner(ids, state6, flow5, nu5):
    members, _, r8, nct = state6.shape[:4]
    rows = r8 * SUB
    return pl.pallas_call(
        functools.partial(inner_kernel, 2, rows - 2),
        out_shape=[
            jax.ShapeDtypeStruct((rows, nct, members, LANES), F32),
            jax.ShapeDtypeStruct((rows, nct // 2, members, LANES), F32),
        ],
        in_specs=[SMEM] + [VMEM] * 3,
        out_specs=[VMEM] * 2,
        scratch_shapes=row_scratch(rows - 4, nct, members),
        compiler_params=params(16),
        cost_estimate=cost(rows, nct, members),
        name="forecast_inner",
    )(ids, state6, flow5, nu5)


def edge_kernel(
    ids, cells, owner, order, state, flow, nu, before, after, full_in, send_in,
    full, send, keep, away, *scratch
):
    members, _, r8, nct = state.shape[:4]
    rows = r8 * SUB
    half = nct // 2
    width = nct * LANES
    slab, member = ids[0], ids[1]

    def put(r, ct, at, value):
        full[r, ct, at, :] = value
        if ct >= half:
            send[r, ct - half, at, :] = value

    for lo, hi in ((0, 2), (rows - 2, rows)):
        forecast_rows(lo, hi, 0, member, state, flow, nu, before, after, *scratch, put)

    nobs = cells.shape[1]
    bits = width.bit_length() - 1
    assert width == 1 << bits
    lane = lax.broadcasted_iota(jnp.int32, (members, LANES), 1)
    for position in range(order.shape[0]):
        batch = order[position]
        mine = owner[batch] == slab
        kept = lax.rem(position, 2) == member

        def pick(tile, carry, batch=batch, mine=mine, kept=kept, position=position):
            def some(group, acc):
                for u in range(GATHER):
                    o = group * GATHER + u
                    cell = cells[batch, tile * LANES + o]
                    r = lax.shift_right_logical(cell, bits)
                    c = cell & (width - 1)
                    at = (lax.shift_right_logical(c, 7) + member * half) & (nct - 1)
                    moved = pltpu.roll(full[r, at], (o - c) & (LANES - 1), 1)
                    acc = jnp.where(lane == o, moved, acc)
                return acc

            acc = lax.fori_loop(
                0, jnp.where(mine, LANES // GATHER, 0), some, jnp.zeros((members, LANES), F32)
            )

            @pl.when(kept)
            def _():
                keep[position // 2, tile] = acc

            @pl.when(jnp.logical_not(kept))
            def _():
                away[position // 2, tile] = acc

            return carry

        lax.fori_loop(0, nobs // LANES, pick, 0)


def forecast_edges(ids, cells, owner, order, state6, flow5, nu5, before, after, full, send):
    members, _, r8, nct = state6.shape[:4]
    nb, nobs = cells.shape
    picks = jax.ShapeDtypeStruct((nb // 2, nobs // LANES, members, LANES), F32)
    return pl.pallas_call(
        edge_kernel,
        out_shape=[
            jax.ShapeDtypeStruct(full.shape, F32), jax.ShapeDtypeStruct(send.shape, F32), picks, picks,
        ],
        in_specs=[SMEM] * 4 + [VMEM] * 7,
        out_specs=[VMEM] * 4,
        input_output_aliases={9: 0, 10: 1},
        scratch_shapes=row_scratch(2, nct, members),
        compiler_params=params(8),
        cost_estimate=cost(SUB, nct, members),
        name="forecast_edges",
    )(ids, cells, owner, order, state6, flow5, nu5, before, after, full, send)


def piece_kernel(lo, hi, ids, state, flow, nu, before, after, *rest):
    own, send, *scratch = rest[-5:]
    half = own.shape[1]

    def put(r, ct, at, value):
        if ct < half:
            own[r, ct, at, :] = value
        else:
            send[r, ct - half, at, :] = value

    forecast_rows(lo, hi, 1, ids[1], state, flow, nu, before, after, *scratch, put)


def forecast_piece(lo, hi, ids, state6, flow5, nu5, before, after, done):
    members, _, r8, nct = state6.shape[:4]
    rows = r8 * SUB
    part = jax.ShapeDtypeStruct((rows, nct // 2, members, LANES), F32)
    return pl.pallas_call(
        functools.partial(piece_kernel, lo, hi),
        out_shape=[part, part],
        in_specs=[SMEM] + [VMEM] * (5 + len(done)),
        out_specs=[VMEM] * 2,
        input_output_aliases={6: 0, 7: 1} if done else {},
        scratch_shapes=row_scratch(hi - lo, nct, members),
        compiler_params=params(10),
        cost_estimate=cost(hi - lo, nct, members),
        name=f"forecast_rows_{lo}",
    )(ids, state6, flow5, nu5, before, after, *done)


def gram_kernel(ids, owner, order, keep, other, observed, variance, out):
    slab, member = ids[0], ids[1]
    count, tiles, members = keep.shape[:3]
    for k in range(count):
        batch = order[2 * k + member]
        mine = owner[batch] == slab

        @pl.when(jnp.logical_not(mine))
        def _():
            out[k] = jnp.zeros(out.shape[1:], F32)

        @pl.when(mine)
        def _():
            total = jnp.zeros(out.shape[1:], F32)
            for t in range(tiles):
                a, b = keep[k, t], other[k, t]
                prior = jnp.concatenate(
                    [jnp.where(member == 0, a, b), jnp.where(member == 0, b, a)], axis=0
                )
                mean = jnp.sum(prior, axis=0, keepdims=True) / (2 * members)
                anomaly = prior - mean
                scaled = anomaly / variance[batch, :, pl.ds(t * LANES, LANES)]
                misfit = observed[batch, :, pl.ds(t * LANES, LANES)] - mean
                total += lax.dot_general(
                    scaled,
                    jnp.concatenate([anomaly, misfit], axis=0),
                    (((1,), (1,)), ((), ())),
                    precision=HIGH,
                    preferred_element_type=F32,
                )
            out[k] = total


def gram(ids, owner, order, keep, other, observed, variance):
    count, _, members, _ = keep.shape
    total = 2 * members
    smem = pl.BlockSpec(memory_space=pltpu.SMEM)
    vmem = pl.BlockSpec(memory_space=pltpu.VMEM)
    return pl.pallas_call(
        gram_kernel,
        out_shape=jax.ShapeDtypeStruct((count, total, 2 * total), F32),
        in_specs=[smem] * 3 + [vmem] * 4,
        out_specs=vmem,
        compiler_params=params(12),
        name="gram",
    )(ids, owner, order, keep, other, observed, variance[:, None, :])


def solve(inner, rhs):
    size = inner.shape[0]
    groups = size // SUB
    wide = (SUB, LANES)
    sub = lax.broadcasted_iota(jnp.int32, wide, 0)
    a = [inner[g * SUB : (g + 1) * SUB] for g in range(groups)]
    b = [rhs[g * SUB : (g + 1) * SUB] for g in range(groups)]

    def column(x, k):
        return jnp.broadcast_to(x[:, k : k + 1], wide)

    def row(x, k):
        return jnp.broadcast_to(x[k : k + 1, :], wide)

    for p in range(groups):
        cols = [[column(a[g], p * SUB + k) for k in range(SUB)] for g in range(groups)]
        c, pa, pb = cols[p], a[p], b[p]
        for k in range(0, SUB, 2):
            ck, cl = c[k], c[k + 1]
            kk, kl, lk, ll = row(ck, k), row(cl, k), row(ck, k + 1), row(cl, k + 1)
            scale = 1.0 / (kk * ll - kl * lk)

            def eliminate(x, k=k, ck=ck, cl=cl, kk=kk, kl=kl, lk=lk, ll=ll, scale=scale):
                u, w = row(x, k), row(x, k + 1)
                n0, n1 = ll * u - kl * w, kk * w - lk * u
                rest = x - scale * (ck * n0 + cl * n1)
                return jnp.where(sub == k, scale * n0, jnp.where(sub == k + 1, scale * n1, rest))

            for j in range(k + 2, SUB):
                c[j] = eliminate(c[j])
            pa, pb = eliminate(pa), eliminate(pb)
        a[p], b[p] = pa, pb
        ra = [row(pa, k) for k in range(SUB)]
        rb = [row(pb, k) for k in range(SUB)]
        for g in range(groups):
            if g == p:
                continue
            for k in range(SUB):
                if p + 1 < groups:
                    a[g] = a[g] - cols[g][k] * ra[k]
                b[g] = b[g] - cols[g][k] * rb[k]
    return jnp.concatenate(b, axis=0)


def chain_kernel(ids, mine, other, out):
    member = ids[1]
    count, size, _ = mine.shape
    eye = (
        lax.broadcasted_iota(jnp.int32, (size, 2 * size), 0)
        == lax.broadcasted_iota(jnp.int32, (size, 2 * size), 1)
    ).astype(F32)
    unit = eye[:, :size]

    def dot(x, y, lhs=1):
        return lax.dot_general(
            x, y, (((lhs,), (0,)), ((), ())), precision=HIGH, preferred_element_type=F32
        )

    def step(position, v):
        k = lax.div(position, 2)
        gh = jnp.where(lax.rem(position, 2) == member, mine[k], other[k])
        g, h = gh[:, :size], gh[:, size:]
        centred = h - jnp.sum(h, axis=1, keepdims=True) / size
        z = v[:, :size]
        gv = dot(g, v)
        both = dot(z, jnp.concatenate([gv, centred, h], axis=1), lhs=0)
        inner = both[:, : 2 * size] + (size - 1) * eye
        rhs = both[:, 2 * size :] - both[:, : 2 * size]
        return v + dot(z, solve(inner, rhs))

    start = jnp.concatenate([unit - 1.0 / size, unit], axis=1)
    v = lax.fori_loop(0, 2 * count, step, start)
    w = v[:, size:].T
    half = size // 2
    first, second = w[:, :half], w[:, half:]
    w = jnp.concatenate(
        [jnp.where(member == 0, first, second), jnp.where(member == 0, second, first)], axis=1
    )
    high = w.astype(BF16).astype(F32)
    low = w - high
    out[...] = jnp.concatenate(
        [jnp.concatenate([high, high], axis=1), jnp.concatenate([low, jnp.zeros_like(low)], axis=1)],
        axis=0,
    )


def chain(ids, mine, other):
    count, size, _ = mine.shape
    smem = pl.BlockSpec(memory_space=pltpu.SMEM)
    vmem = pl.BlockSpec(memory_space=pltpu.VMEM)
    return pl.pallas_call(
        chain_kernel,
        out_shape=jax.ShapeDtypeStruct((2 * size, 2 * size), F32),
        in_specs=[smem, vmem, vmem],
        out_specs=vmem,
        compiler_params=params(12),
        name="chain",
    )(ids, mine, other)


def apply_kernel(w_ref, own0, other0, own1, other1, out):
    field = pl.program_id(0)
    size = w_ref.shape[0] // 2
    rows, half = own0.shape[:2]
    weights = w_ref[...].astype(BF16)
    flat = out.reshape(size * half * rows, LANES)

    def run(own, other):
        for r in range(rows):
            parts = [
                jnp.concatenate([src[r, ct] for ct in range(half)], axis=1) for src in (own, other)
            ]
            high = [x.astype(BF16) for x in parts]
            low = [(x - y.astype(F32)).astype(BF16) for x, y in zip(parts, high)]
            stacked = jnp.concatenate([*high, *low], axis=0)
            result = jnp.dot(weights, stacked, preferred_element_type=F32)
            result = result[:size] + result[size:]
            for ct in range(half):
                flat[pl.ds(ct * rows + r, size, stride=half * rows), :] = result[
                    :, ct * LANES : (ct + 1) * LANES
                ]

    @pl.when(field == 0)
    def _():
        run(own0, other0)

    @pl.when(field == 1)
    def _():
        run(own1, other1)


def apply(weights, own0, other0, own1, other1):
    rows, half, members, _ = other0.shape
    size = 2 * members
    r8 = rows // SUB
    block = (SUB, half, members, LANES)
    zero = pl.BlockSpec(block, lambda f, r: (jnp.where(f == 0, r, r8 - 1), 0, 0, 0))
    one = pl.BlockSpec(block, lambda f, r: (jnp.where(f == 1, r, 0), 0, 0, 0))
    return pl.pallas_call(
        apply_kernel,
        grid=(2, r8),
        out_shape=jax.ShapeDtypeStruct((size, 2, r8, half, SUB, LANES), F32),
        in_specs=[
            pl.BlockSpec(weights.shape, lambda f, r: (0, 0)), zero, zero, one, one,
        ],
        out_specs=pl.BlockSpec((size, 1, 1, half, SUB, LANES), lambda f, r: (0, f, r, 0, 0, 0)),
        compiler_params=params(12),
        name="apply",
    )(weights, own0, other0, own1, other1)


def body(state, courant, diffusion, obs_cells, obs_owner, batch_order, obs_values, obs_error):
    slab = lax.axis_index("space")
    member = lax.axis_index("member")
    space = lax.axis_size("space")
    ids = jnp.stack([slab, member]).astype(jnp.int32)
    up = [(i, i + 1) for i in range(space - 1)]
    down = [(i + 1, i) for i in range(space - 1)]
    swap = [(0, 1), (1, 0)]

    state6, flow5, nu5 = tiled(state), tiled(courant), tiled(diffusion)
    up0, up1, down0, down1 = pack_edges(state6, flow5, nu5)
    before0 = lax.ppermute(up0, "space", up)
    after0 = lax.ppermute(down0, "space", down)
    full0, send0 = forecast_inner(ids, state6, flow5, nu5)
    full0, send0, keep, away = forecast_edges(
        ids, obs_cells, obs_owner, batch_order, state6, flow5, nu5, before0, after0, full0, send0
    )
    other = lax.ppermute(away, "member", swap)
    up1, down1, keep = lax.optimization_barrier((up1, down1, keep))
    before1 = lax.ppermute(up1, "space", up)
    after1 = lax.ppermute(down1, "space", down)
    gh = gram(ids, obs_owner, batch_order, keep, other, obs_values, obs_error)
    send0, gh = lax.optimization_barrier((send0, gh))
    other0 = lax.ppermute(send0, "member", swap)

    rows = state.shape[2]
    pieces = [(r, r + rows // 4) for r in range(0, rows, rows // 4)]
    pieces = pieces[1:] + pieces[:1]
    field1 = ()
    bit = 1
    while bit < space:
        received = lax.ppermute(gh, "space", [(i, i ^ bit) for i in range(space)])
        if pieces:
            before1, after1, gh = lax.optimization_barrier((before1, after1, gh))
            field1 = forecast_piece(*pieces.pop(0), ids, state6, flow5, nu5, before1, after1, field1)
            received, *field1 = lax.optimization_barrier((received, *field1))
        gh = gh + received
        bit *= 2
    for piece in pieces:
        field1 = forecast_piece(*piece, ids, state6, flow5, nu5, before1, after1, field1)
    own1, send1 = field1
    theirs = lax.ppermute(gh, "member", swap)
    other1 = lax.ppermute(send1, "member", swap)
    weights = chain(ids, gh, theirs)
    return untiled(apply(weights, full0, other0, own1, other1))


def solution(mesh):
    placed = (
        P("member", None, "space", None),
        P(None, "space", None),
        P(None, "space", None),
        P(),
        P(),
        P(),
        P(),
        P(),
    )
    return jax.shard_map(
        body,
        mesh=mesh,
        in_specs=placed,
        out_specs=P(None, None, "space", "member"),
        check_vma=False,
    )
```

```python
import functools

import jax
import jax.numpy as jnp
from jax import lax
from jax.experimental import pallas as pl
from jax.experimental.pallas import tpu as pltpu
from jax.sharding import PartitionSpec as P

HIGH = lax.Precision.HIGHEST
F32 = jnp.float32
BF16 = jnp.bfloat16
LANES = 128
SUB = 8
GATHER = 32
PACK = 8


def params(mib):
    return pltpu.CompilerParams(vmem_limit_bytes=mib * 1024 * 1024)


def unrolled(count, most):
    return max(d for d in range(1, most + 1) if count % d == 0)


def rows_loop(count, most, fn):
    step = unrolled(count, most)

    def run(i, carry):
        for u in range(step):
            fn(i * step + u)
        return carry

    lax.fori_loop(0, count // step, run, 0)


def tiled(array):
    *lead, rows, cols = array.shape
    n = len(lead)
    split = array.reshape(*lead, rows // SUB, SUB, cols // LANES, LANES)
    return jnp.transpose(split, (*range(n), n, n + 2, n + 1, n + 3))


def untiled(array):
    *lead, r8, ct, sub, lanes = array.shape
    n = len(lead)
    back = jnp.transpose(array, (*range(n), n, n + 2, n + 1, n + 3))
    return back.reshape(*lead, r8 * sub, ct * lanes)


def pack_kernel(state, flow, nu, up, down, edge_flow, edge_nu, sems):
    members, fields, r8, nct = state.shape[:4]
    sides = ((up, r8 - 1, (SUB - 2, SUB - 1)), (down, 0, (0, 1)))
    copies = []

    def copy(src, dst):
        copies.append(pltpu.make_async_copy(src, dst, sems.at[len(copies)]))

    for side, (msg, block, rows) in enumerate(sides):
        copy(flow.at[:, block], edge_flow.at[side])
        copy(nu.at[:, block], edge_nu.at[side])
    for msg, block, rows in sides:
        for field in range(fields):
            for ct in range(nct):
                for at, row in enumerate(rows):
                    copy(
                        state.at[:, field, block, ct, row, :],
                        msg.at[ct, pl.ds((field * 2 + at) * members, members), :],
                    )
    for one in copies:
        one.start()
    for one in copies[:4]:
        one.wait()
    for side, (msg, block, rows) in enumerate(sides):
        edge = (SUB - 1, 0)[side]
        for ct in range(nct):
            numbers = [edge_flow[side, k, ct, edge : edge + 1, :] for k in range(2)]
            numbers += [edge_nu[side, k, ct, edge : edge + 1, :] for k in range(fields)]
            numbers.append(jnp.zeros((PACK - 2 - fields, LANES), F32))
            msg[ct, pl.ds(2 * fields * members, PACK), :] = jnp.concatenate(numbers, axis=0)
    for one in copies[4:]:
        one.wait()


def pack_edges(state6, flow5, nu5):
    members, fields, r8, nct = state6.shape[:4]
    msg = jax.ShapeDtypeStruct((nct, 2 * fields * members + PACK, LANES), F32)
    edge = pltpu.VMEM((2, 2, nct, SUB, LANES), F32)
    return pl.pallas_call(
        pack_kernel,
        out_shape=[msg] * 2,
        in_specs=[pl.BlockSpec(memory_space=pl.ANY)] * 3,
        out_specs=[pl.BlockSpec(memory_space=pltpu.VMEM)] * 2,
        scratch_shapes=[edge, edge, pltpu.SemaphoreType.DMA((4 + 4 * fields * nct,))],
        compiler_params=params(56),
        name="pack_edges",
    )(state6, flow5, nu5)


def stencil_coefs(flow_x, flow_y, nu, col, width):
    east = nu - jnp.minimum(flow_x, 0.0)
    west = nu + jnp.maximum(flow_x, 0.0)
    north = nu - jnp.minimum(flow_y, 0.0)
    south = nu + jnp.maximum(flow_y, 0.0)
    centre = 1.0 - (east + west + north + south)
    south = jnp.where(col == 0, 0.0, south)
    north = jnp.where(col == width - 1, 0.0, north)
    return centre, west, east, south, north


def stencil_row(src, row, dst, coef, members):
    nct = src.shape[1]
    lane = lax.broadcasted_iota(jnp.int32, (SUB, LANES), 1)
    first, last = lane == 0, lane == LANES - 1
    weights = [
        [coef(k, ct, row) for k in range(5)] for ct in range(nct)
    ]
    for group in range(members // SUB):
        rows = pl.ds(group * SUB, SUB)
        mid = [src[row + 1, ct, rows, :] for ct in range(nct)]
        right = [pltpu.roll(x, 1, 1) for x in mid]
        left = [pltpu.roll(x, LANES - 1, 1) for x in mid]
        for ct in range(nct):
            south = jnp.where(first, right[(ct - 1) % nct], right[ct])
            north = jnp.where(last, left[(ct + 1) % nct], left[ct])
            centre, west, east, w_s, w_n = weights[ct]
            value = (
                centre * mid[ct]
                + west * src[row, ct, rows, :]
                + east * src[row + 2, ct, rows, :]
                + (w_s * south + w_n * north)
            )
            dst(ct, rows, value)


def forecast_rows(
    lo, hi, field, member, state, flow, nu, before, after, q0, q1, coef, put, wait=None
):
    members, fields, r8, nct = state.shape[:4]
    rows = r8 * SUB
    half = nct // 2
    width = nct * LANES
    flat = state.reshape(members * fields * r8 * nct * SUB, LANES)
    stride = fields * r8 * nct * SUB
    offset = min(field, fields - 1) * r8 * nct * SUB
    room = coef.shape[2]
    coef_flat = coef.reshape(5 * nct * room, LANES)

    def weight(k, ct, at):
        return coef_flat[pl.ds((k * nct + ct) * room + at, SUB, stride=0), :]

    def phys(ct):
        return lax.rem(ct + member * half, nct)

    first = max(lo - 1, 0) // SUB
    count = min(hi, rows - 1) // SUB + 1 - first
    base = first * SUB - SUB
    for ct in range(nct):
        at = phys(ct)
        col = lax.broadcasted_iota(jnp.int32, (count * SUB, LANES), 1) + at * LANES
        block = pl.ds(first, count)
        flow_x = flow[0, block, at, :, :].reshape(count * SUB, LANES)
        flow_y = flow[1, block, at, :, :].reshape(count * SUB, LANES)
        diffuse = nu[field, block, at, :, :].reshape(count * SUB, LANES)
        for k, value in enumerate(stencil_coefs(flow_x, flow_y, diffuse, col, width)):
            coef[k, ct, pl.ds(SUB, count * SUB), :] = value
        for msg, row, needed in ((before, -1, lo == 0), (after, rows, hi == rows)):
            if needed:
                edge = [msg[at, pl.ds(4 * members + k, 1), :] for k in (0, 1, 2 + field)]
                for k, value in enumerate(stencil_coefs(*edge, col[0:1], width)):
                    coef[k, ct, pl.ds(row - base, 1), :] = value
        if lo == 0:
            for k in range(2):
                q0[k, ct] = before[at, pl.ds((2 * field + k) * members, members), :]
        if hi == rows:
            for k in range(2):
                q0[rows - lo + 2 + k, ct] = after[at, pl.ds((2 * field + k) * members, members), :]

    start = max(lo - 2, 0)
    stop = min(hi + 2, rows)

    def load(i):
        r = start + i
        for ct in range(nct):
            at = (lax.div(r, SUB) * nct + phys(ct)) * SUB + lax.rem(r, SUB) + offset
            q0[r - lo + 2, ct] = flat[pl.ds(at, members, stride=stride), :]

    if wait is None:
        rows_loop(stop - start, 8, load)
    else:
        for block in range(r8):
            wait(block)
            for r in range(max(start, block * SUB), min(stop, block * SUB + SUB)):
                load(r - start)

    def first_step(i):
        def keep(ct, at, value):
            q1[i, ct, at, :] = value

        stencil_row(
            q0, i, keep, lambda k, ct, r: weight(k, ct, r + (lo - 1 - base)), members
        )

    rows_loop(hi - lo + 2, 6, first_step)

    def second_step(i):
        def keep(ct, at, value):
            put(lo + i, ct, at, value)

        stencil_row(
            q1, i, keep, lambda k, ct, r: weight(k, ct, r + (lo - base)), members
        )

    rows_loop(hi - lo, 4, second_step)


def row_scratch(count, nct, members):
    return [
        pltpu.VMEM((count + 4, nct, members, LANES), F32),
        pltpu.VMEM((count + 2, nct, members, LANES), F32),
        pltpu.VMEM((5, nct, -(-count // SUB) * SUB + 4 * SUB, LANES), F32),
    ]


def cost(count, nct, members):
    cells = count * nct * members * LANES
    return pl.CostEstimate(flops=40 * cells, bytes_accessed=8 * cells, transcendentals=0)


SMEM = pl.BlockSpec(memory_space=pltpu.SMEM)
VMEM = pl.BlockSpec(memory_space=pltpu.VMEM)


def inner_kernel(lo, hi, ids, state, flow, nu, full, send, held, sems, *scratch):
    half = full.shape[1] // 2
    copies = [
        pltpu.make_async_copy(state.at[:, 0, block], held.at[:, 0, block], sems.at[block])
        for block in range(state.shape[2])
    ]
    for one in copies:
        one.start()

    def put(r, ct, at, value):
        full[r, ct, at, :] = value
        if ct >= half:
            send[r, ct - half, at, :] = value

    forecast_rows(
        lo, hi, 0, ids[1], held, flow, nu, None, None, *scratch, put,
        wait=lambda block: copies[block].wait(),
    )


def forecast_inner(ids, state6, flow5, nu5):
    members, _, r8, nct = state6.shape[:4]
    rows = r8 * SUB
    return pl.pallas_call(
        functools.partial(inner_kernel, 2, rows - 2),
        out_shape=[
            jax.ShapeDtypeStruct((rows, nct, members, LANES), F32),
            jax.ShapeDtypeStruct((rows, nct // 2, members, LANES), F32),
        ],
        in_specs=[SMEM, pl.BlockSpec(memory_space=pl.ANY)] + [VMEM] * 2,
        out_specs=[VMEM] * 2,
        scratch_shapes=[
            pltpu.VMEM((members, 1, r8, nct, SUB, LANES), F32),
            pltpu.SemaphoreType.DMA((r8,)),
            *row_scratch(rows - 4, nct, members),
        ],
        compiler_params=params(44),
        cost_estimate=cost(rows, nct, members),
        name="forecast_inner",
    )(ids, state6, flow5, nu5)


def edge_kernel(
    ids, cells, owner, order, state, flow, nu, before, after, full_in, send_in,
    full, send, keep, away, *scratch
):
    members, _, r8, nct = state.shape[:4]
    rows = r8 * SUB
    half = nct // 2
    width = nct * LANES
    slab, member = ids[0], ids[1]

    def put(r, ct, at, value):
        full[r, ct, at, :] = value
        if ct >= half:
            send[r, ct - half, at, :] = value

    for lo, hi in ((0, 2), (rows - 2, rows)):
        forecast_rows(lo, hi, 0, member, state, flow, nu, before, after, *scratch, put)

    nobs = cells.shape[1]
    bits = width.bit_length() - 1
    assert width == 1 << bits
    lane = lax.broadcasted_iota(jnp.int32, (members, LANES), 1)
    for position in range(order.shape[0]):
        batch = order[position]
        mine = owner[batch] == slab
        kept = lax.rem(position, 2) == member

        def pick(tile, carry, batch=batch, mine=mine, kept=kept, position=position):
            def some(group, acc):
                for u in range(GATHER):
                    o = group * GATHER + u
                    cell = cells[batch, tile * LANES + o]
                    r = lax.shift_right_logical(cell, bits)
                    c = cell & (width - 1)
                    at = (lax.shift_right_logical(c, 7) + member * half) & (nct - 1)
                    moved = pltpu.roll(full[r, at], (o - c) & (LANES - 1), 1)
                    acc = jnp.where(lane == o, moved, acc)
                return acc

            acc = lax.fori_loop(
                0, jnp.where(mine, LANES // GATHER, 0), some, jnp.zeros((members, LANES), F32)
            )

            @pl.when(kept)
            def _():
                keep[position // 2, tile] = acc

            @pl.when(jnp.logical_not(kept))
            def _():
                away[position // 2, tile] = acc

            return carry

        lax.fori_loop(0, nobs // LANES, pick, 0)


def forecast_edges(ids, cells, owner, order, state6, flow5, nu5, before, after, full, send):
    members, _, r8, nct = state6.shape[:4]
    nb, nobs = cells.shape
    picks = jax.ShapeDtypeStruct((nb // 2, nobs // LANES, members, LANES), F32)
    return pl.pallas_call(
        edge_kernel,
        out_shape=[
            jax.ShapeDtypeStruct(full.shape, F32), jax.ShapeDtypeStruct(send.shape, F32), picks, picks,
        ],
        in_specs=[SMEM] * 4 + [VMEM] * 7,
        out_specs=[VMEM] * 4,
        input_output_aliases={9: 0, 10: 1},
        scratch_shapes=row_scratch(2, nct, members),
        compiler_params=params(8),
        cost_estimate=cost(SUB, nct, members),
        name="forecast_edges",
    )(ids, cells, owner, order, state6, flow5, nu5, before, after, full, send)


def piece_kernel(lo, hi, ids, state, flow, nu, before, after, *rest):
    own, send, *scratch = rest[-5:]
    half = own.shape[1]

    def put(r, ct, at, value):
        if ct < half:
            own[r, ct, at, :] = value
        else:
            send[r, ct - half, at, :] = value

    forecast_rows(lo, hi, 1, ids[1], state, flow, nu, before, after, *scratch, put)


def forecast_piece(lo, hi, ids, state6, flow5, nu5, before, after, done):
    members, _, r8, nct = state6.shape[:4]
    rows = r8 * SUB
    part = jax.ShapeDtypeStruct((rows, nct // 2, members, LANES), F32)
    return pl.pallas_call(
        functools.partial(piece_kernel, lo, hi),
        out_shape=[part, part],
        in_specs=[SMEM] + [VMEM] * (5 + len(done)),
        out_specs=[VMEM] * 2,
        input_output_aliases={6: 0, 7: 1} if done else {},
        scratch_shapes=row_scratch(hi - lo, nct, members),
        compiler_params=params(10),
        cost_estimate=cost(hi - lo, nct, members),
        name=f"forecast_rows_{lo}",
    )(ids, state6, flow5, nu5, before, after, *done)


def gram_kernel(ids, owner, order, keep, other, observed, variance, out):
    slab, member = ids[0], ids[1]
    count, tiles, members = keep.shape[:3]
    for k in range(count):
        batch = order[2 * k + member]
        mine = owner[batch] == slab

        @pl.when(jnp.logical_not(mine))
        def _():
            out[k] = jnp.zeros(out.shape[1:], F32)

        @pl.when(mine)
        def _():
            total = jnp.zeros(out.shape[1:], F32)
            for t in range(tiles):
                a, b = keep[k, t], other[k, t]
                prior = jnp.concatenate(
                    [jnp.where(member == 0, a, b), jnp.where(member == 0, b, a)], axis=0
                )
                mean = jnp.sum(prior, axis=0, keepdims=True) / (2 * members)
                anomaly = prior - mean
                scaled = anomaly / variance[batch, :, pl.ds(t * LANES, LANES)]
                misfit = observed[batch, :, pl.ds(t * LANES, LANES)] - mean
                total += lax.dot_general(
                    scaled,
                    jnp.concatenate([anomaly, misfit], axis=0),
                    (((1,), (1,)), ((), ())),
                    precision=HIGH,
                    preferred_element_type=F32,
                )
            out[k] = total


def gram(ids, owner, order, keep, other, observed, variance):
    count, _, members, _ = keep.shape
    total = 2 * members
    smem = pl.BlockSpec(memory_space=pltpu.SMEM)
    vmem = pl.BlockSpec(memory_space=pltpu.VMEM)
    return pl.pallas_call(
        gram_kernel,
        out_shape=jax.ShapeDtypeStruct((count, total, 2 * total), F32),
        in_specs=[smem] * 3 + [vmem] * 4,
        out_specs=vmem,
        compiler_params=params(12),
        name="gram",
    )(ids, owner, order, keep, other, observed, variance[:, None, :])


def solve(inner, rhs):
    size = inner.shape[0]
    groups = size // SUB
    wide = (SUB, LANES)
    sub = lax.broadcasted_iota(jnp.int32, wide, 0)
    a = [inner[g * SUB : (g + 1) * SUB] for g in range(groups)]
    b = [rhs[g * SUB : (g + 1) * SUB] for g in range(groups)]

    def column(x, k):
        return jnp.broadcast_to(x[:, k : k + 1], wide)

    def row(x, k):
        return jnp.broadcast_to(x[k : k + 1, :], wide)

    for p in range(groups):
        cols = [[column(a[g], p * SUB + k) for k in range(SUB)] for g in range(groups)]
        c, pa, pb = cols[p], a[p], b[p]
        for k in range(0, SUB, 2):
            ck, cl = c[k], c[k + 1]
            kk, kl, lk, ll = row(ck, k), row(cl, k), row(ck, k + 1), row(cl, k + 1)
            scale = 1.0 / (kk * ll - kl * lk)

            def eliminate(x, k=k, ck=ck, cl=cl, kk=kk, kl=kl, lk=lk, ll=ll, scale=scale):
                u, w = row(x, k), row(x, k + 1)
                n0, n1 = ll * u - kl * w, kk * w - lk * u
                rest = x - scale * (ck * n0 + cl * n1)
                return jnp.where(sub == k, scale * n0, jnp.where(sub == k + 1, scale * n1, rest))

            for j in range(k + 2, SUB):
                c[j] = eliminate(c[j])
            pa, pb = eliminate(pa), eliminate(pb)
        a[p], b[p] = pa, pb
        ra = [row(pa, k) for k in range(SUB)]
        rb = [row(pb, k) for k in range(SUB)]
        for g in range(groups):
            if g == p:
                continue
            for k in range(SUB):
                if p + 1 < groups:
                    a[g] = a[g] - cols[g][k] * ra[k]
                b[g] = b[g] - cols[g][k] * rb[k]
    return jnp.concatenate(b, axis=0)


def chain_kernel(ids, mine, other, out):
    member = ids[1]
    count, size, _ = mine.shape
    eye = (
        lax.broadcasted_iota(jnp.int32, (size, 2 * size), 0)
        == lax.broadcasted_iota(jnp.int32, (size, 2 * size), 1)
    ).astype(F32)
    unit = eye[:, :size]

    def dot(x, y, lhs=1):
        return lax.dot_general(
            x, y, (((lhs,), (0,)), ((), ())), precision=HIGH, preferred_element_type=F32
        )

    def step(position, v):
        k = lax.div(position, 2)
        gh = jnp.where(lax.rem(position, 2) == member, mine[k], other[k])
        g, h = gh[:, :size], gh[:, size:]
        centred = h - jnp.sum(h, axis=1, keepdims=True) / size
        z = v[:, :size]
        gv = dot(g, v)
        both = dot(z, jnp.concatenate([gv, centred, h], axis=1), lhs=0)
        inner = both[:, : 2 * size] + (size - 1) * eye
        rhs = both[:, 2 * size :] - both[:, : 2 * size]
        return v + dot(z, solve(inner, rhs))

    start = jnp.concatenate([unit - 1.0 / size, unit], axis=1)
    v = lax.fori_loop(0, 2 * count, step, start)
    w = v[:, size:].T
    half = size // 2
    first, second = w[:, :half], w[:, half:]
    w = jnp.concatenate(
        [jnp.where(member == 0, first, second), jnp.where(member == 0, second, first)], axis=1
    )
    high = w.astype(BF16).astype(F32)
    low = w - high
    out[...] = jnp.concatenate(
        [jnp.concatenate([high, high], axis=1), jnp.concatenate([low, jnp.zeros_like(low)], axis=1)],
        axis=0,
    )


def chain(ids, mine, other):
    count, size, _ = mine.shape
    smem = pl.BlockSpec(memory_space=pltpu.SMEM)
    vmem = pl.BlockSpec(memory_space=pltpu.VMEM)
    return pl.pallas_call(
        chain_kernel,
        out_shape=jax.ShapeDtypeStruct((2 * size, 2 * size), F32),
        in_specs=[smem, vmem, vmem],
        out_specs=vmem,
        compiler_params=params(12),
        name="chain",
    )(ids, mine, other)


def apply_kernel(w_ref, own0, other0, own1, other1, out):
    field = pl.program_id(0)
    size = w_ref.shape[0] // 2
    rows, half = own0.shape[:2]
    weights = w_ref[...].astype(BF16)
    flat = out.reshape(size * half * rows, LANES)

    def run(own, other):
        for r in range(rows):
            parts = [
                jnp.concatenate([src[r, ct] for ct in range(half)], axis=1) for src in (own, other)
            ]
            high = [x.astype(BF16) for x in parts]
            low = [(x - y.astype(F32)).astype(BF16) for x, y in zip(parts, high)]
            stacked = jnp.concatenate([*high, *low], axis=0)
            result = jnp.dot(weights, stacked, preferred_element_type=F32)
            result = result[:size] + result[size:]
            for ct in range(half):
                flat[pl.ds(ct * rows + r, size, stride=half * rows), :] = result[
                    :, ct * LANES : (ct + 1) * LANES
                ]

    @pl.when(field == 0)
    def _():
        run(own0, other0)

    @pl.when(field == 1)
    def _():
        run(own1, other1)


def apply(weights, own0, other0, own1, other1):
    rows, half, members, _ = other0.shape
    size = 2 * members
    r8 = rows // SUB
    block = (SUB, half, members, LANES)
    zero = pl.BlockSpec(block, lambda f, r: (jnp.where(f == 0, r, r8 - 1), 0, 0, 0))
    one = pl.BlockSpec(block, lambda f, r: (jnp.where(f == 1, r, 0), 0, 0, 0))
    return pl.pallas_call(
        apply_kernel,
        grid=(2, r8),
        out_shape=jax.ShapeDtypeStruct((size, 2, r8, half, SUB, LANES), F32),
        in_specs=[
            pl.BlockSpec(weights.shape, lambda f, r: (0, 0)), zero, zero, one, one,
        ],
        out_specs=pl.BlockSpec((size, 1, 1, half, SUB, LANES), lambda f, r: (0, f, r, 0, 0, 0)),
        compiler_params=params(12),
        name="apply",
    )(weights, own0, other0, own1, other1)


def body(state, courant, diffusion, obs_cells, obs_owner, batch_order, obs_values, obs_error):
    slab = lax.axis_index("space")
    member = lax.axis_index("member")
    space = lax.axis_size("space")
    ids = jnp.stack([slab, member]).astype(jnp.int32)
    up = [(i, i + 1) for i in range(space - 1)]
    down = [(i + 1, i) for i in range(space - 1)]
    swap = [(0, 1), (1, 0)]

    state6, flow5, nu5 = tiled(state), tiled(courant), tiled(diffusion)
    up_edge, down_edge = pack_edges(state6, flow5, nu5)
    before = lax.ppermute(up_edge, "space", up)
    after = lax.ppermute(down_edge, "space", down)
    full0, send0 = forecast_inner(ids, state6, flow5, nu5)
    full0, send0, keep, away = forecast_edges(
        ids, obs_cells, obs_owner, batch_order, state6, flow5, nu5, before, after, full0, send0
    )
    other = lax.ppermute(away, "member", swap)
    gh = gram(ids, obs_owner, batch_order, keep, other, obs_values, obs_error)

    rows = state.shape[2]
    pieces = [(r, r + rows // 4) for r in range(0, rows, rows // 4)]
    field1 = ()
    bit = 1
    while bit < space:
        received = lax.ppermute(gh, "space", [(i, i ^ bit) for i in range(space)])
        if pieces:
            before, after, gh = lax.optimization_barrier((before, after, gh))
            field1 = forecast_piece(*pieces.pop(0), ids, state6, flow5, nu5, before, after, field1)
            received, *field1 = lax.optimization_barrier((received, *field1))
        gh = gh + received
        bit *= 2
    for piece in pieces:
        field1 = forecast_piece(*piece, ids, state6, flow5, nu5, before, after, field1)
    own1, send1 = field1
    theirs = lax.ppermute(gh, "member", swap)
    send0, send1, gh = lax.optimization_barrier((send0, send1, gh))
    other0 = lax.ppermute(send0, "member", swap)
    other1 = lax.ppermute(send1, "member", swap)
    weights = chain(ids, gh, theirs)
    return untiled(apply(weights, full0, other0, own1, other1))


def solution(mesh):
    placed = (
        P("member", None, "space", None),
        P(None, "space", None),
        P(None, "space", None),
        P(),
        P(),
        P(),
        P(),
        P(),
    )
    return jax.shard_map(
        body,
        mesh=mesh,
        in_specs=placed,
        out_specs=P(None, None, "space", "member"),
        check_vma=False,
    )
```

```python
import functools

import jax
import jax.numpy as jnp
from jax import lax
from jax.experimental import pallas as pl
from jax.experimental.pallas import tpu as pltpu
from jax.sharding import PartitionSpec as P

HIGH = lax.Precision.HIGHEST
F32 = jnp.float32
BF16 = jnp.bfloat16
LANES = 128
SUB = 8
GATHER = 32
PACK = 8


def params(mib):
    return pltpu.CompilerParams(vmem_limit_bytes=mib * 1024 * 1024)


def unrolled(count, most):
    return max(d for d in range(1, most + 1) if count % d == 0)


def rows_loop(count, most, fn):
    step = unrolled(count, most)

    def run(i, carry):
        for u in range(step):
            fn(i * step + u)
        return carry

    lax.fori_loop(0, count // step, run, 0)


def tiled(array):
    *lead, rows, cols = array.shape
    n = len(lead)
    split = array.reshape(*lead, rows // SUB, SUB, cols // LANES, LANES)
    return jnp.transpose(split, (*range(n), n, n + 2, n + 1, n + 3))


def untiled(array):
    *lead, r8, ct, sub, lanes = array.shape
    n = len(lead)
    back = jnp.transpose(array, (*range(n), n, n + 2, n + 1, n + 3))
    return back.reshape(*lead, r8 * sub, ct * lanes)


def pack_kernel(state, flow, nu, up, down, edge_flow, edge_nu, sems):
    members, fields, r8, nct = state.shape[:4]
    sides = ((up, r8 - 1, (SUB - 2, SUB - 1)), (down, 0, (0, 1)))
    copies = []

    def copy(src, dst):
        copies.append(pltpu.make_async_copy(src, dst, sems.at[len(copies)]))

    for side, (msg, block, rows) in enumerate(sides):
        copy(flow.at[:, block], edge_flow.at[side])
        copy(nu.at[:, block], edge_nu.at[side])
    for msg, block, rows in sides:
        for field in range(fields):
            for ct in range(nct):
                for at, row in enumerate(rows):
                    copy(
                        state.at[:, field, block, ct, row, :],
                        msg.at[ct, pl.ds((field * 2 + at) * members, members), :],
                    )
    for one in copies:
        one.start()
    for one in copies[:4]:
        one.wait()
    for side, (msg, block, rows) in enumerate(sides):
        edge = (SUB - 1, 0)[side]
        for ct in range(nct):
            numbers = [edge_flow[side, k, ct, edge : edge + 1, :] for k in range(2)]
            numbers += [edge_nu[side, k, ct, edge : edge + 1, :] for k in range(fields)]
            numbers.append(jnp.zeros((PACK - 2 - fields, LANES), F32))
            msg[ct, pl.ds(2 * fields * members, PACK), :] = jnp.concatenate(numbers, axis=0)
    for one in copies[4:]:
        one.wait()


def pack_edges(state6, flow5, nu5):
    members, fields, r8, nct = state6.shape[:4]
    msg = jax.ShapeDtypeStruct((nct, 2 * fields * members + PACK, LANES), F32)
    edge = pltpu.VMEM((2, 2, nct, SUB, LANES), F32)
    return pl.pallas_call(
        pack_kernel,
        out_shape=[msg] * 2,
        in_specs=[pl.BlockSpec(memory_space=pl.ANY)] * 3,
        out_specs=[pl.BlockSpec(memory_space=pltpu.VMEM)] * 2,
        scratch_shapes=[edge, edge, pltpu.SemaphoreType.DMA((4 + 4 * fields * nct,))],
        compiler_params=params(56),
        name="pack_edges",
    )(state6, flow5, nu5)


def stencil_coefs(flow_x, flow_y, nu, col, width):
    east = nu - jnp.minimum(flow_x, 0.0)
    west = nu + jnp.maximum(flow_x, 0.0)
    north = nu - jnp.minimum(flow_y, 0.0)
    south = nu + jnp.maximum(flow_y, 0.0)
    centre = 1.0 - (east + west + north + south)
    south = jnp.where(col == 0, 0.0, south)
    north = jnp.where(col == width - 1, 0.0, north)
    return centre, west, east, south, north


def stencil_row(src, row, dst, coef, members):
    nct = src.shape[1]
    lane = lax.broadcasted_iota(jnp.int32, (SUB, LANES), 1)
    first, last = lane == 0, lane == LANES - 1
    weights = [
        [coef(k, ct, row) for k in range(5)] for ct in range(nct)
    ]
    for group in range(members // SUB):
        rows = pl.ds(group * SUB, SUB)
        mid = [src[row + 1, ct, rows, :] for ct in range(nct)]
        right = [pltpu.roll(x, 1, 1) for x in mid]
        left = [pltpu.roll(x, LANES - 1, 1) for x in mid]
        for ct in range(nct):
            south = jnp.where(first, right[(ct - 1) % nct], right[ct])
            north = jnp.where(last, left[(ct + 1) % nct], left[ct])
            centre, west, east, w_s, w_n = weights[ct]
            value = (
                centre * mid[ct]
                + west * src[row, ct, rows, :]
                + east * src[row + 2, ct, rows, :]
                + (w_s * south + w_n * north)
            )
            dst(ct, rows, value)


def forecast_rows(
    lo, hi, field, member, state, flow, nu, before, after, q0, q1, coef, put, wait=None
):
    members, fields, r8, nct = state.shape[:4]
    rows = r8 * SUB
    half = nct // 2
    width = nct * LANES
    flat = state.reshape(members * fields * r8 * nct * SUB, LANES)
    stride = fields * r8 * nct * SUB
    offset = min(field, fields - 1) * r8 * nct * SUB
    room = coef.shape[2]
    coef_flat = coef.reshape(5 * nct * room, LANES)

    def weight(k, ct, at):
        return coef_flat[pl.ds((k * nct + ct) * room + at, SUB, stride=0), :]

    def phys(ct):
        return lax.rem(ct + member * half, nct)

    first = max(lo - 1, 0) // SUB
    count = min(hi, rows - 1) // SUB + 1 - first
    base = first * SUB - SUB
    for ct in range(nct):
        at = phys(ct)
        col = lax.broadcasted_iota(jnp.int32, (count * SUB, LANES), 1) + at * LANES
        block = pl.ds(first, count)
        flow_x = flow[0, block, at, :, :].reshape(count * SUB, LANES)
        flow_y = flow[1, block, at, :, :].reshape(count * SUB, LANES)
        diffuse = nu[field, block, at, :, :].reshape(count * SUB, LANES)
        for k, value in enumerate(stencil_coefs(flow_x, flow_y, diffuse, col, width)):
            coef[k, ct, pl.ds(SUB, count * SUB), :] = value
        for msg, row, needed in ((before, -1, lo == 0), (after, rows, hi == rows)):
            if needed:
                edge = [msg[at, pl.ds(4 * members + k, 1), :] for k in (0, 1, 2 + field)]
                for k, value in enumerate(stencil_coefs(*edge, col[0:1], width)):
                    coef[k, ct, pl.ds(row - base, 1), :] = value
        if lo == 0:
            for k in range(2):
                q0[k, ct] = before[at, pl.ds((2 * field + k) * members, members), :]
        if hi == rows:
            for k in range(2):
                q0[rows - lo + 2 + k, ct] = after[at, pl.ds((2 * field + k) * members, members), :]

    start = max(lo - 2, 0)
    stop = min(hi + 2, rows)

    def load(i):
        r = start + i
        for ct in range(nct):
            at = (lax.div(r, SUB) * nct + phys(ct)) * SUB + lax.rem(r, SUB) + offset
            q0[r - lo + 2, ct] = flat[pl.ds(at, members, stride=stride), :]

    if wait is None:
        rows_loop(stop - start, 8, load)
    else:
        for block in range(r8):
            wait(block)
            for r in range(max(start, block * SUB), min(stop, block * SUB + SUB)):
                load(r - start)

    def first_step(i):
        def keep(ct, at, value):
            q1[i, ct, at, :] = value

        stencil_row(
            q0, i, keep, lambda k, ct, r: weight(k, ct, r + (lo - 1 - base)), members
        )

    rows_loop(hi - lo + 2, 6, first_step)

    def second_step(i):
        def keep(ct, at, value):
            put(lo + i, ct, at, value)

        stencil_row(
            q1, i, keep, lambda k, ct, r: weight(k, ct, r + (lo - base)), members
        )

    rows_loop(hi - lo, 4, second_step)


def row_scratch(count, nct, members):
    return [
        pltpu.VMEM((count + 4, nct, members, LANES), F32),
        pltpu.VMEM((count + 2, nct, members, LANES), F32),
        pltpu.VMEM((5, nct, -(-count // SUB) * SUB + 4 * SUB, LANES), F32),
    ]


def cost(count, nct, members):
    cells = count * nct * members * LANES
    return pl.CostEstimate(flops=40 * cells, bytes_accessed=8 * cells, transcendentals=0)


SMEM = pl.BlockSpec(memory_space=pltpu.SMEM)
VMEM = pl.BlockSpec(memory_space=pltpu.VMEM)


def inner_kernel(lo, hi, ids, state, flow, nu, full, send, held, sems, *scratch):
    half = full.shape[1] // 2
    copies = [
        pltpu.make_async_copy(state.at[:, 0, block], held.at[:, 0, block], sems.at[block])
        for block in range(state.shape[2])
    ]
    for one in copies:
        one.start()

    def put(r, ct, at, value):
        full[r, ct, at, :] = value
        if ct >= half:
            send[r, ct - half, at, :] = value

    forecast_rows(
        lo, hi, 0, ids[1], held, flow, nu, None, None, *scratch, put,
        wait=lambda block: copies[block].wait(),
    )


def forecast_inner(ids, state6, flow5, nu5):
    members, _, r8, nct = state6.shape[:4]
    rows = r8 * SUB
    return pl.pallas_call(
        functools.partial(inner_kernel, 2, rows - 2),
        out_shape=[
            jax.ShapeDtypeStruct((rows, nct, members, LANES), F32),
            jax.ShapeDtypeStruct((rows, nct // 2, members, LANES), F32),
        ],
        in_specs=[SMEM, pl.BlockSpec(memory_space=pl.ANY)] + [VMEM] * 2,
        out_specs=[VMEM] * 2,
        scratch_shapes=[
            pltpu.VMEM((members, 1, r8, nct, SUB, LANES), F32),
            pltpu.SemaphoreType.DMA((r8,)),
            *row_scratch(rows - 4, nct, members),
        ],
        compiler_params=params(44),
        cost_estimate=cost(rows, nct, members),
        name="forecast_inner",
    )(ids, state6, flow5, nu5)


def edge_kernel(
    ids, cells, owner, order, state, flow, nu, before, after, full_in, send_in,
    full, send, keep, away, *scratch
):
    members, _, r8, nct = state.shape[:4]
    rows = r8 * SUB
    half = nct // 2
    width = nct * LANES
    slab, member = ids[0], ids[1]

    def put(r, ct, at, value):
        full[r, ct, at, :] = value
        if ct >= half:
            send[r, ct - half, at, :] = value

    for lo, hi in ((0, 2), (rows - 2, rows)):
        forecast_rows(lo, hi, 0, member, state, flow, nu, before, after, *scratch, put)

    nobs = cells.shape[1]
    bits = width.bit_length() - 1
    assert width == 1 << bits
    lane = lax.broadcasted_iota(jnp.int32, (members, LANES), 1)
    for position in range(order.shape[0]):
        batch = order[position]
        mine = owner[batch] == slab
        kept = lax.rem(position, 2) == member

        def pick(tile, carry, batch=batch, mine=mine, kept=kept, position=position):
            def some(group, acc):
                for u in range(GATHER):
                    o = group * GATHER + u
                    cell = cells[batch, tile * LANES + o]
                    r = lax.shift_right_logical(cell, bits)
                    c = cell & (width - 1)
                    at = (lax.shift_right_logical(c, 7) + member * half) & (nct - 1)
                    moved = pltpu.roll(full[r, at], (o - c) & (LANES - 1), 1)
                    acc = jnp.where(lane == o, moved, acc)
                return acc

            acc = lax.fori_loop(
                0, jnp.where(mine, LANES // GATHER, 0), some, jnp.zeros((members, LANES), F32)
            )

            @pl.when(kept)
            def _():
                keep[position // 2, tile] = acc

            @pl.when(jnp.logical_not(kept))
            def _():
                away[position // 2, tile] = acc

            return carry

        lax.fori_loop(0, nobs // LANES, pick, 0)


def forecast_edges(ids, cells, owner, order, state6, flow5, nu5, before, after, full, send):
    members, _, r8, nct = state6.shape[:4]
    nb, nobs = cells.shape
    picks = jax.ShapeDtypeStruct((nb // 2, nobs // LANES, members, LANES), F32)
    return pl.pallas_call(
        edge_kernel,
        out_shape=[
            jax.ShapeDtypeStruct(full.shape, F32), jax.ShapeDtypeStruct(send.shape, F32), picks, picks,
        ],
        in_specs=[SMEM] * 4 + [VMEM] * 7,
        out_specs=[VMEM] * 4,
        input_output_aliases={9: 0, 10: 1},
        scratch_shapes=row_scratch(2, nct, members),
        compiler_params=params(8),
        cost_estimate=cost(SUB, nct, members),
        name="forecast_edges",
    )(ids, cells, owner, order, state6, flow5, nu5, before, after, full, send)


def piece_kernel(lo, hi, ids, state, flow, nu, before, after, *rest):
    own, send, *scratch = rest[-5:]
    half = own.shape[1]

    def put(r, ct, at, value):
        if ct < half:
            own[r, ct, at, :] = value
        else:
            send[r, ct - half, at, :] = value

    forecast_rows(lo, hi, 1, ids[1], state, flow, nu, before, after, *scratch, put)


def forecast_piece(lo, hi, ids, state6, flow5, nu5, before, after, done):
    members, _, r8, nct = state6.shape[:4]
    rows = r8 * SUB
    part = jax.ShapeDtypeStruct((rows, nct // 2, members, LANES), F32)
    return pl.pallas_call(
        functools.partial(piece_kernel, lo, hi),
        out_shape=[part, part],
        in_specs=[SMEM] + [VMEM] * (5 + len(done)),
        out_specs=[VMEM] * 2,
        input_output_aliases={6: 0, 7: 1} if done else {},
        scratch_shapes=row_scratch(hi - lo, nct, members),
        compiler_params=params(10),
        cost_estimate=cost(hi - lo, nct, members),
        name=f"forecast_rows_{lo}",
    )(ids, state6, flow5, nu5, before, after, *done)


def gram_kernel(ids, owner, order, keep, other, observed, variance, *outs):
    slab, member = ids[0], ids[1]
    count, tiles, members = keep.shape[:3]
    for k in range(count):
        batch = order[2 * k + member]
        mine = owner[batch] == slab
        part = count // len(outs)
        out = outs[k // part].at[k % part]

        @pl.when(jnp.logical_not(mine))
        def _():
            out[...] = jnp.zeros(out.shape, F32)

        @pl.when(mine)
        def _():
            pair = jnp.zeros(out.shape, F32)
            for t in range(tiles):
                a, b = keep[k, t], other[k, t]
                prior = jnp.concatenate(
                    [jnp.where(member == 0, a, b), jnp.where(member == 0, b, a)], axis=0
                )
                mean = jnp.sum(prior, axis=0, keepdims=True) / (2 * members)
                anomaly = prior - mean
                scaled = anomaly / variance[batch, :, pl.ds(t * LANES, LANES)]
                misfit = observed[batch, :, pl.ds(t * LANES, LANES)] - mean
                pair += lax.dot_general(
                    scaled,
                    jnp.concatenate([anomaly, misfit], axis=0),
                    (((1,), (1,)), ((), ())),
                    precision=HIGH,
                    preferred_element_type=F32,
                )
            out[...] = pair


def gram(ids, owner, order, keep, other, observed, variance):
    count, _, members, _ = keep.shape
    total = 2 * members
    smem = pl.BlockSpec(memory_space=pltpu.SMEM)
    vmem = pl.BlockSpec(memory_space=pltpu.VMEM)
    return pl.pallas_call(
        gram_kernel,
        out_shape=[jax.ShapeDtypeStruct((count // 2, total, 2 * total), F32)] * 2,
        in_specs=[smem] * 3 + [vmem] * 4,
        out_specs=[vmem] * 2,
        compiler_params=params(12),
        name="gram",
    )(ids, owner, order, keep, other, observed, variance[:, None, :])


def total(terms):
    while len(terms) > 1:
        terms = [x + y for x, y in zip(terms[::2], terms[1::2])]
    return terms[0]


def solve(inner, rhs):
    size = inner.shape[0]
    groups = size // SUB
    wide = (SUB, LANES)
    sub = lax.broadcasted_iota(jnp.int32, wide, 0)
    a = [inner[g * SUB : (g + 1) * SUB] for g in range(groups)]
    b = [rhs[g * SUB : (g + 1) * SUB] for g in range(groups)]

    def column(x, k):
        return jnp.broadcast_to(x[:, k : k + 1], wide)

    def row(x, k):
        return jnp.broadcast_to(x[k : k + 1, :], wide)

    for p in range(groups):
        cols = [[column(a[g], p * SUB + k) for k in range(SUB)] for g in range(groups)]
        c, pa, pb = cols[p], a[p], b[p]
        after = p + 1 if p + 1 < groups else None
        e = cols[after] if after else []
        for k in range(0, SUB, 2):
            ck, cl = c[k], c[k + 1]
            kk, kl, lk, ll = row(ck, k), row(cl, k), row(ck, k + 1), row(cl, k + 1)
            scale = 1.0 / (kk * ll - kl * lk)

            def pivot_rows(x, k=k, kk=kk, kl=kl, lk=lk, ll=ll):
                u, w = row(x, k), row(x, k + 1)
                return ll * u - kl * w, kk * w - lk * u

            def inside(x, n0, n1, k=k, ck=ck, cl=cl, scale=scale):
                rest = x - scale * (ck * n0 + cl * n1)
                return jnp.where(sub == k, scale * n0, jnp.where(sub == k + 1, scale * n1, rest))

            def outside(x, n0, n1, k=k, scale=scale):
                return x - scale * (e[k] * n0 + e[k + 1] * n1)

            for j in range(k + 2, SUB):
                n = pivot_rows(c[j])
                c[j] = inside(c[j], *n)
                if after:
                    e[j] = outside(e[j], *n)
            n = pivot_rows(pa)
            pa = inside(pa, *n)
            if after:
                a[after] = outside(a[after], *n)
            n = pivot_rows(pb)
            pb = inside(pb, *n)
            if after:
                b[after] = outside(b[after], *n)
        a[p], b[p] = pa, pb
        ra = [row(pa, k) for k in range(SUB)]
        rb = [row(pb, k) for k in range(SUB)]
        for g in range(groups):
            if g in (p, after):
                continue
            if p + 1 < groups:
                a[g] = a[g] - total([cols[g][k] * ra[k] for k in range(SUB)])
            b[g] = b[g] - total([cols[g][k] * rb[k] for k in range(SUB)])
    return jnp.concatenate(b, axis=0)


def chain_kernel(last, ids, mine, other, *rest):
    member = ids[1]
    count, size, _ = mine.shape
    out = rest[-1]
    eye = (
        lax.broadcasted_iota(jnp.int32, (size, 2 * size), 0)
        == lax.broadcasted_iota(jnp.int32, (size, 2 * size), 1)
    ).astype(F32)
    unit = eye[:, :size]

    def dot(x, y, lhs=1):
        return lax.dot_general(
            x, y, (((lhs,), (0,)), ((), ())), precision=HIGH, preferred_element_type=F32
        )

    def step(position, v):
        k = lax.div(position, 2)
        gh = jnp.where(lax.rem(position, 2) == member, mine[k], other[k])
        g, h = gh[:, :size], gh[:, size:]
        centred = h - jnp.sum(h, axis=1, keepdims=True) / size
        z = v[:, :size]
        gv = dot(g, v)
        both = dot(z, jnp.concatenate([gv, centred, h], axis=1), lhs=0)
        inner = both[:, : 2 * size] + (size - 1) * eye
        rhs = both[:, 2 * size :] - both[:, : 2 * size]
        return v + dot(z, solve(inner, rhs))

    if len(rest) > 1:
        start = rest[0][...]
    else:
        start = jnp.concatenate([unit - 1.0 / size, unit], axis=1)
    v = lax.fori_loop(0, 2 * count, step, start)
    if not last:
        out[...] = v
        return
    w = v[:, size:].T
    half = size // 2
    first, second = w[:, :half], w[:, half:]
    w = jnp.concatenate(
        [jnp.where(member == 0, first, second), jnp.where(member == 0, second, first)], axis=1
    )
    high = w.astype(BF16).astype(F32)
    low = w - high
    out[...] = jnp.concatenate(
        [jnp.concatenate([high, high], axis=1), jnp.concatenate([low, jnp.zeros_like(low)], axis=1)],
        axis=0,
    )


def chain(last, ids, mine, other, *start):
    size = mine.shape[1]
    return pl.pallas_call(
        functools.partial(chain_kernel, last),
        out_shape=jax.ShapeDtypeStruct(((1 + last) * size, 2 * size), F32),
        in_specs=[SMEM] + [VMEM] * (2 + len(start)),
        out_specs=VMEM,
        compiler_params=params(12),
        name="chain_last" if last else "chain_first",
    )(ids, mine, other, *start)


def apply_kernel(w_ref, own0, other0, own1, other1, out):
    field = pl.program_id(0)
    size = w_ref.shape[0] // 2
    rows, half = own0.shape[:2]
    weights = w_ref[...].astype(BF16)
    flat = out.reshape(size * half * rows, LANES)

    def run(own, other):
        for r in range(rows):
            parts = [
                jnp.concatenate([src[r, ct] for ct in range(half)], axis=1) for src in (own, other)
            ]
            high = [x.astype(BF16) for x in parts]
            low = [(x - y.astype(F32)).astype(BF16) for x, y in zip(parts, high)]
            stacked = jnp.concatenate([*high, *low], axis=0)
            result = jnp.dot(weights, stacked, preferred_element_type=F32)
            result = result[:size] + result[size:]
            for ct in range(half):
                flat[pl.ds(ct * rows + r, size, stride=half * rows), :] = result[
                    :, ct * LANES : (ct + 1) * LANES
                ]

    @pl.when(field == 0)
    def _():
        run(own0, other0)

    @pl.when(field == 1)
    def _():
        run(own1, other1)


def apply(weights, own0, other0, own1, other1):
    rows, half, members, _ = other0.shape
    size = 2 * members
    r8 = rows // SUB
    block = (SUB, half, members, LANES)
    zero = pl.BlockSpec(block, lambda f, r: (jnp.where(f == 0, r, r8 - 1), 0, 0, 0))
    one = pl.BlockSpec(block, lambda f, r: (jnp.where(f == 1, r, 0), 0, 0, 0))
    return pl.pallas_call(
        apply_kernel,
        grid=(2, r8),
        out_shape=jax.ShapeDtypeStruct((size, 2, r8, half, SUB, LANES), F32),
        in_specs=[
            pl.BlockSpec(weights.shape, lambda f, r: (0, 0)), zero, zero, one, one,
        ],
        out_specs=pl.BlockSpec((size, 1, 1, half, SUB, LANES), lambda f, r: (0, f, r, 0, 0, 0)),
        compiler_params=params(12),
        name="apply",
    )(weights, own0, other0, own1, other1)


def body(state, courant, diffusion, obs_cells, obs_owner, batch_order, obs_values, obs_error):
    slab = lax.axis_index("space")
    member = lax.axis_index("member")
    space = lax.axis_size("space")
    ids = jnp.stack([slab, member]).astype(jnp.int32)
    up = [(i, i + 1) for i in range(space - 1)]
    down = [(i + 1, i) for i in range(space - 1)]
    swap = [(0, 1), (1, 0)]

    state6, flow5, nu5 = tiled(state), tiled(courant), tiled(diffusion)
    up_edge, down_edge = pack_edges(state6, flow5, nu5)
    before = lax.ppermute(up_edge, "space", up)
    after = lax.ppermute(down_edge, "space", down)
    full0, send0 = forecast_inner(ids, state6, flow5, nu5)
    full0, send0, keep, away = forecast_edges(
        ids, obs_cells, obs_owner, batch_order, state6, flow5, nu5, before, after, full0, send0
    )
    other = lax.ppermute(away, "member", swap)
    early, late = gram(ids, obs_owner, batch_order, keep, other, obs_values, obs_error)

    rows = state.shape[2]
    pieces = [(r, r + rows // 4) for r in range(0, rows, rows // 4)]
    field1 = ()
    bits = [1 << i for i in range(space.bit_length() - 1)]

    def partner(bit):
        return [(i, i ^ bit) for i in range(space)]

    for turn, bit in enumerate(bits):
        received = [lax.ppermute(early, "space", partner(bit))]
        if turn > 0:
            received.append(lax.ppermute(late, "space", partner(bits[turn - 1])))
        if pieces:
            before, after, early, late = lax.optimization_barrier((before, after, early, late))
            field1 = forecast_piece(*pieces.pop(0), ids, state6, flow5, nu5, before, after, field1)
            received, field1 = lax.optimization_barrier((received, field1))
        early = early + received[0]
        if turn > 0:
            late = late + received[1]
    for piece in pieces:
        field1 = forecast_piece(*piece, ids, state6, flow5, nu5, before, after, field1)
    own1, send1 = field1
    early_theirs = lax.ppermute(early, "member", swap)
    late = late + lax.ppermute(late, "space", partner(bits[-1]))
    early, early_theirs, late = lax.optimization_barrier((early, early_theirs, late))
    late_theirs = lax.ppermute(late, "member", swap)
    send0, send1, early = lax.optimization_barrier((send0, send1, early))
    other0 = lax.ppermute(send0, "member", swap)
    other1 = lax.ppermute(send1, "member", swap)
    v = chain(False, ids, early, early_theirs)
    weights = chain(True, ids, late, late_theirs, v)
    return untiled(apply(weights, full0, other0, own1, other1))


def solution(mesh):
    placed = (
        P("member", None, "space", None),
        P(None, "space", None),
        P(None, "space", None),
        P(),
        P(),
        P(),
        P(),
        P(),
    )
    return jax.shard_map(
        body,
        mesh=mesh,
        in_specs=placed,
        out_specs=P(None, None, "space", "member"),
        check_vma=False,
    )
```

```python
import functools

import jax
import jax.numpy as jnp
from jax import lax
from jax.experimental import pallas as pl
from jax.experimental.pallas import tpu as pltpu
from jax.sharding import PartitionSpec as P

HIGH = lax.Precision.HIGHEST
F32 = jnp.float32
BF16 = jnp.bfloat16
LANES = 128
SUB = 8
GATHER = 32
PACK = 8


def params(mib):
    return pltpu.CompilerParams(vmem_limit_bytes=mib * 1024 * 1024)


def unrolled(count, most):
    return max(d for d in range(1, most + 1) if count % d == 0)


def rows_loop(count, most, fn):
    step = unrolled(count, most)

    def run(i, carry):
        for u in range(step):
            fn(i * step + u)
        return carry

    lax.fori_loop(0, count // step, run, 0)


def tiled(array):
    *lead, rows, cols = array.shape
    n = len(lead)
    split = array.reshape(*lead, rows // SUB, SUB, cols // LANES, LANES)
    return jnp.transpose(split, (*range(n), n, n + 2, n + 1, n + 3))


def untiled(array):
    *lead, r8, ct, sub, lanes = array.shape
    n = len(lead)
    back = jnp.transpose(array, (*range(n), n, n + 2, n + 1, n + 3))
    return back.reshape(*lead, r8 * sub, ct * lanes)


def pack_kernel(state, flow, nu, up, down, edge_flow, edge_nu, sems):
    members, fields, r8, nct = state.shape[:4]
    sides = ((up, r8 - 1, (SUB - 2, SUB - 1)), (down, 0, (0, 1)))
    copies = []

    def copy(src, dst):
        copies.append(pltpu.make_async_copy(src, dst, sems.at[len(copies)]))

    for side, (msg, block, rows) in enumerate(sides):
        copy(flow.at[:, block], edge_flow.at[side])
        copy(nu.at[:, block], edge_nu.at[side])
    for msg, block, rows in sides:
        for field in range(fields):
            for ct in range(nct):
                for at, row in enumerate(rows):
                    copy(
                        state.at[:, field, block, ct, row, :],
                        msg.at[ct, pl.ds((field * 2 + at) * members, members), :],
                    )
    for one in copies:
        one.start()
    for one in copies[:4]:
        one.wait()
    for side, (msg, block, rows) in enumerate(sides):
        edge = (SUB - 1, 0)[side]
        for ct in range(nct):
            numbers = [edge_flow[side, k, ct, edge : edge + 1, :] for k in range(2)]
            numbers += [edge_nu[side, k, ct, edge : edge + 1, :] for k in range(fields)]
            numbers.append(jnp.zeros((PACK - 2 - fields, LANES), F32))
            msg[ct, pl.ds(2 * fields * members, PACK), :] = jnp.concatenate(numbers, axis=0)
    for one in copies[4:]:
        one.wait()


def pack_edges(state6, flow5, nu5):
    members, fields, r8, nct = state6.shape[:4]
    msg = jax.ShapeDtypeStruct((nct, 2 * fields * members + PACK, LANES), F32)
    edge = pltpu.VMEM((2, 2, nct, SUB, LANES), F32)
    return pl.pallas_call(
        pack_kernel,
        out_shape=[msg] * 2,
        in_specs=[pl.BlockSpec(memory_space=pl.ANY)] * 3,
        out_specs=[pl.BlockSpec(memory_space=pltpu.VMEM)] * 2,
        scratch_shapes=[edge, edge, pltpu.SemaphoreType.DMA((4 + 4 * fields * nct,))],
        compiler_params=params(56),
        name="pack_edges",
    )(state6, flow5, nu5)


PAD = SUB


def stencil_coefs(flow_x, flow_y, nu, col, width):
    east = nu - jnp.minimum(flow_x, 0.0)
    west = nu + jnp.maximum(flow_x, 0.0)
    north = nu - jnp.minimum(flow_y, 0.0)
    south = nu + jnp.maximum(flow_y, 0.0)
    centre = 1.0 - (east + west + north + south)
    south = jnp.where(col == 0, 0.0, south)
    north = jnp.where(col == width - 1, 0.0, north)
    return centre, west, east, south, north


def fill_coefs(coef, field, member, flow, nu, blocks, before=None, after=None):
    _, r8, nct = flow.shape[:3]
    width = nct * LANES
    for ct in range(nct):
        at = lax.rem(ct + member * (nct // 2), nct)
        for first, count in blocks:
            shape = (count * SUB, LANES)
            col = lax.broadcasted_iota(jnp.int32, shape, 1) + at * LANES
            part = pl.ds(first, count)
            numbers = (flow[0, part, at], flow[1, part, at], nu[field, part, at])
            numbers = [x.reshape(shape) for x in numbers]
            for k, value in enumerate(stencil_coefs(*numbers, col, width)):
                coef[k, ct, pl.ds(PAD + first * SUB, count * SUB), :] = value
        for msg, row in ((before, PAD - 1), (after, PAD + r8 * SUB)):
            if msg is not None:
                col = lax.broadcasted_iota(jnp.int32, (1, LANES), 1) + at * LANES
                base = msg.shape[1] - PACK
                numbers = [msg[at, pl.ds(base + k, 1), :] for k in (0, 1, 2 + field)]
                for k, value in enumerate(stencil_coefs(*numbers, col, width)):
                    coef[k, ct, pl.ds(row, 1), :] = value


def stencil(mid, west, east, weights):
    nct = len(mid)
    lane = lax.broadcasted_iota(jnp.int32, (SUB, LANES), 1)
    right = [pltpu.roll(x, 1, 1) for x in mid]
    left = [pltpu.roll(x, LANES - 1, 1) for x in mid]
    out = []
    for ct in range(nct):
        south = jnp.where(lane == 0, right[(ct - 1) % nct], right[ct])
        north = jnp.where(lane == LANES - 1, left[(ct + 1) % nct], left[ct])
        centre, w_w, w_e, w_s, w_n = weights[ct]
        out.append(
            (centre * mid[ct] + w_w * west[ct]) + (w_e * east[ct] + (w_s * south + w_n * north))
        )
    return out


class Rows:
    def __init__(self, held, coef):
        self.nct, _, blocks = held.shape[-5:-2]
        self.room = blocks * SUB
        self.flat = held.reshape(held.size // LANES, LANES)
        self.coef = coef.reshape(coef.size // LANES, LANES)

    def at(self, group, ct, row):
        start = (group * self.nct + ct) * SUB * self.room + PAD + row
        return pl.ds(start, SUB, stride=self.room)

    def load(self, group, row):
        return [self.flat[self.at(group, ct, row), :] for ct in range(self.nct)]

    def weights(self, row):
        return [
            [
                self.coef[pl.ds((k * self.nct + ct) * self.room + PAD + row, SUB, stride=0), :]
                for k in range(5)
            ]
            for ct in range(self.nct)
        ]


def group_steps(group, held, between, coef, put, edges):
    groups, nct, _, blocks = held.shape[:4]
    room = blocks * SUB
    source = held.reshape(groups, nct, SUB, room, LANES)
    middle = between.reshape(nct, SUB, room, LANES)

    def block_step(block, load, store):
        at = PAD + block * SUB
        weights = [[coef[k, ct, pl.ds(at, SUB), :] for k in range(5)] for ct in range(nct)]
        for m in range(SUB):
            mid, west, east = [
                [load(ct, m, pl.ds(at + off, SUB)) for ct in range(nct)] for off in (0, -1, 1)
            ]
            for ct, value in enumerate(stencil(mid, west, east, weights)):
                store(block, ct, m, value)

    def keep(block, ct, m, value):
        middle[ct, m, pl.ds(PAD + block * SUB, SUB), :] = value

    for block in range(blocks - 2):
        block_step(block, lambda ct, m, rows: source[group, ct, m, rows, :], keep)
    if edges:
        field, inner = Rows(held, coef), Rows(between, coef)
        for row in (-1, (blocks - 2) * SUB):
            around = [field.load(group, row + off) for off in (0, -1, 1)]
            for ct, value in enumerate(stencil(*around, field.weights(row))):
                inner.flat[inner.at(0, ct, row), :] = value
    for block in range(blocks - 2):
        block_step(block, lambda ct, m, rows: middle[ct, m, rows, :], put)


def held_shape(members, nct, r8):
    return (members // SUB, nct, SUB, r8 + 2, SUB, LANES)


def cost(cells):
    return pl.CostEstimate(flops=40 * cells, bytes_accessed=8 * cells, transcendentals=0)


SMEM = pl.BlockSpec(memory_space=pltpu.SMEM)
VMEM = pl.BlockSpec(memory_space=pltpu.VMEM)


def inner_kernel(ids, state, flow, nu, full, held0, held1, between, coef, sems):
    groups, nct, _, blocks = held0.shape[:4]
    members = groups * SUB
    r8 = blocks - 2
    half = nct // 2
    member = ids[1]
    copies = []
    for field, held in ((0, held0), (1, held1)):
        for group in range(groups):
            for ct in range(nct):
                at = lax.rem(ct + member * half, nct)
                copies.append(
                    pltpu.make_async_copy(
                        state.at[pl.ds(group * SUB, SUB), field, :, at],
                        held.at[group, ct, :, pl.ds(1, r8)],
                        sems.at[len(copies)],
                    )
                )
    for one in copies:
        one.start()
    fill_coefs(coef, 0, member, flow, nu, [(0, r8)])
    flat = full.reshape(full.size // LANES, LANES)

    for group in range(groups):
        for one in copies[group * nct : (group + 1) * nct]:
            one.wait()

    def run(group, carry):
        def put(block, ct, m, value):
            start = ((ct // half) * r8 * SUB + block * SUB) * half + ct % half
            flat[pl.ds(start * members + group * SUB + m, SUB, stride=half * members), :] = value

        group_steps(group, held0, between, coef, put, False)
        return carry

    lax.fori_loop(0, groups, run, 0)
    for one in copies[groups * nct :]:
        one.wait()


def forecast_inner(ids, state6, flow5, nu5):
    members, _, r8, nct = state6.shape[:4]
    held = held_shape(members, nct, r8)
    return pl.pallas_call(
        inner_kernel,
        out_shape=[
            jax.ShapeDtypeStruct((2, r8 * SUB, nct // 2, members, LANES), F32),
            jax.ShapeDtypeStruct(held, F32),
            jax.ShapeDtypeStruct(held, F32),
        ],
        in_specs=[SMEM, pl.BlockSpec(memory_space=pl.ANY)] + [VMEM] * 2,
        out_specs=[VMEM] * 3,
        scratch_shapes=[
            pltpu.VMEM(held[1:], F32),
            pltpu.VMEM((5, nct, (r8 + 2) * SUB, LANES), F32),
            pltpu.SemaphoreType.DMA((2 * held[0] * nct,)),
        ],
        compiler_params=params(34),
        cost_estimate=cost(members * r8 * SUB * nct * LANES),
        name="forecast_inner",
    )(ids, state6, flow5, nu5)


def edge_kernel(
    ids, cells, owner, order, flow, nu, before, after, full_in, held0_in, held1_in,
    full, held0, held1, keep, away, coef
):
    groups, nct, _, blocks = held0.shape[:4]
    members = groups * SUB
    r8 = blocks - 2
    rows = r8 * SUB
    half = nct // 2
    width = nct * LANES
    slab, member = ids[0], ids[1]

    for field, held in ((0, held0), (1, held1)):
        view = Rows(held, coef)
        for ct in range(nct):
            at = lax.rem(ct + member * half, nct)
            for group in range(groups):
                for k in range(2):
                    part = pl.ds((2 * field + k) * members + group * SUB, SUB)
                    view.flat[view.at(group, ct, k - 2), :] = before[at, part, :]
                    view.flat[view.at(group, ct, rows + k), :] = after[at, part, :]

    fill_coefs(coef, 0, member, flow, nu, [(0, 1), (r8 - 1, 1)], before, after)
    view = Rows(held0, coef)
    for first in (0, rows - 2):
        for group in range(groups):
            old = {r: view.load(group, r) for r in range(first - 2, first + 4)}
            one = {
                r: stencil(old[r], old[r - 1], old[r + 1], view.weights(r))
                for r in range(first - 1, first + 3)
            }
            for r in range(first, first + 2):
                new = stencil(one[r], one[r - 1], one[r + 1], view.weights(r))
                for ct, value in enumerate(new):
                    full[ct // half, r, ct % half, pl.ds(group * SUB, SUB), :] = value

    nobs = cells.shape[1]
    bits = width.bit_length() - 1
    assert width == 1 << bits
    lane = lax.broadcasted_iota(jnp.int32, (members, LANES), 1)
    for position in range(order.shape[0]):
        batch = order[position]
        mine = owner[batch] == slab
        kept = lax.rem(position, 2) == member

        def pick(tile, carry, batch=batch, mine=mine, kept=kept, position=position):
            def some(group, acc):
                for u in range(GATHER):
                    o = group * GATHER + u
                    cell = cells[batch, tile * LANES + o]
                    r = lax.shift_right_logical(cell, bits)
                    c = cell & (width - 1)
                    at = (lax.shift_right_logical(c, 7) + member * half) & (nct - 1)
                    moved = pltpu.roll(full[at // half, r, at % half], (o - c) & (LANES - 1), 1)
                    acc = jnp.where(lane == o, moved, acc)
                return acc

            acc = lax.fori_loop(
                0, jnp.where(mine, LANES // GATHER, 0), some, jnp.zeros((members, LANES), F32)
            )

            @pl.when(kept)
            def _():
                keep[position // 2, tile] = acc

            @pl.when(jnp.logical_not(kept))
            def _():
                away[position // 2, tile] = acc

            return carry

        lax.fori_loop(0, nobs // LANES, pick, 0)


def forecast_edges(ids, cells, owner, order, flow5, nu5, before, after, full, held0, held1):
    members = full.shape[3]
    nct, _, blocks = held0.shape[1:4]
    nb, nobs = cells.shape
    picks = jax.ShapeDtypeStruct((nb // 2, nobs // LANES, members, LANES), F32)
    same = [jax.ShapeDtypeStruct(x.shape, F32) for x in (full, held0, held1)]
    return pl.pallas_call(
        edge_kernel,
        out_shape=[*same, picks, picks],
        in_specs=[SMEM] * 4 + [VMEM] * 7,
        out_specs=[VMEM] * 5,
        input_output_aliases={8: 0, 9: 1, 10: 2},
        scratch_shapes=[pltpu.VMEM((5, nct, blocks * SUB, LANES), F32)],
        compiler_params=params(6),
        cost_estimate=cost(members * SUB * nct * LANES),
        name="forecast_edges",
    )(ids, cells, owner, order, flow5, nu5, before, after, full, held0, held1)


def piece_kernel(group, ids, flow, nu, before, after, held, *rest):
    own, send, between, coef = rest[-4:]
    rows, half, members = own.shape[:3]
    flats = [x.reshape(x.size // LANES, LANES) for x in (own, send)]
    fill_coefs(coef, 1, ids[1], flow, nu, [(0, rows // SUB)], before, after)

    def put(block, ct, m, value):
        start = block * SUB * half + ct % half
        flats[ct // half][
            pl.ds(start * members + group * SUB + m, SUB, stride=half * members), :
        ] = value

    group_steps(group, held, between, coef, put, True)


def forecast_piece(group, ids, flow5, nu5, before, after, held, done):
    groups, nct, _, blocks = held.shape[:4]
    rows = (blocks - 2) * SUB
    part = jax.ShapeDtypeStruct((rows, nct // 2, groups * SUB, LANES), F32)
    return pl.pallas_call(
        functools.partial(piece_kernel, group),
        out_shape=[part, part],
        in_specs=[SMEM] + [VMEM] * (5 + len(done)),
        out_specs=[VMEM] * 2,
        input_output_aliases={6: 0, 7: 1} if done else {},
        scratch_shapes=[
            pltpu.VMEM(held.shape[1:], F32),
            pltpu.VMEM((5, nct, blocks * SUB, LANES), F32),
        ],
        compiler_params=params(6),
        cost_estimate=cost(SUB * rows * nct * LANES),
        name=f"forecast_members_{group}",
    )(ids, flow5, nu5, before, after, held, *done)


def gram_kernel(ids, owner, order, keep, other, observed, variance, gh):
    slab, member = ids[0], ids[1]
    count, tiles, members = keep.shape[:3]
    for k in range(count):
        batch = order[2 * k + member]
        mine = owner[batch] == slab
        out = gh.at[k]

        @pl.when(jnp.logical_not(mine))
        def _():
            out[...] = jnp.zeros(out.shape, F32)

        @pl.when(mine)
        def _():
            pair = jnp.zeros(out.shape, F32)
            for t in range(tiles):
                a, b = keep[k, t], other[k, t]
                prior = jnp.concatenate(
                    [jnp.where(member == 0, a, b), jnp.where(member == 0, b, a)], axis=0
                )
                mean = jnp.sum(prior, axis=0, keepdims=True) / (2 * members)
                anomaly = prior - mean
                scaled = anomaly / variance[batch, :, pl.ds(t * LANES, LANES)]
                misfit = observed[batch, :, pl.ds(t * LANES, LANES)] - mean
                pair += lax.dot_general(
                    scaled,
                    jnp.concatenate([anomaly, misfit], axis=0),
                    (((1,), (1,)), ((), ())),
                    precision=HIGH,
                    preferred_element_type=F32,
                )
            out[...] = pair


def gram(ids, owner, order, keep, other, observed, variance):
    count, _, members, _ = keep.shape
    total = 2 * members
    smem = pl.BlockSpec(memory_space=pltpu.SMEM)
    vmem = pl.BlockSpec(memory_space=pltpu.VMEM)
    return pl.pallas_call(
        gram_kernel,
        out_shape=jax.ShapeDtypeStruct((count, total, 2 * total), F32),
        in_specs=[smem] * 3 + [vmem] * 4,
        out_specs=vmem,
        compiler_params=params(12),
        name="gram",
    )(ids, owner, order, keep, other, observed, variance[:, None, :])


def total(terms):
    while len(terms) > 1:
        terms = [x + y for x, y in zip(terms[::2], terms[1::2])]
    return terms[0]


def solve(inner, rhs):
    size = inner.shape[0]
    groups = size // SUB
    wide = (SUB, LANES)
    sub = lax.broadcasted_iota(jnp.int32, wide, 0)
    a = [inner[g * SUB : (g + 1) * SUB] for g in range(groups)]
    b = [rhs[g * SUB : (g + 1) * SUB] for g in range(groups)]

    def column(x, k):
        return jnp.broadcast_to(x[:, k : k + 1], wide)

    def row(x, k):
        return jnp.broadcast_to(x[k : k + 1, :], wide)

    for p in range(groups):
        cols = [[column(a[g], p * SUB + k) for k in range(SUB)] for g in range(groups)]
        c, pa, pb = cols[p], a[p], b[p]
        after = p + 1 if p + 1 < groups else None
        e = cols[after] if after else []
        for k in range(0, SUB, 2):
            ck, cl = c[k], c[k + 1]
            kk, kl, lk, ll = row(ck, k), row(cl, k), row(ck, k + 1), row(cl, k + 1)
            scale = 1.0 / (kk * ll - kl * lk)

            def pivot_rows(x, k=k, kk=kk, kl=kl, lk=lk, ll=ll):
                u, w = row(x, k), row(x, k + 1)
                return ll * u - kl * w, kk * w - lk * u

            def inside(x, n0, n1, k=k, ck=ck, cl=cl, scale=scale):
                rest = x - scale * (ck * n0 + cl * n1)
                return jnp.where(sub == k, scale * n0, jnp.where(sub == k + 1, scale * n1, rest))

            def outside(x, n0, n1, k=k, scale=scale):
                return x - scale * (e[k] * n0 + e[k + 1] * n1)

            for j in range(k + 2, SUB):
                n = pivot_rows(c[j])
                c[j] = inside(c[j], *n)
                if after:
                    e[j] = outside(e[j], *n)
            n = pivot_rows(pa)
            pa = inside(pa, *n)
            if after:
                a[after] = outside(a[after], *n)
            n = pivot_rows(pb)
            pb = inside(pb, *n)
            if after:
                b[after] = outside(b[after], *n)
        a[p], b[p] = pa, pb
        ra = [row(pa, k) for k in range(SUB)]
        rb = [row(pb, k) for k in range(SUB)]
        for g in range(groups):
            if g in (p, after):
                continue
            if p + 1 < groups:
                a[g] = a[g] - total([cols[g][k] * ra[k] for k in range(SUB)])
            b[g] = b[g] - total([cols[g][k] * rb[k] for k in range(SUB)])
    return jnp.concatenate(b, axis=0)


def chain_kernel(last, ids, mine, other, *rest):
    member = ids[1]
    count, size, _ = mine.shape
    out = rest[-1]
    eye = (
        lax.broadcasted_iota(jnp.int32, (size, 2 * size), 0)
        == lax.broadcasted_iota(jnp.int32, (size, 2 * size), 1)
    ).astype(F32)
    unit = eye[:, :size]

    def dot(x, y, lhs=1):
        return lax.dot_general(
            x, y, (((lhs,), (0,)), ((), ())), precision=HIGH, preferred_element_type=F32
        )

    def step(position, v):
        k = lax.div(position, 2)
        gh = jnp.where(lax.rem(position, 2) == member, mine[k], other[k])
        g, h = gh[:, :size], gh[:, size:]
        centred = h - jnp.sum(h, axis=1, keepdims=True) / size
        z = v[:, :size]
        gv = dot(g, v)
        both = dot(z, jnp.concatenate([gv, centred, h], axis=1), lhs=0)
        inner = both[:, : 2 * size] + (size - 1) * eye
        rhs = both[:, 2 * size :] - both[:, : 2 * size]
        return v + dot(z, solve(inner, rhs))

    if len(rest) > 1:
        start = rest[0][...]
    else:
        start = jnp.concatenate([unit - 1.0 / size, unit], axis=1)
    v = lax.fori_loop(0, 2 * count, step, start)
    if not last:
        out[...] = v
        return
    w = v[:, size:].T
    half = size // 2
    first, second = w[:, :half], w[:, half:]
    w = jnp.concatenate(
        [jnp.where(member == 0, first, second), jnp.where(member == 0, second, first)], axis=1
    )
    high = w.astype(BF16).astype(F32)
    low = w - high
    out[...] = jnp.concatenate(
        [jnp.concatenate([high, high], axis=1), jnp.concatenate([low, jnp.zeros_like(low)], axis=1)],
        axis=0,
    )


def chain(last, ids, mine, other, *start):
    size = mine.shape[1]
    return pl.pallas_call(
        functools.partial(chain_kernel, last),
        out_shape=jax.ShapeDtypeStruct(((1 + last) * size, 2 * size), F32),
        in_specs=[SMEM] + [VMEM] * (2 + len(start)),
        out_specs=VMEM,
        compiler_params=params(12),
        name="chain_last" if last else "chain_first",
    )(ids, mine, other, *start)


def apply_kernel(w_ref, own0, other0, own1, other1, out):
    field = pl.program_id(0)
    size = w_ref.shape[0] // 2
    rows, half = own1.shape[:2]
    weights = w_ref[...].astype(BF16)
    flat = out.reshape(size * half * rows, LANES)

    def run(own, other):
        for r in range(rows):
            parts = [
                jnp.concatenate([src[r, ct] for ct in range(half)], axis=1) for src in (own, other)
            ]
            high = [x.astype(BF16) for x in parts]
            low = [(x - y.astype(F32)).astype(BF16) for x, y in zip(parts, high)]
            stacked = jnp.concatenate([*high, *low], axis=0)
            result = jnp.dot(weights, stacked, preferred_element_type=F32)
            result = result[:size] + result[size:]
            for ct in range(half):
                flat[pl.ds(ct * rows + r, size, stride=half * rows), :] = result[
                    :, ct * LANES : (ct + 1) * LANES
                ]

    @pl.when(field == 0)
    def _():
        run(own0, other0)

    @pl.when(field == 1)
    def _():
        run(own1, other1)


def apply(weights, own0, other0, own1, other1):
    rows, half, members, _ = other1.shape
    size = 2 * members
    r8 = rows // SUB
    block = (SUB, half, members, LANES)

    def zero(part):
        return pl.BlockSpec(
            (None, *block), lambda f, r: (part, jnp.where(f == 0, r, r8 - 1), 0, 0, 0)
        )

    one = pl.BlockSpec(block, lambda f, r: (jnp.where(f == 1, r, 0), 0, 0, 0))
    return pl.pallas_call(
        apply_kernel,
        grid=(2, r8),
        out_shape=jax.ShapeDtypeStruct((size, 2, r8, half, SUB, LANES), F32),
        in_specs=[
            pl.BlockSpec(weights.shape, lambda f, r: (0, 0)), zero(0), zero(1), one, one,
        ],
        out_specs=pl.BlockSpec((size, 1, 1, half, SUB, LANES), lambda f, r: (0, f, r, 0, 0, 0)),
        compiler_params=params(12),
        name="apply",
    )(weights, own0, other0, own1, other1)


def body(state, courant, diffusion, obs_cells, obs_owner, batch_order, obs_values, obs_error):
    slab = lax.axis_index("space")
    member = lax.axis_index("member")
    space = lax.axis_size("space")
    ids = jnp.stack([slab, member]).astype(jnp.int32)
    up = [(i, i + 1) for i in range(space - 1)]
    down = [(i + 1, i) for i in range(space - 1)]
    swap = [(0, 1), (1, 0)]

    state6, flow5, nu5 = tiled(state), tiled(courant), tiled(diffusion)
    up_edge, down_edge = pack_edges(state6, flow5, nu5)
    before = lax.ppermute(up_edge, "space", up)
    after = lax.ppermute(down_edge, "space", down)
    full0, held0, held1 = forecast_inner(ids, state6, flow5, nu5)
    full0, _, held1, keep, away = forecast_edges(
        ids, obs_cells, obs_owner, batch_order, flow5, nu5, before, after, full0, held0, held1
    )
    other = lax.ppermute(away, "member", swap)
    gh = gram(ids, obs_owner, batch_order, keep, other, obs_values, obs_error)

    groups = list(range(held1.shape[0]))
    field1 = ()
    bit = 1
    while bit < space:
        received = lax.ppermute(gh, "space", [(i, i ^ bit) for i in range(space)])
        if groups:
            held1, gh = lax.optimization_barrier((held1, gh))
            field1 = forecast_piece(groups.pop(0), ids, flow5, nu5, before, after, held1, field1)
            received, field1 = lax.optimization_barrier((received, field1))
        gh = gh + received
        bit *= 2
    for group in groups:
        field1 = forecast_piece(group, ids, flow5, nu5, before, after, held1, field1)
    own1, send1 = field1
    theirs = lax.ppermute(gh, "member", swap)
    full0, send1, gh, theirs = lax.optimization_barrier((full0, send1, gh, theirs))
    other0 = lax.ppermute(full0, "member", swap)
    other1 = lax.ppermute(send1, "member", swap)
    weights = chain(True, ids, gh, theirs)
    return untiled(apply(weights, full0, other0, own1, other1))


def solution(mesh):
    placed = (
        P("member", None, "space", None),
        P(None, "space", None),
        P(None, "space", None),
        P(),
        P(),
        P(),
        P(),
        P(),
    )
    return jax.shard_map(
        body,
        mesh=mesh,
        in_specs=placed,
        out_specs=P(None, None, "space", "member"),
        check_vma=False,
    )
```

```python
import functools

import jax
import jax.numpy as jnp
from jax import lax
from jax.experimental import pallas as pl
from jax.experimental.pallas import tpu as pltpu
from jax.sharding import PartitionSpec as P

HIGH = lax.Precision.HIGHEST
F32 = jnp.float32
BF16 = jnp.bfloat16
LANES = 128
SUB = 8
GATHER = 32
PACK = 8


def params(mib):
    return pltpu.CompilerParams(vmem_limit_bytes=mib * 1024 * 1024)


def unrolled(count, most):
    return max(d for d in range(1, most + 1) if count % d == 0)


def rows_loop(count, most, fn):
    step = unrolled(count, most)

    def run(i, carry):
        for u in range(step):
            fn(i * step + u)
        return carry

    lax.fori_loop(0, count // step, run, 0)


def tiled(array):
    *lead, rows, cols = array.shape
    n = len(lead)
    split = array.reshape(*lead, rows // SUB, SUB, cols // LANES, LANES)
    return jnp.transpose(split, (*range(n), n, n + 2, n + 1, n + 3))


def untiled(array):
    *lead, r8, ct, sub, lanes = array.shape
    n = len(lead)
    back = jnp.transpose(array, (*range(n), n, n + 2, n + 1, n + 3))
    return back.reshape(*lead, r8 * sub, ct * lanes)


def pack_kernel(state, flow, nu, up, down, edge_flow, edge_nu, sems):
    members, fields, r8, nct = state.shape[:4]
    sides = ((up, r8 - 1, (SUB - 2, SUB - 1)), (down, 0, (0, 1)))
    copies = []

    def copy(src, dst):
        copies.append(pltpu.make_async_copy(src, dst, sems.at[len(copies)]))

    for side, (msg, block, rows) in enumerate(sides):
        copy(flow.at[:, block], edge_flow.at[side])
        copy(nu.at[:, block], edge_nu.at[side])
    for msg, block, rows in sides:
        for field in range(fields):
            for ct in range(nct):
                for at, row in enumerate(rows):
                    copy(
                        state.at[:, field, block, ct, row, :],
                        msg.at[ct, pl.ds((field * 2 + at) * members, members), :],
                    )
    for one in copies:
        one.start()
    for one in copies[:4]:
        one.wait()
    for side, (msg, block, rows) in enumerate(sides):
        edge = (SUB - 1, 0)[side]
        for ct in range(nct):
            numbers = [edge_flow[side, k, ct, edge : edge + 1, :] for k in range(2)]
            numbers += [edge_nu[side, k, ct, edge : edge + 1, :] for k in range(fields)]
            numbers.append(jnp.zeros((PACK - 2 - fields, LANES), F32))
            msg[ct, pl.ds(2 * fields * members, PACK), :] = jnp.concatenate(numbers, axis=0)
    for one in copies[4:]:
        one.wait()


def pack_edges(state6, flow5, nu5):
    members, fields, r8, nct = state6.shape[:4]
    msg = jax.ShapeDtypeStruct((nct, 2 * fields * members + PACK, LANES), F32)
    edge = pltpu.VMEM((2, 2, nct, SUB, LANES), F32)
    return pl.pallas_call(
        pack_kernel,
        out_shape=[msg] * 2,
        in_specs=[pl.BlockSpec(memory_space=pl.ANY)] * 3,
        out_specs=[pl.BlockSpec(memory_space=pltpu.VMEM)] * 2,
        scratch_shapes=[edge, edge, pltpu.SemaphoreType.DMA((4 + 4 * fields * nct,))],
        compiler_params=params(56),
        name="pack_edges",
    )(state6, flow5, nu5)


PAD = SUB


def stencil_coefs(flow_x, flow_y, nu, col, width):
    east = nu - jnp.minimum(flow_x, 0.0)
    west = nu + jnp.maximum(flow_x, 0.0)
    north = nu - jnp.minimum(flow_y, 0.0)
    south = nu + jnp.maximum(flow_y, 0.0)
    centre = 1.0 - (east + west + north + south)
    south = jnp.where(col == 0, 0.0, south)
    north = jnp.where(col == width - 1, 0.0, north)
    return centre, west, east, south, north


def fill_coefs(coef, field, flow, nu, blocks, before=None, after=None):
    _, r8, nct = flow.shape[:3]
    width = nct * LANES
    for ct in range(nct):
        for first, count in blocks:
            shape = (count * SUB, LANES)
            col = lax.broadcasted_iota(jnp.int32, shape, 1) + ct * LANES
            part = pl.ds(first, count)
            numbers = (flow[0, part, ct], flow[1, part, ct], nu[field, part, ct])
            numbers = [x.reshape(shape) for x in numbers]
            for k, value in enumerate(stencil_coefs(*numbers, col, width)):
                coef[k, ct, pl.ds(PAD + first * SUB, count * SUB), :] = value
        for msg, row in ((before, PAD - 1), (after, PAD + r8 * SUB)):
            if msg is not None:
                col = lax.broadcasted_iota(jnp.int32, (1, LANES), 1) + ct * LANES
                base = msg.shape[1] - PACK
                numbers = [msg[ct, pl.ds(base + k, 1), :] for k in (0, 1, 2 + field)]
                for k, value in enumerate(stencil_coefs(*numbers, col, width)):
                    coef[k, ct, pl.ds(row, 1), :] = value


def stencil(mid, west, east, weights):
    nct = len(mid)
    lane = lax.broadcasted_iota(jnp.int32, (SUB, LANES), 1)
    right = [pltpu.roll(x, 1, 1) for x in mid]
    left = [pltpu.roll(x, LANES - 1, 1) for x in mid]
    out = []
    for ct in range(nct):
        south = jnp.where(lane == 0, right[(ct - 1) % nct], right[ct])
        north = jnp.where(lane == LANES - 1, left[(ct + 1) % nct], left[ct])
        centre, w_w, w_e, w_s, w_n = weights[ct]
        out.append(
            (centre * mid[ct] + w_w * west[ct]) + (w_e * east[ct] + (w_s * south + w_n * north))
        )
    return out


class Rows:
    def __init__(self, held, coef):
        self.nct, _, blocks = held.shape[-5:-2]
        self.room = blocks * SUB
        self.flat = held.reshape(held.size // LANES, LANES)
        self.coef = coef.reshape(coef.size // LANES, LANES)

    def at(self, group, ct, row):
        start = (group * self.nct + ct) * SUB * self.room + PAD + row
        return pl.ds(start, SUB, stride=self.room)

    def load(self, group, row):
        return [self.flat[self.at(group, ct, row), :] for ct in range(self.nct)]

    def weights(self, row):
        return [
            [
                self.coef[pl.ds((k * self.nct + ct) * self.room + PAD + row, SUB, stride=0), :]
                for k in range(5)
            ]
            for ct in range(self.nct)
        ]


def group_steps(group, held, between, coef, put, edges):
    groups, nct, _, blocks = held.shape[:4]
    room = blocks * SUB
    source = held.reshape(groups, nct, SUB, room, LANES)
    middle = between.reshape(nct, SUB, room, LANES)

    def block_step(block, load, store):
        at = PAD + block * SUB
        weights = [[coef[k, ct, pl.ds(at, SUB), :] for k in range(5)] for ct in range(nct)]
        for m in range(SUB):
            mid, west, east = [
                [load(ct, m, pl.ds(at + off, SUB)) for ct in range(nct)] for off in (0, -1, 1)
            ]
            for ct, value in enumerate(stencil(mid, west, east, weights)):
                store(block, ct, m, value)

    def keep(block, ct, m, value):
        middle[ct, m, pl.ds(PAD + block * SUB, SUB), :] = value

    for block in range(blocks - 2):
        block_step(block, lambda ct, m, rows: source[group, ct, m, rows, :], keep)
    if edges:
        field, inner = Rows(held, coef), Rows(between, coef)
        for row in (-1, (blocks - 2) * SUB):
            around = [field.load(group, row + off) for off in (0, -1, 1)]
            for ct, value in enumerate(stencil(*around, field.weights(row))):
                inner.flat[inner.at(0, ct, row), :] = value
    for block in range(blocks - 2):
        block_step(block, lambda ct, m, rows: middle[ct, m, rows, :], put)


def held_shape(members, nct, r8):
    return (members // SUB, nct, SUB, r8 + 2, SUB, LANES)


def cost(cells):
    return pl.CostEstimate(flops=40 * cells, bytes_accessed=8 * cells, transcendentals=0)


SMEM = pl.BlockSpec(memory_space=pltpu.SMEM)
VMEM = pl.BlockSpec(memory_space=pltpu.VMEM)


def inner_kernel(state, flow, nu, full, held0, held1, between, coef, sems):
    groups, nct, _, blocks = held0.shape[:4]
    members = groups * SUB
    r8 = blocks - 2

    def copies(field, held, group):
        return [
            pltpu.make_async_copy(
                state.at[pl.ds(group * SUB, SUB), field, :, ct],
                held.at[group, ct, :, pl.ds(1, r8)],
                sems.at[field, group, ct],
            )
            for ct in range(nct)
        ]

    for group in range(groups):
        for one in copies(0, held0, group):
            one.start()
    fill_coefs(coef, 0, flow, nu, [(0, r8)])
    flat = full.reshape(full.size // LANES, LANES)

    def run(group, carry):
        for one in copies(0, held0, group):
            one.wait()
        for one in copies(1, held1, group):
            one.start()

        def put(block, ct, m, value):
            start = (block * SUB * nct + ct) * members + group * SUB + m
            flat[pl.ds(start, SUB, stride=nct * members), :] = value

        group_steps(group, held0, between, coef, put, False)
        return carry

    lax.fori_loop(0, groups, run, 0)
    for group in range(groups):
        for one in copies(1, held1, group):
            one.wait()


def forecast_inner(state6, flow5, nu5):
    members, _, r8, nct = state6.shape[:4]
    held = held_shape(members, nct, r8)
    return pl.pallas_call(
        inner_kernel,
        out_shape=[
            jax.ShapeDtypeStruct((r8 * SUB, nct, members, LANES), F32),
            jax.ShapeDtypeStruct(held, F32),
            jax.ShapeDtypeStruct(held, F32),
        ],
        in_specs=[pl.BlockSpec(memory_space=pl.ANY)] + [VMEM] * 2,
        out_specs=[VMEM] * 3,
        scratch_shapes=[
            pltpu.VMEM(held[1:], F32),
            pltpu.VMEM((5, nct, (r8 + 2) * SUB, LANES), F32),
            pltpu.SemaphoreType.DMA((2, held[0], nct)),
        ],
        compiler_params=params(34),
        cost_estimate=cost(members * r8 * SUB * nct * LANES),
        name="forecast_inner",
    )(state6, flow5, nu5)


def edge_kernel(
    ids, cells, owner, order, flow, nu, before, after, full_in, held0_in, held1_in,
    full, held0, held1, keep, away, coef
):
    groups, nct, _, blocks = held0.shape[:4]
    members = groups * SUB
    r8 = blocks - 2
    rows = r8 * SUB
    slab, member = ids[0], ids[1]

    for field, held in ((0, held0), (1, held1)):
        view = Rows(held, coef)
        for ct in range(nct):
            for group in range(groups):
                for k in range(2):
                    part = pl.ds((2 * field + k) * members + group * SUB, SUB)
                    view.flat[view.at(group, ct, k - 2), :] = before[ct, part, :]
                    view.flat[view.at(group, ct, rows + k), :] = after[ct, part, :]

    fill_coefs(coef, 0, flow, nu, [(0, 1), (r8 - 1, 1)], before, after)
    view = Rows(held0, coef)
    for first in (0, rows - 2):
        for group in range(groups):
            old = {r: view.load(group, r) for r in range(first - 2, first + 4)}
            one = {
                r: stencil(old[r], old[r - 1], old[r + 1], view.weights(r))
                for r in range(first - 1, first + 3)
            }
            for r in range(first, first + 2):
                new = stencil(one[r], one[r - 1], one[r + 1], view.weights(r))
                for ct, value in enumerate(new):
                    full[r, ct, pl.ds(group * SUB, SUB), :] = value

    nobs = cells.shape[1]
    tiles = full.reshape(rows * nct, members, LANES)
    lane = lax.broadcasted_iota(jnp.int32, (members, LANES), 1)
    for position in range(order.shape[0]):
        batch = order[position]
        mine = owner[batch] == slab
        kept = lax.rem(position, 2) == member

        def pick(tile, carry, batch=batch, mine=mine, kept=kept, position=position):
            def some(group, acc):
                for u in range(GATHER):
                    o = group * GATHER + u
                    cell = cells[batch, tile * LANES + o]
                    tile_at = lax.shift_right_logical(cell, LANES.bit_length() - 1)
                    moved = pltpu.roll(tiles[tile_at], (o - cell) & (LANES - 1), 1)
                    acc = jnp.where(lane == o, moved, acc)
                return acc

            acc = lax.fori_loop(
                0, jnp.where(mine, LANES // GATHER, 0), some, jnp.zeros((members, LANES), F32)
            )

            @pl.when(kept)
            def _():
                keep[position // 2, tile] = acc

            @pl.when(jnp.logical_not(kept))
            def _():
                away[position // 2, tile] = acc

            return carry

        lax.fori_loop(0, nobs // LANES, pick, 0)


def forecast_edges(ids, cells, owner, order, flow5, nu5, before, after, full, held0, held1):
    members = full.shape[2]
    nct, _, blocks = held0.shape[1:4]
    nb, nobs = cells.shape
    picks = jax.ShapeDtypeStruct((nb // 2, nobs // LANES, members, LANES), F32)
    same = [jax.ShapeDtypeStruct(x.shape, F32) for x in (full, held0, held1)]
    return pl.pallas_call(
        edge_kernel,
        out_shape=[*same, picks, picks],
        in_specs=[SMEM] * 4 + [VMEM] * 7,
        out_specs=[VMEM] * 5,
        input_output_aliases={8: 0, 9: 1, 10: 2},
        scratch_shapes=[pltpu.VMEM((5, nct, blocks * SUB, LANES), F32)],
        compiler_params=params(6),
        cost_estimate=cost(members * SUB * nct * LANES),
        name="forecast_edges",
    )(ids, cells, owner, order, flow5, nu5, before, after, full, held0, held1)


def piece_kernel(group, flow, nu, before, after, held, *rest):
    full, between, coef = rest[-3:]
    rows, nct, members = full.shape[:3]
    flat = full.reshape(full.size // LANES, LANES)
    fill_coefs(coef, 1, flow, nu, [(0, rows // SUB)], before, after)

    def put(block, ct, m, value):
        start = (block * SUB * nct + ct) * members + group * SUB + m
        flat[pl.ds(start, SUB, stride=nct * members), :] = value

    group_steps(group, held, between, coef, put, True)


def forecast_piece(group, flow5, nu5, before, after, held, done):
    groups, nct, _, blocks = held.shape[:4]
    rows = (blocks - 2) * SUB
    return pl.pallas_call(
        functools.partial(piece_kernel, group),
        out_shape=jax.ShapeDtypeStruct((rows, nct, groups * SUB, LANES), F32),
        in_specs=[VMEM] * (5 + len(done)),
        out_specs=VMEM,
        input_output_aliases={5: 0} if done else {},
        scratch_shapes=[
            pltpu.VMEM(held.shape[1:], F32),
            pltpu.VMEM((5, nct, blocks * SUB, LANES), F32),
        ],
        compiler_params=params(6),
        cost_estimate=cost(SUB * rows * nct * LANES),
        name=f"forecast_members_{group}",
    )(flow5, nu5, before, after, held, *done)


def gram_kernel(ids, owner, order, keep, other, observed, variance, gh):
    slab, member = ids[0], ids[1]
    count, tiles, members = keep.shape[:3]
    for k in range(count):
        batch = order[2 * k + member]
        mine = owner[batch] == slab
        out = gh.at[k]

        @pl.when(jnp.logical_not(mine))
        def _():
            out[...] = jnp.zeros(out.shape, F32)

        @pl.when(mine)
        def _():
            pair = jnp.zeros(out.shape, F32)
            for t in range(tiles):
                a, b = keep[k, t], other[k, t]
                prior = jnp.concatenate(
                    [jnp.where(member == 0, a, b), jnp.where(member == 0, b, a)], axis=0
                )
                mean = jnp.sum(prior, axis=0, keepdims=True) / (2 * members)
                anomaly = prior - mean
                scaled = anomaly / variance[batch, :, pl.ds(t * LANES, LANES)]
                misfit = observed[batch, :, pl.ds(t * LANES, LANES)] - mean
                pair += lax.dot_general(
                    scaled,
                    jnp.concatenate([anomaly, misfit], axis=0),
                    (((1,), (1,)), ((), ())),
                    precision=HIGH,
                    preferred_element_type=F32,
                )
            out[...] = pair


def gram(ids, owner, order, keep, other, observed, variance):
    count, _, members, _ = keep.shape
    total = 2 * members
    smem = pl.BlockSpec(memory_space=pltpu.SMEM)
    vmem = pl.BlockSpec(memory_space=pltpu.VMEM)
    return pl.pallas_call(
        gram_kernel,
        out_shape=jax.ShapeDtypeStruct((count, total, 2 * total), F32),
        in_specs=[smem] * 3 + [vmem] * 4,
        out_specs=vmem,
        compiler_params=params(12),
        name="gram",
    )(ids, owner, order, keep, other, observed, variance[:, None, :])


def total(terms):
    while len(terms) > 1:
        terms = [x + y for x, y in zip(terms[::2], terms[1::2])]
    return terms[0]


def solve(inner, rhs):
    size = inner.shape[0]
    groups = size // SUB
    wide = (SUB, LANES)
    sub = lax.broadcasted_iota(jnp.int32, wide, 0)
    a = [inner[g * SUB : (g + 1) * SUB] for g in range(groups)]
    b = [rhs[g * SUB : (g + 1) * SUB] for g in range(groups)]

    def column(x, k):
        return jnp.broadcast_to(x[:, k : k + 1], wide)

    def row(x, k):
        return jnp.broadcast_to(x[k : k + 1, :], wide)

    for p in range(groups):
        cols = [[column(a[g], p * SUB + k) for k in range(SUB)] for g in range(groups)]
        c, pa, pb = cols[p], a[p], b[p]
        after = p + 1 if p + 1 < groups else None
        e = cols[after] if after else []
        for k in range(0, SUB, 2):
            ck, cl = c[k], c[k + 1]
            kk, kl, lk, ll = row(ck, k), row(cl, k), row(ck, k + 1), row(cl, k + 1)
            scale = 1.0 / (kk * ll - kl * lk)

            def pivot_rows(x, k=k, kk=kk, kl=kl, lk=lk, ll=ll):
                u, w = row(x, k), row(x, k + 1)
                return ll * u - kl * w, kk * w - lk * u

            def inside(x, n0, n1, k=k, ck=ck, cl=cl, scale=scale):
                rest = x - scale * (ck * n0 + cl * n1)
                return jnp.where(sub == k, scale * n0, jnp.where(sub == k + 1, scale * n1, rest))

            def outside(x, n0, n1, k=k, scale=scale):
                return x - scale * (e[k] * n0 + e[k + 1] * n1)

            for j in range(k + 2, SUB):
                n = pivot_rows(c[j])
                c[j] = inside(c[j], *n)
                if after:
                    e[j] = outside(e[j], *n)
            n = pivot_rows(pa)
            pa = inside(pa, *n)
            if after:
                a[after] = outside(a[after], *n)
            n = pivot_rows(pb)
            pb = inside(pb, *n)
            if after:
                b[after] = outside(b[after], *n)
        a[p], b[p] = pa, pb
        ra = [row(pa, k) for k in range(SUB)]
        rb = [row(pb, k) for k in range(SUB)]
        for g in range(groups):
            if g in (p, after):
                continue
            if p + 1 < groups:
                a[g] = a[g] - total([cols[g][k] * ra[k] for k in range(SUB)])
            b[g] = b[g] - total([cols[g][k] * rb[k] for k in range(SUB)])
    return jnp.concatenate(b, axis=0)


def chain_kernel(last, ids, mine, other, *rest):
    member = ids[1]
    count, size, _ = mine.shape
    out = rest[-1]
    eye = (
        lax.broadcasted_iota(jnp.int32, (size, 2 * size), 0)
        == lax.broadcasted_iota(jnp.int32, (size, 2 * size), 1)
    ).astype(F32)
    unit = eye[:, :size]

    def dot(x, y, lhs=1):
        return lax.dot_general(
            x, y, (((lhs,), (0,)), ((), ())), precision=HIGH, preferred_element_type=F32
        )

    def step(position, v):
        k = lax.div(position, 2)
        gh = jnp.where(lax.rem(position, 2) == member, mine[k], other[k])
        g, h = gh[:, :size], gh[:, size:]
        centred = h - jnp.sum(h, axis=1, keepdims=True) / size
        z = v[:, :size]
        known = dot(z, jnp.concatenate([centred, h], axis=1), lhs=0)
        both = dot(z, dot(g, v), lhs=0)
        return v + dot(z, solve(both + (size - 1) * eye, known - both))

    if len(rest) > 1:
        start = rest[0][...]
    else:
        start = jnp.concatenate([unit - 1.0 / size, unit], axis=1)
    v = lax.fori_loop(0, 2 * count, step, start)
    if not last:
        out[...] = v
        return
    w = v[:, size:].T
    half = size // 2
    first, second = w[:, :half], w[:, half:]
    w = jnp.concatenate(
        [jnp.where(member == 0, first, second), jnp.where(member == 0, second, first)], axis=1
    )
    high = w.astype(BF16).astype(F32)
    low = w - high
    out[...] = jnp.concatenate(
        [jnp.concatenate([high, high], axis=1), jnp.concatenate([low, jnp.zeros_like(low)], axis=1)],
        axis=0,
    )


def chain(last, ids, mine, other, *start):
    size = mine.shape[1]
    return pl.pallas_call(
        functools.partial(chain_kernel, last),
        out_shape=jax.ShapeDtypeStruct(((1 + last) * size, 2 * size), F32),
        in_specs=[SMEM] + [VMEM] * (2 + len(start)),
        out_specs=VMEM,
        compiler_params=params(12),
        name="chain_last" if last else "chain_first",
    )(ids, mine, other, *start)


def apply_kernel(ids, w_ref, own0, other0, own1, other1, out):
    del ids
    field = pl.program_id(0)
    size = w_ref.shape[0] // 2
    rows, half = own0.shape[:2]
    weights = w_ref[...].astype(BF16)
    flat = out.reshape(size * half * rows, LANES)
    wide = 2

    def run(own, other):
        for first in range(0, rows, wide):
            places = [(r, ct) for r in range(first, first + wide) for ct in range(half)]
            parts = [jnp.concatenate([src[at] for at in places], axis=1) for src in (own, other)]
            high = [x.astype(BF16) for x in parts]
            low = [(x - y.astype(F32)).astype(BF16) for x, y in zip(parts, high)]
            stacked = jnp.concatenate([*high, *low], axis=0)
            result = jnp.dot(weights, stacked, preferred_element_type=F32)
            result = result[:size] + result[size:]
            for k, (r, ct) in enumerate(places):
                flat[pl.ds(ct * rows + r, size, stride=half * rows), :] = result[
                    :, k * LANES : (k + 1) * LANES
                ]

    @pl.when(field == 0)
    def _():
        run(own0, other0)

    @pl.when(field == 1)
    def _():
        run(own1, other1)


def apply(ids, weights, own0, other0, own1, other1):
    rows, nct, members, _ = own0.shape
    size = 2 * members
    half = nct // 2
    r8 = rows // SUB
    block = (SUB, half, members, LANES)
    zero = pl.BlockSpec(block, lambda f, r, ids: (jnp.where(f == 0, r, r8 - 1), ids[1], 0, 0))
    one = pl.BlockSpec(block, lambda f, r, ids: (jnp.where(f == 1, r, 0), ids[1], 0, 0))
    return pl.pallas_call(
        apply_kernel,
        out_shape=jax.ShapeDtypeStruct((size, 2, r8, half, SUB, LANES), F32),
        grid_spec=pltpu.PrefetchScalarGridSpec(
            num_scalar_prefetch=1,
            grid=(2, r8),
            in_specs=[
                pl.BlockSpec(weights.shape, lambda f, r, ids: (0, 0)), zero, zero, one, one,
            ],
            out_specs=pl.BlockSpec(
                (size, 1, 1, half, SUB, LANES), lambda f, r, ids: (0, f, r, 0, 0, 0)
            ),
        ),
        compiler_params=params(12),
        name="apply",
    )(ids, weights, own0, other0, own1, other1)


def body(state, courant, diffusion, obs_cells, obs_owner, batch_order, obs_values, obs_error):
    slab = lax.axis_index("space")
    member = lax.axis_index("member")
    space = lax.axis_size("space")
    ids = jnp.stack([slab, member]).astype(jnp.int32)
    up = [(i, i + 1) for i in range(space - 1)]
    down = [(i + 1, i) for i in range(space - 1)]
    swap = [(0, 1), (1, 0)]

    state6, flow5, nu5 = tiled(state), tiled(courant), tiled(diffusion)
    up_edge, down_edge = pack_edges(state6, flow5, nu5)
    before = lax.ppermute(up_edge, "space", up)
    after = lax.ppermute(down_edge, "space", down)
    full0, held0, held1 = forecast_inner(state6, flow5, nu5)
    full0, _, held1, keep, away = forecast_edges(
        ids, obs_cells, obs_owner, batch_order, flow5, nu5, before, after, full0, held0, held1
    )
    other = lax.ppermute(away, "member", swap)
    gh = gram(ids, obs_owner, batch_order, keep, other, obs_values, obs_error)

    groups = list(range(held1.shape[0]))
    field1 = ()
    bit = 1
    while bit < space:
        received = lax.ppermute(gh, "space", [(i, i ^ bit) for i in range(space)])
        if groups:
            held1, gh = lax.optimization_barrier((held1, gh))
            field1 = forecast_piece(groups.pop(0), flow5, nu5, before, after, held1, field1)
            received, field1 = lax.optimization_barrier((received, (field1,)))
        gh = gh + received
        bit *= 2
    for group in groups:
        field1 = (forecast_piece(group, flow5, nu5, before, after, held1, field1),)
    (full1,) = field1
    theirs = lax.ppermute(gh, "member", swap)
    full0, full1, gh, theirs = lax.optimization_barrier((full0, full1, gh, theirs))
    other0 = lax.ppermute(full0, "member", swap)
    other1 = lax.ppermute(full1, "member", swap)
    weights = chain(True, ids, gh, theirs)
    return untiled(apply(ids, weights, full0, other0, full1, other1))


def solution(mesh):
    placed = (
        P("member", None, "space", None),
        P(None, "space", None),
        P(None, "space", None),
        P(),
        P(),
        P(),
        P(),
        P(),
    )
    return jax.shard_map(
        body,
        mesh=mesh,
        in_specs=placed,
        out_specs=P(None, None, "space", "member"),
        check_vma=False,
    )
```

```python
import functools

import jax
import jax.numpy as jnp
from jax import lax
from jax.experimental import pallas as pl
from jax.experimental.pallas import tpu as pltpu
from jax.sharding import PartitionSpec as P

HIGH = lax.Precision.HIGHEST
F32 = jnp.float32
BF16 = jnp.bfloat16
LANES = 128
SUB = 8
GATHER = 32
PACK = 8


def params(mib):
    return pltpu.CompilerParams(vmem_limit_bytes=mib * 1024 * 1024)


def unrolled(count, most):
    return max(d for d in range(1, most + 1) if count % d == 0)


def rows_loop(count, most, fn):
    step = unrolled(count, most)

    def run(i, carry):
        for u in range(step):
            fn(i * step + u)
        return carry

    lax.fori_loop(0, count // step, run, 0)


def tiled(array):
    *lead, rows, cols = array.shape
    n = len(lead)
    split = array.reshape(*lead, rows // SUB, SUB, cols // LANES, LANES)
    return jnp.transpose(split, (*range(n), n, n + 2, n + 1, n + 3))


def untiled(array):
    *lead, r8, ct, sub, lanes = array.shape
    n = len(lead)
    back = jnp.transpose(array, (*range(n), n, n + 2, n + 1, n + 3))
    return back.reshape(*lead, r8 * sub, ct * lanes)


def pack_kernel(state, flow, nu, up, down, edge_flow, edge_nu, sems):
    members, fields, r8, nct = state.shape[:4]
    sides = ((up, r8 - 1, (SUB - 2, SUB - 1)), (down, 0, (0, 1)))
    copies = []

    def copy(src, dst):
        copies.append(pltpu.make_async_copy(src, dst, sems.at[len(copies)]))

    for side, (msg, block, rows) in enumerate(sides):
        copy(flow.at[:, block], edge_flow.at[side])
        copy(nu.at[:, block], edge_nu.at[side])
    for msg, block, rows in sides:
        for field in range(fields):
            for ct in range(nct):
                for at, row in enumerate(rows):
                    copy(
                        state.at[:, field, block, ct, row, :],
                        msg.at[ct, pl.ds((field * 2 + at) * members, members), :],
                    )
    for one in copies:
        one.start()
    for one in copies[:4]:
        one.wait()
    for side, (msg, block, rows) in enumerate(sides):
        edge = (SUB - 1, 0)[side]
        for ct in range(nct):
            numbers = [edge_flow[side, k, ct, edge : edge + 1, :] for k in range(2)]
            numbers += [edge_nu[side, k, ct, edge : edge + 1, :] for k in range(fields)]
            numbers.append(jnp.zeros((PACK - 2 - fields, LANES), F32))
            msg[ct, pl.ds(2 * fields * members, PACK), :] = jnp.concatenate(numbers, axis=0)
    for one in copies[4:]:
        one.wait()


def pack_edges(state6, flow5, nu5):
    members, fields, r8, nct = state6.shape[:4]
    msg = jax.ShapeDtypeStruct((nct, 2 * fields * members + PACK, LANES), F32)
    edge = pltpu.VMEM((2, 2, nct, SUB, LANES), F32)
    return pl.pallas_call(
        pack_kernel,
        out_shape=[msg] * 2,
        in_specs=[pl.BlockSpec(memory_space=pl.ANY)] * 3,
        out_specs=[pl.BlockSpec(memory_space=pltpu.VMEM)] * 2,
        scratch_shapes=[edge, edge, pltpu.SemaphoreType.DMA((4 + 4 * fields * nct,))],
        compiler_params=params(56),
        name="pack_edges",
    )(state6, flow5, nu5)


PAD = SUB


def stencil_coefs(flow_x, flow_y, nu, col, width):
    east = nu - jnp.minimum(flow_x, 0.0)
    west = nu + jnp.maximum(flow_x, 0.0)
    north = nu - jnp.minimum(flow_y, 0.0)
    south = nu + jnp.maximum(flow_y, 0.0)
    centre = 1.0 - (east + west + north + south)
    south = jnp.where(col == 0, 0.0, south)
    north = jnp.where(col == width - 1, 0.0, north)
    return centre, west, east, south, north


def fill_coefs(coef, field, flow, nu, blocks, before=None, after=None):
    _, r8, nct = flow.shape[:3]
    width = nct * LANES
    for ct in range(nct):
        for first, count in blocks:
            shape = (count * SUB, LANES)
            col = lax.broadcasted_iota(jnp.int32, shape, 1) + ct * LANES
            part = pl.ds(first, count)
            numbers = (flow[0, part, ct], flow[1, part, ct], nu[field, part, ct])
            numbers = [x.reshape(shape) for x in numbers]
            for k, value in enumerate(stencil_coefs(*numbers, col, width)):
                coef[k, ct, pl.ds(PAD + first * SUB, count * SUB), :] = value
        for msg, row in ((before, PAD - 1), (after, PAD + r8 * SUB)):
            if msg is not None:
                col = lax.broadcasted_iota(jnp.int32, (1, LANES), 1) + ct * LANES
                base = msg.shape[1] - PACK
                numbers = [msg[ct, pl.ds(base + k, 1), :] for k in (0, 1, 2 + field)]
                for k, value in enumerate(stencil_coefs(*numbers, col, width)):
                    coef[k, ct, pl.ds(row, 1), :] = value


def stencil(mid, west, east, weights):
    nct = len(mid)
    lane = lax.broadcasted_iota(jnp.int32, (SUB, LANES), 1)
    right = [pltpu.roll(x, 1, 1) for x in mid]
    left = [pltpu.roll(x, LANES - 1, 1) for x in mid]
    out = []
    for ct in range(nct):
        south = jnp.where(lane == 0, right[(ct - 1) % nct], right[ct])
        north = jnp.where(lane == LANES - 1, left[(ct + 1) % nct], left[ct])
        centre, w_w, w_e, w_s, w_n = weights[ct]
        out.append(
            (centre * mid[ct] + w_w * west[ct]) + (w_e * east[ct] + (w_s * south + w_n * north))
        )
    return out


class Rows:
    def __init__(self, held, coef):
        self.nct, _, blocks = held.shape[-5:-2]
        self.room = blocks * SUB
        self.flat = held.reshape(held.size // LANES, LANES)
        self.coef = coef.reshape(coef.size // LANES, LANES)

    def at(self, group, ct, row):
        start = (group * self.nct + ct) * SUB * self.room + PAD + row
        return pl.ds(start, SUB, stride=self.room)

    def load(self, group, row):
        return [self.flat[self.at(group, ct, row), :] for ct in range(self.nct)]

    def weights(self, row):
        return [
            [
                self.coef[pl.ds((k * self.nct + ct) * self.room + PAD + row, SUB, stride=0), :]
                for k in range(5)
            ]
            for ct in range(self.nct)
        ]


def group_steps(group, held, between, coef, put, edges):
    groups, nct, _, blocks = held.shape[:4]
    room = blocks * SUB
    source = held.reshape(groups, nct, SUB, room, LANES)
    middle = between.reshape(nct, SUB, room, LANES)

    def block_step(block, load, store):
        at = PAD + block * SUB
        weights = [[coef[k, ct, pl.ds(at, SUB), :] for k in range(5)] for ct in range(nct)]
        for m in range(SUB):
            mid, west, east = [
                [load(ct, m, pl.ds(at + off, SUB)) for ct in range(nct)] for off in (0, -1, 1)
            ]
            for ct, value in enumerate(stencil(mid, west, east, weights)):
                store(block, ct, m, value)

    def keep(block, ct, m, value):
        middle[ct, m, pl.ds(PAD + block * SUB, SUB), :] = value

    for block in range(blocks - 2):
        block_step(block, lambda ct, m, rows: source[group, ct, m, rows, :], keep)
    if edges:
        field, inner = Rows(held, coef), Rows(between, coef)
        for row in (-1, (blocks - 2) * SUB):
            around = [field.load(group, row + off) for off in (0, -1, 1)]
            for ct, value in enumerate(stencil(*around, field.weights(row))):
                inner.flat[inner.at(0, ct, row), :] = value
    for block in range(blocks - 2):
        block_step(block, lambda ct, m, rows: middle[ct, m, rows, :], put)


def held_shape(members, nct, r8):
    return (members // SUB, nct, SUB, r8 + 2, SUB, LANES)


def cost(cells):
    return pl.CostEstimate(flops=40 * cells, bytes_accessed=8 * cells, transcendentals=0)


SMEM = pl.BlockSpec(memory_space=pltpu.SMEM)
VMEM = pl.BlockSpec(memory_space=pltpu.VMEM)


def inner_kernel(state, flow, nu, full, held0, held1, between, coef, sems):
    groups, nct, _, blocks = held0.shape[:4]
    members = groups * SUB
    r8 = blocks - 2

    def copies(field, held, group):
        return [
            pltpu.make_async_copy(
                state.at[pl.ds(group * SUB, SUB), field, :, ct],
                held.at[group, ct, :, pl.ds(1, r8)],
                sems.at[field, group, ct],
            )
            for ct in range(nct)
        ]

    for group in range(groups):
        for one in copies(0, held0, group):
            one.start()
    fill_coefs(coef, 0, flow, nu, [(0, r8)])
    flat = full.reshape(full.size // LANES, LANES)

    def run(group, carry):
        for one in copies(0, held0, group):
            one.wait()
        for one in copies(1, held1, group):
            one.start()

        def put(block, ct, m, value):
            start = (block * SUB * nct + ct) * members + group * SUB + m
            flat[pl.ds(start, SUB, stride=nct * members), :] = value

        group_steps(group, held0, between, coef, put, False)
        return carry

    lax.fori_loop(0, groups, run, 0)
    for group in range(groups):
        for one in copies(1, held1, group):
            one.wait()


def forecast_inner(state6, flow5, nu5):
    members, _, r8, nct = state6.shape[:4]
    held = held_shape(members, nct, r8)
    return pl.pallas_call(
        inner_kernel,
        out_shape=[
            jax.ShapeDtypeStruct((r8 * SUB, nct, members, LANES), F32),
            jax.ShapeDtypeStruct(held, F32),
            jax.ShapeDtypeStruct(held, F32),
        ],
        in_specs=[pl.BlockSpec(memory_space=pl.ANY)] + [VMEM] * 2,
        out_specs=[VMEM] * 3,
        scratch_shapes=[
            pltpu.VMEM(held[1:], F32),
            pltpu.VMEM((5, nct, (r8 + 2) * SUB, LANES), F32),
            pltpu.SemaphoreType.DMA((2, held[0], nct)),
        ],
        compiler_params=params(34),
        cost_estimate=cost(members * r8 * SUB * nct * LANES),
        name="forecast_inner",
    )(state6, flow5, nu5)


def edge_kernel(
    ids, cells, owner, order, flow, nu, before, after, full_in, held0_in, held1_in,
    full, held0, held1, keep, away, coef
):
    groups, nct, _, blocks = held0.shape[:4]
    members = groups * SUB
    r8 = blocks - 2
    rows = r8 * SUB
    slab, member = ids[0], ids[1]

    for field, held in ((0, held0), (1, held1)):
        view = Rows(held, coef)
        for ct in range(nct):
            for group in range(groups):
                for k in range(2):
                    part = pl.ds((2 * field + k) * members + group * SUB, SUB)
                    view.flat[view.at(group, ct, k - 2), :] = before[ct, part, :]
                    view.flat[view.at(group, ct, rows + k), :] = after[ct, part, :]

    fill_coefs(coef, 0, flow, nu, [(0, 1), (r8 - 1, 1)], before, after)
    view = Rows(held0, coef)
    for first in (0, rows - 2):
        for group in range(groups):
            old = {r: view.load(group, r) for r in range(first - 2, first + 4)}
            one = {
                r: stencil(old[r], old[r - 1], old[r + 1], view.weights(r))
                for r in range(first - 1, first + 3)
            }
            for r in range(first, first + 2):
                new = stencil(one[r], one[r - 1], one[r + 1], view.weights(r))
                for ct, value in enumerate(new):
                    full[r, ct, pl.ds(group * SUB, SUB), :] = value

    nobs = cells.shape[1]
    tiles = full.reshape(rows * nct, members, LANES)
    lane = lax.broadcasted_iota(jnp.int32, (members, LANES), 1)
    for position in range(order.shape[0]):
        batch = order[position]
        mine = owner[batch] == slab
        kept = lax.rem(position, 2) == member

        def pick(tile, carry, batch=batch, mine=mine, kept=kept, position=position):
            def some(group, acc):
                for u in range(GATHER):
                    o = group * GATHER + u
                    cell = cells[batch, tile * LANES + o]
                    tile_at = lax.shift_right_logical(cell, LANES.bit_length() - 1)
                    moved = pltpu.roll(tiles[tile_at], (o - cell) & (LANES - 1), 1)
                    acc = jnp.where(lane == o, moved, acc)
                return acc

            acc = lax.fori_loop(
                0, jnp.where(mine, LANES // GATHER, 0), some, jnp.zeros((members, LANES), F32)
            )

            @pl.when(kept)
            def _():
                keep[position // 2, tile] = acc

            @pl.when(jnp.logical_not(kept))
            def _():
                away[position // 2, tile] = acc

            return carry

        lax.fori_loop(0, nobs // LANES, pick, 0)


def forecast_edges(ids, cells, owner, order, flow5, nu5, before, after, full, held0, held1):
    members = full.shape[2]
    nct, _, blocks = held0.shape[1:4]
    nb, nobs = cells.shape
    picks = jax.ShapeDtypeStruct((nb // 2, nobs // LANES, members, LANES), F32)
    same = [jax.ShapeDtypeStruct(x.shape, F32) for x in (full, held0, held1)]
    return pl.pallas_call(
        edge_kernel,
        out_shape=[*same, picks, picks],
        in_specs=[SMEM] * 4 + [VMEM] * 7,
        out_specs=[VMEM] * 5,
        input_output_aliases={8: 0, 9: 1, 10: 2},
        scratch_shapes=[pltpu.VMEM((5, nct, blocks * SUB, LANES), F32)],
        compiler_params=params(6),
        cost_estimate=cost(members * SUB * nct * LANES),
        name="forecast_edges",
    )(ids, cells, owner, order, flow5, nu5, before, after, full, held0, held1)


def piece_kernel(group, flow, nu, before, after, held, *rest):
    full, between, coef = rest[-3:]
    rows, nct, members = full.shape[:3]
    flat = full.reshape(full.size // LANES, LANES)
    fill_coefs(coef, 1, flow, nu, [(0, rows // SUB)], before, after)

    def put(block, ct, m, value):
        start = (block * SUB * nct + ct) * members + group * SUB + m
        flat[pl.ds(start, SUB, stride=nct * members), :] = value

    group_steps(group, held, between, coef, put, True)


def forecast_piece(group, flow5, nu5, before, after, held, done):
    groups, nct, _, blocks = held.shape[:4]
    rows = (blocks - 2) * SUB
    return pl.pallas_call(
        functools.partial(piece_kernel, group),
        out_shape=jax.ShapeDtypeStruct((rows, nct, groups * SUB, LANES), F32),
        in_specs=[VMEM] * (5 + len(done)),
        out_specs=VMEM,
        input_output_aliases={5: 0} if done else {},
        scratch_shapes=[
            pltpu.VMEM(held.shape[1:], F32),
            pltpu.VMEM((5, nct, blocks * SUB, LANES), F32),
        ],
        compiler_params=params(6),
        cost_estimate=cost(SUB * rows * nct * LANES),
        name=f"forecast_members_{group}",
    )(flow5, nu5, before, after, held, *done)


def gram_kernel(ids, owner, order, keep, other, observed, variance, gh):
    slab, member = ids[0], ids[1]
    count, tiles, members = keep.shape[:3]
    for k in range(count):
        batch = order[2 * k + member]
        mine = owner[batch] == slab
        out = gh.at[k]

        @pl.when(jnp.logical_not(mine))
        def _():
            out[...] = jnp.zeros(out.shape, F32)

        @pl.when(mine)
        def _():
            pair = jnp.zeros(out.shape, F32)
            for t in range(tiles):
                a, b = keep[k, t], other[k, t]
                prior = jnp.concatenate(
                    [jnp.where(member == 0, a, b), jnp.where(member == 0, b, a)], axis=0
                )
                mean = jnp.sum(prior, axis=0, keepdims=True) / (2 * members)
                anomaly = prior - mean
                scaled = anomaly / variance[batch, :, pl.ds(t * LANES, LANES)]
                misfit = observed[batch, :, pl.ds(t * LANES, LANES)] - mean
                pair += lax.dot_general(
                    scaled,
                    jnp.concatenate([anomaly, misfit], axis=0),
                    (((1,), (1,)), ((), ())),
                    precision=HIGH,
                    preferred_element_type=F32,
                )
            h = lax.dot_general(
                pair[:, 2 * members :], rotation(2 * members), (((1,), (0,)), ((), ())),
                precision=HIGH, preferred_element_type=F32,
            )
            out[...] = jnp.concatenate([pair[:, : 2 * members], h], axis=1)


def gram(ids, owner, order, keep, other, observed, variance):
    count, _, members, _ = keep.shape
    total = 2 * members
    smem = pl.BlockSpec(memory_space=pltpu.SMEM)
    vmem = pl.BlockSpec(memory_space=pltpu.VMEM)
    return pl.pallas_call(
        gram_kernel,
        out_shape=jax.ShapeDtypeStruct((count, total, 2 * total), F32),
        in_specs=[smem] * 3 + [vmem] * 4,
        out_specs=vmem,
        compiler_params=params(12),
        name="gram",
    )(ids, owner, order, keep, other, observed, variance[:, None, :])


def rotation(size):
    step = size**-0.5
    row = lax.broadcasted_iota(jnp.int32, (size, size), 0)
    col = lax.broadcasted_iota(jnp.int32, (size, size), 1)
    v_row = (row == size - 1).astype(F32) - step
    v_col = (col == size - 1).astype(F32) - step
    return (row == col).astype(F32) - v_row * v_col / (1.0 - step)


def total(terms):
    while len(terms) > 1:
        terms = [x + y for x, y in zip(terms[::2], terms[1::2])]
    return terms[0]


def eliminate(a, b, rows_a, rows_b):
    groups = a.shape[0] // SUB
    wide = (SUB, LANES)
    sub = lax.broadcasted_iota(jnp.int32, wide, 0)
    a = [a[g * SUB : (g + 1) * SUB] for g in range(groups)]
    b = [b[g * SUB : (g + 1) * SUB] for g in range(groups)]
    plain, scaled = [], []

    def column(x, k):
        return jnp.broadcast_to(x[:, k : k + 1], wide)

    def row(x, k):
        return jnp.broadcast_to(x[k : k + 1, :], wide)

    for p in range(groups):
        cols = {
            g: [column(a[g], p * SUB + k) for k in range(SUB)] for g in range(p, groups)
        }
        c, pa, pb = cols[p], a[p], b[p]
        plain.append(pb)
        after = p + 1 if p + 1 < groups else None
        e = cols[after] if after else []
        for k in range(0, SUB, 2):
            ck, cl = c[k], c[k + 1]
            kk, kl, lk, ll = row(ck, k), row(cl, k), row(ck, k + 1), row(cl, k + 1)
            scale = 1.0 / (kk * ll - kl * lk)

            def pivot_rows(x, k=k, kk=kk, kl=kl, lk=lk, ll=ll):
                u, w = row(x, k), row(x, k + 1)
                return ll * u - kl * w, kk * w - lk * u

            def inside(x, n0, n1, k=k, ck=ck, cl=cl, scale=scale):
                rest = x - scale * (ck * n0 + cl * n1)
                return jnp.where(sub == k, scale * n0, jnp.where(sub == k + 1, scale * n1, rest))

            def outside(x, n0, n1, k=k, scale=scale):
                return x - scale * (e[k] * n0 + e[k + 1] * n1)

            for j in range(k + 2, SUB):
                n = pivot_rows(c[j])
                c[j] = inside(c[j], *n)
                if after:
                    e[j] = outside(e[j], *n)
            if after:
                n = pivot_rows(pa)
                pa = inside(pa, *n)
                a[after] = outside(a[after], *n)
            n = pivot_rows(pb)
            pb = inside(pb, *n)
            if after:
                b[after] = outside(b[after], *n)
        scaled.append(pb)
        if p + 2 < groups:
            here = p % 2
            rows_a[here] = pa
            rows_b[here] = pb
            ra = [rows_a[here, pl.ds(k, SUB, stride=0), :] for k in range(SUB)]
            rb = [rows_b[here, pl.ds(k, SUB, stride=0), :] for k in range(SUB)]
            for g in range(p + 2, groups):
                a[g] = a[g] - total([cols[g][k] * ra[k] for k in range(SUB)])
                b[g] = b[g] - total([cols[g][k] * rb[k] for k in range(SUB)])
    return jnp.concatenate(plain, axis=0), jnp.concatenate(scaled, axis=0)


def chain_kernel(ids, mine, other, out, rows_a, rows_b):
    member = ids[1]
    count, size, width = mine.shape
    row = lax.broadcasted_iota(jnp.int32, (size, width), 0)
    lane = lax.broadcasted_iota(jnp.int32, (size, width), 1)
    diagonal = jnp.where(row == lane, size - 1.0, 0.0)

    def dot(x, y, lhs, rhs):
        return lax.dot_general(
            x, y, (((lhs,), (rhs,)), ((), ())), precision=HIGH, preferred_element_type=F32
        )

    def step(position, vt):
        k = lax.div(position, 2)
        gh = jnp.where(lax.rem(position, 2) == member, mine[k], other[k])
        zt = jnp.where(row == size - 1, 0.0, vt)
        s = dot(zt[:, :size], gh, 1, 0)
        v = vt[:, :size]
        t = dot(s[:, :size], jnp.concatenate([v, v], axis=0), 1, 1)
        a = jnp.where(lane == size - 1, 0.0, t) + diagonal
        b = jnp.where(lane < size, zt, s - t)
        plain, scaled = eliminate(a, b, rows_a, rows_b)
        return vt + dot(plain, scaled, 0, 0)[size:]

    unit = rotation(size)
    start = jnp.concatenate([unit, jnp.zeros_like(unit)], axis=1)
    vt = lax.fori_loop(0, 2 * count, step, start)
    w = dot(unit, vt[:, :size], 1, 0)
    half = size // 2
    first, second = w[:, :half], w[:, half:]
    w = jnp.concatenate(
        [jnp.where(member == 0, first, second), jnp.where(member == 0, second, first)], axis=1
    )
    high = w.astype(BF16).astype(F32)
    low = w - high
    out[...] = jnp.concatenate(
        [jnp.concatenate([high, high], axis=1), jnp.concatenate([low, jnp.zeros_like(low)], axis=1)],
        axis=0,
    )


def chain(ids, mine, other):
    size = mine.shape[1]
    rows = pltpu.VMEM((2, SUB, LANES), F32)
    return pl.pallas_call(
        chain_kernel,
        out_shape=jax.ShapeDtypeStruct((2 * size, 2 * size), F32),
        in_specs=[SMEM] + [VMEM] * 2,
        out_specs=VMEM,
        scratch_shapes=[rows, rows],
        compiler_params=params(12),
        name="chain",
    )(ids, mine, other)


def apply_kernel(ids, w_ref, own0, other0, own1, other1, out):
    del ids
    field = pl.program_id(0)
    size = w_ref.shape[0] // 2
    rows, half = own0.shape[:2]
    weights = w_ref[...].astype(BF16)
    flat = out.reshape(size * half * rows, LANES)
    wide = 1

    def run(own, other):
        for first in range(0, rows, wide):
            places = [(r, ct) for r in range(first, first + wide) for ct in range(half)]
            parts = [jnp.concatenate([src[at] for at in places], axis=1) for src in (own, other)]
            high = [x.astype(BF16) for x in parts]
            low = [(x - y.astype(F32)).astype(BF16) for x, y in zip(parts, high)]
            stacked = jnp.concatenate([*high, *low], axis=0)
            result = jnp.dot(weights, stacked, preferred_element_type=F32)
            result = result[:size] + result[size:]
            for k, (r, ct) in enumerate(places):
                flat[pl.ds(ct * rows + r, size, stride=half * rows), :] = result[
                    :, k * LANES : (k + 1) * LANES
                ]

    @pl.when(field == 0)
    def _():
        run(own0, other0)

    @pl.when(field == 1)
    def _():
        run(own1, other1)


def apply(ids, weights, own0, other0, own1, other1):
    rows, nct, members, _ = own0.shape
    size = 2 * members
    half = nct // 2
    r8 = rows // SUB
    block = (SUB, half, members, LANES)
    zero = pl.BlockSpec(block, lambda f, r, ids: (jnp.where(f == 0, r, r8 - 1), ids[1], 0, 0))
    one = pl.BlockSpec(block, lambda f, r, ids: (jnp.where(f == 1, r, 0), ids[1], 0, 0))
    return pl.pallas_call(
        apply_kernel,
        out_shape=jax.ShapeDtypeStruct((size, 2, r8, half, SUB, LANES), F32),
        grid_spec=pltpu.PrefetchScalarGridSpec(
            num_scalar_prefetch=1,
            grid=(2, r8),
            in_specs=[
                pl.BlockSpec(weights.shape, lambda f, r, ids: (0, 0)), zero, zero, one, one,
            ],
            out_specs=pl.BlockSpec(
                (size, 1, 1, half, SUB, LANES), lambda f, r, ids: (0, f, r, 0, 0, 0)
            ),
        ),
        compiler_params=params(12),
        name="apply",
    )(ids, weights, own0, other0, own1, other1)


def body(state, courant, diffusion, obs_cells, obs_owner, batch_order, obs_values, obs_error):
    slab = lax.axis_index("space")
    member = lax.axis_index("member")
    space = lax.axis_size("space")
    ids = jnp.stack([slab, member]).astype(jnp.int32)
    up = [(i, i + 1) for i in range(space - 1)]
    down = [(i + 1, i) for i in range(space - 1)]
    swap = [(0, 1), (1, 0)]

    state6, flow5, nu5 = tiled(state), tiled(courant), tiled(diffusion)
    up_edge, down_edge = pack_edges(state6, flow5, nu5)
    before = lax.ppermute(up_edge, "space", up)
    after = lax.ppermute(down_edge, "space", down)
    full0, held0, held1 = forecast_inner(state6, flow5, nu5)
    full0, _, held1, keep, away = forecast_edges(
        ids, obs_cells, obs_owner, batch_order, flow5, nu5, before, after, full0, held0, held1
    )
    other = lax.ppermute(away, "member", swap)
    gh = gram(ids, obs_owner, batch_order, keep, other, obs_values, obs_error)

    groups = list(range(held1.shape[0]))
    field1 = ()
    bit = 1
    while bit < space:
        received = lax.ppermute(gh, "space", [(i, i ^ bit) for i in range(space)])
        if groups:
            held1, gh = lax.optimization_barrier((held1, gh))
            field1 = forecast_piece(groups.pop(0), flow5, nu5, before, after, held1, field1)
            received, field1 = lax.optimization_barrier((received, (field1,)))
        gh = gh + received
        bit *= 2
    for group in groups:
        field1 = (forecast_piece(group, flow5, nu5, before, after, held1, field1),)
    (full1,) = field1
    theirs = lax.ppermute(gh, "member", swap)
    full0, full1, gh, theirs = lax.optimization_barrier((full0, full1, gh, theirs))
    other0 = lax.ppermute(full0, "member", swap)
    other1 = lax.ppermute(full1, "member", swap)
    weights = chain(ids, gh, theirs)
    return untiled(apply(ids, weights, full0, other0, full1, other1))


def solution(mesh):
    placed = (
        P("member", None, "space", None),
        P(None, "space", None),
        P(None, "space", None),
        P(),
        P(),
        P(),
        P(),
        P(),
    )
    return jax.shard_map(
        body,
        mesh=mesh,
        in_specs=placed,
        out_specs=P(None, None, "space", "member"),
        check_vma=False,
    )
```

```python
import functools

import jax
import jax.numpy as jnp
from jax import lax
from jax.experimental import pallas as pl
from jax.experimental.pallas import tpu as pltpu
from jax.sharding import PartitionSpec as P

HIGH = lax.Precision.HIGHEST
F32 = jnp.float32
BF16 = jnp.bfloat16
LANES = 128
SUB = 8
GATHER = 32
PACK = 8


def params(mib):
    return pltpu.CompilerParams(vmem_limit_bytes=mib * 1024 * 1024)


def unrolled(count, most):
    return max(d for d in range(1, most + 1) if count % d == 0)


def rows_loop(count, most, fn):
    step = unrolled(count, most)

    def run(i, carry):
        for u in range(step):
            fn(i * step + u)
        return carry

    lax.fori_loop(0, count // step, run, 0)


def tiled(array):
    *lead, rows, cols = array.shape
    n = len(lead)
    split = array.reshape(*lead, rows // SUB, SUB, cols // LANES, LANES)
    return jnp.transpose(split, (*range(n), n, n + 2, n + 1, n + 3))


def untiled(array):
    *lead, r8, ct, sub, lanes = array.shape
    n = len(lead)
    back = jnp.transpose(array, (*range(n), n, n + 2, n + 1, n + 3))
    return back.reshape(*lead, r8 * sub, ct * lanes)


def pack_kernel(state, flow, nu, up, down, edge_flow, edge_nu, sems):
    members, fields, r8, nct = state.shape[:4]
    sides = ((up, r8 - 1, (SUB - 2, SUB - 1)), (down, 0, (0, 1)))
    copies = []

    def copy(src, dst):
        copies.append(pltpu.make_async_copy(src, dst, sems.at[len(copies)]))

    for side, (msg, block, rows) in enumerate(sides):
        copy(flow.at[:, block], edge_flow.at[side])
        copy(nu.at[:, block], edge_nu.at[side])
    for msg, block, rows in sides:
        for field in range(fields):
            for ct in range(nct):
                for at, row in enumerate(rows):
                    copy(
                        state.at[:, field, block, ct, row, :],
                        msg.at[ct, pl.ds((field * 2 + at) * members, members), :],
                    )
    for one in copies:
        one.start()
    for one in copies[:4]:
        one.wait()
    for side, (msg, block, rows) in enumerate(sides):
        edge = (SUB - 1, 0)[side]
        for ct in range(nct):
            numbers = [edge_flow[side, k, ct, edge : edge + 1, :] for k in range(2)]
            numbers += [edge_nu[side, k, ct, edge : edge + 1, :] for k in range(fields)]
            numbers.append(jnp.zeros((PACK - 2 - fields, LANES), F32))
            msg[ct, pl.ds(2 * fields * members, PACK), :] = jnp.concatenate(numbers, axis=0)
    for one in copies[4:]:
        one.wait()


def pack_edges(state6, flow5, nu5):
    members, fields, r8, nct = state6.shape[:4]
    msg = jax.ShapeDtypeStruct((nct, 2 * fields * members + PACK, LANES), F32)
    edge = pltpu.VMEM((2, 2, nct, SUB, LANES), F32)
    return pl.pallas_call(
        pack_kernel,
        out_shape=[msg] * 2,
        in_specs=[pl.BlockSpec(memory_space=pl.ANY)] * 3,
        out_specs=[pl.BlockSpec(memory_space=pltpu.VMEM)] * 2,
        scratch_shapes=[edge, edge, pltpu.SemaphoreType.DMA((4 + 4 * fields * nct,))],
        compiler_params=params(56),
        name="pack_edges",
    )(state6, flow5, nu5)


PAD = SUB


def stencil_coefs(flow_x, flow_y, nu, col, width):
    east = nu - jnp.minimum(flow_x, 0.0)
    west = nu + jnp.maximum(flow_x, 0.0)
    north = nu - jnp.minimum(flow_y, 0.0)
    south = nu + jnp.maximum(flow_y, 0.0)
    centre = 1.0 - (east + west + north + south)
    south = jnp.where(col == 0, 0.0, south)
    north = jnp.where(col == width - 1, 0.0, north)
    return centre, west, east, south, north


def fill_coefs(coef, field, flow, nu, blocks, before=None, after=None):
    _, r8, nct = flow.shape[:3]
    width = nct * LANES
    for ct in range(nct):
        for first, count in blocks:
            shape = (count * SUB, LANES)
            col = lax.broadcasted_iota(jnp.int32, shape, 1) + ct * LANES
            part = pl.ds(first, count)
            numbers = (flow[0, part, ct], flow[1, part, ct], nu[field, part, ct])
            numbers = [x.reshape(shape) for x in numbers]
            for k, value in enumerate(stencil_coefs(*numbers, col, width)):
                coef[k, ct, pl.ds(PAD + first * SUB, count * SUB), :] = value
        for msg, row in ((before, PAD - 1), (after, PAD + r8 * SUB)):
            if msg is not None:
                col = lax.broadcasted_iota(jnp.int32, (1, LANES), 1) + ct * LANES
                base = msg.shape[1] - PACK
                numbers = [msg[ct, pl.ds(base + k, 1), :] for k in (0, 1, 2 + field)]
                for k, value in enumerate(stencil_coefs(*numbers, col, width)):
                    coef[k, ct, pl.ds(row, 1), :] = value


def stencil(mid, west, east, weights):
    nct = len(mid)
    lane = lax.broadcasted_iota(jnp.int32, (SUB, LANES), 1)
    right = [pltpu.roll(x, 1, 1) for x in mid]
    left = [pltpu.roll(x, LANES - 1, 1) for x in mid]
    out = []
    for ct in range(nct):
        south = jnp.where(lane == 0, right[(ct - 1) % nct], right[ct])
        north = jnp.where(lane == LANES - 1, left[(ct + 1) % nct], left[ct])
        centre, w_w, w_e, w_s, w_n = weights[ct]
        out.append(
            (centre * mid[ct] + w_w * west[ct]) + (w_e * east[ct] + (w_s * south + w_n * north))
        )
    return out


class Rows:
    def __init__(self, held, coef):
        self.nct, _, blocks = held.shape[-5:-2]
        self.room = blocks * SUB
        self.flat = held.reshape(held.size // LANES, LANES)
        self.coef = coef.reshape(coef.size // LANES, LANES)

    def at(self, group, ct, row):
        start = (group * self.nct + ct) * SUB * self.room + PAD + row
        return pl.ds(start, SUB, stride=self.room)

    def load(self, group, row):
        return [self.flat[self.at(group, ct, row), :] for ct in range(self.nct)]

    def weights(self, row):
        return [
            [
                self.coef[pl.ds((k * self.nct + ct) * self.room + PAD + row, SUB, stride=0), :]
                for k in range(5)
            ]
            for ct in range(self.nct)
        ]


def group_steps(group, held, between, coef, put, edges):
    groups, nct, _, blocks = held.shape[:4]
    room = blocks * SUB
    source = held.reshape(groups, nct, SUB, room, LANES)
    middle = between.reshape(nct, SUB, room, LANES)

    def block_step(block, load, store):
        at = PAD + block * SUB
        weights = [[coef[k, ct, pl.ds(at, SUB), :] for k in range(5)] for ct in range(nct)]
        for m in range(SUB):
            mid, west, east = [
                [load(ct, m, pl.ds(at + off, SUB)) for ct in range(nct)] for off in (0, -1, 1)
            ]
            for ct, value in enumerate(stencil(mid, west, east, weights)):
                store(block, ct, m, value)

    def keep(block, ct, m, value):
        middle[ct, m, pl.ds(PAD + block * SUB, SUB), :] = value

    for block in range(blocks - 2):
        block_step(block, lambda ct, m, rows: source[group, ct, m, rows, :], keep)
    if edges:
        field, inner = Rows(held, coef), Rows(between, coef)
        for row in (-1, (blocks - 2) * SUB):
            around = [field.load(group, row + off) for off in (0, -1, 1)]
            for ct, value in enumerate(stencil(*around, field.weights(row))):
                inner.flat[inner.at(0, ct, row), :] = value
    for block in range(blocks - 2):
        block_step(block, lambda ct, m, rows: middle[ct, m, rows, :], put)


def held_shape(members, nct, r8):
    return (members // SUB, nct, SUB, r8 + 2, SUB, LANES)


def cost(cells):
    return pl.CostEstimate(flops=40 * cells, bytes_accessed=8 * cells, transcendentals=0)


SMEM = pl.BlockSpec(memory_space=pltpu.SMEM)
VMEM = pl.BlockSpec(memory_space=pltpu.VMEM)


def inner_kernel(state, flow, nu, full, held0, held1, between, coef, sems):
    groups, nct, _, blocks = held0.shape[:4]
    members = groups * SUB
    r8 = blocks - 2

    def copies(field, held, group):
        return [
            pltpu.make_async_copy(
                state.at[pl.ds(group * SUB, SUB), field, :, ct],
                held.at[group, ct, :, pl.ds(1, r8)],
                sems.at[field, group, ct],
            )
            for ct in range(nct)
        ]

    for group in range(groups):
        for one in copies(0, held0, group):
            one.start()
    fill_coefs(coef, 0, flow, nu, [(0, r8)])
    flat = full.reshape(full.size // LANES, LANES)

    def run(group, carry):
        for one in copies(0, held0, group):
            one.wait()
        for one in copies(1, held1, group):
            one.start()

        def put(block, ct, m, value):
            start = (block * SUB * nct + ct) * members + group * SUB + m
            flat[pl.ds(start, SUB, stride=nct * members), :] = value

        group_steps(group, held0, between, coef, put, False)
        return carry

    lax.fori_loop(0, groups, run, 0)
    for group in range(groups):
        for one in copies(1, held1, group):
            one.wait()


def forecast_inner(state6, flow5, nu5):
    members, _, r8, nct = state6.shape[:4]
    held = held_shape(members, nct, r8)
    return pl.pallas_call(
        inner_kernel,
        out_shape=[
            jax.ShapeDtypeStruct((r8 * SUB, nct, members, LANES), F32),
            jax.ShapeDtypeStruct(held, F32),
            jax.ShapeDtypeStruct(held, F32),
        ],
        in_specs=[pl.BlockSpec(memory_space=pl.ANY)] + [VMEM] * 2,
        out_specs=[VMEM] * 3,
        scratch_shapes=[
            pltpu.VMEM(held[1:], F32),
            pltpu.VMEM((5, nct, (r8 + 2) * SUB, LANES), F32),
            pltpu.SemaphoreType.DMA((2, held[0], nct)),
        ],
        compiler_params=params(34),
        cost_estimate=cost(members * r8 * SUB * nct * LANES),
        name="forecast_inner",
    )(state6, flow5, nu5)


def edge_kernel(
    ids, cells, owner, order, flow, nu, before, after, full_in, held0_in, held1_in,
    full, held0, held1, keep, away, coef
):
    groups, nct, _, blocks = held0.shape[:4]
    members = groups * SUB
    r8 = blocks - 2
    rows = r8 * SUB
    slab, member = ids[0], ids[1]

    for field, held in ((0, held0), (1, held1)):
        view = Rows(held, coef)
        for ct in range(nct):
            for group in range(groups):
                for k in range(2):
                    part = pl.ds((2 * field + k) * members + group * SUB, SUB)
                    view.flat[view.at(group, ct, k - 2), :] = before[ct, part, :]
                    view.flat[view.at(group, ct, rows + k), :] = after[ct, part, :]

    fill_coefs(coef, 0, flow, nu, [(0, 1), (r8 - 1, 1)], before, after)
    view = Rows(held0, coef)
    for first in (0, rows - 2):
        for group in range(groups):
            old = {r: view.load(group, r) for r in range(first - 2, first + 4)}
            one = {
                r: stencil(old[r], old[r - 1], old[r + 1], view.weights(r))
                for r in range(first - 1, first + 3)
            }
            for r in range(first, first + 2):
                new = stencil(one[r], one[r - 1], one[r + 1], view.weights(r))
                for ct, value in enumerate(new):
                    full[r, ct, pl.ds(group * SUB, SUB), :] = value

    nobs = cells.shape[1]
    tiles = full.reshape(rows * nct, members, LANES)
    lane = lax.broadcasted_iota(jnp.int32, (members, LANES), 1)
    for position in range(order.shape[0]):
        batch = order[position]
        mine = owner[batch] == slab
        kept = lax.rem(position, 2) == member

        def pick(tile, carry, batch=batch, mine=mine, kept=kept, position=position):
            def some(group, acc):
                for u in range(GATHER):
                    o = group * GATHER + u
                    cell = cells[batch, tile * LANES + o]
                    tile_at = lax.shift_right_logical(cell, LANES.bit_length() - 1)
                    moved = pltpu.roll(tiles[tile_at], (o - cell) & (LANES - 1), 1)
                    acc = jnp.where(lane == o, moved, acc)
                return acc

            acc = lax.fori_loop(
                0, jnp.where(mine, LANES // GATHER, 0), some, jnp.zeros((members, LANES), F32)
            )

            @pl.when(kept)
            def _():
                keep[position // 2, tile] = acc

            @pl.when(jnp.logical_not(kept))
            def _():
                away[position // 2, tile] = acc

            return carry

        lax.fori_loop(0, nobs // LANES, pick, 0)


def forecast_edges(ids, cells, owner, order, flow5, nu5, before, after, full, held0, held1):
    members = full.shape[2]
    nct, _, blocks = held0.shape[1:4]
    nb, nobs = cells.shape
    picks = jax.ShapeDtypeStruct((nb // 2, nobs // LANES, members, LANES), F32)
    same = [jax.ShapeDtypeStruct(x.shape, F32) for x in (full, held0, held1)]
    return pl.pallas_call(
        edge_kernel,
        out_shape=[*same, picks, picks],
        in_specs=[SMEM] * 4 + [VMEM] * 7,
        out_specs=[VMEM] * 5,
        input_output_aliases={8: 0, 9: 1, 10: 2},
        scratch_shapes=[pltpu.VMEM((5, nct, blocks * SUB, LANES), F32)],
        compiler_params=params(6),
        cost_estimate=cost(members * SUB * nct * LANES),
        name="forecast_edges",
    )(ids, cells, owner, order, flow5, nu5, before, after, full, held0, held1)


def piece_kernel(group, flow, nu, before, after, held, *rest):
    full, between, coef = rest[-3:]
    rows, nct, members = full.shape[:3]
    flat = full.reshape(full.size // LANES, LANES)
    fill_coefs(coef, 1, flow, nu, [(0, rows // SUB)], before, after)

    def put(block, ct, m, value):
        start = (block * SUB * nct + ct) * members + group * SUB + m
        flat[pl.ds(start, SUB, stride=nct * members), :] = value

    group_steps(group, held, between, coef, put, True)


def forecast_piece(group, flow5, nu5, before, after, held, done):
    groups, nct, _, blocks = held.shape[:4]
    rows = (blocks - 2) * SUB
    return pl.pallas_call(
        functools.partial(piece_kernel, group),
        out_shape=jax.ShapeDtypeStruct((rows, nct, groups * SUB, LANES), F32),
        in_specs=[VMEM] * (5 + len(done)),
        out_specs=VMEM,
        input_output_aliases={5: 0} if done else {},
        scratch_shapes=[
            pltpu.VMEM(held.shape[1:], F32),
            pltpu.VMEM((5, nct, blocks * SUB, LANES), F32),
        ],
        compiler_params=params(6),
        cost_estimate=cost(SUB * rows * nct * LANES),
        name=f"forecast_members_{group}",
    )(flow5, nu5, before, after, held, *done)


def gram_kernel(ids, owner, order, keep, other, observed, variance, gh):
    slab, member = ids[0], ids[1]
    count, tiles, members = keep.shape[:3]
    for k in range(count):
        batch = order[2 * k + member]
        mine = owner[batch] == slab
        out = gh.at[k]

        @pl.when(jnp.logical_not(mine))
        def _():
            out[...] = jnp.zeros(out.shape, F32)

        @pl.when(mine)
        def _():
            pair = jnp.zeros(out.shape, F32)
            for t in range(tiles):
                a, b = keep[k, t], other[k, t]
                prior = jnp.concatenate(
                    [jnp.where(member == 0, a, b), jnp.where(member == 0, b, a)], axis=0
                )
                mean = jnp.sum(prior, axis=0, keepdims=True) / (2 * members)
                anomaly = prior - mean
                scaled = anomaly / variance[batch, :, pl.ds(t * LANES, LANES)]
                misfit = observed[batch, :, pl.ds(t * LANES, LANES)] - mean
                pair += lax.dot_general(
                    scaled,
                    jnp.concatenate([anomaly, misfit], axis=0),
                    (((1,), (1,)), ((), ())),
                    precision=HIGH,
                    preferred_element_type=F32,
                )
            h = lax.dot_general(
                pair[:, 2 * members :], rotation(2 * members), (((1,), (0,)), ((), ())),
                precision=HIGH, preferred_element_type=F32,
            )
            out[...] = jnp.concatenate([pair[:, : 2 * members], h], axis=1)


def gram(ids, owner, order, keep, other, observed, variance):
    count, _, members, _ = keep.shape
    total = 2 * members
    smem = pl.BlockSpec(memory_space=pltpu.SMEM)
    vmem = pl.BlockSpec(memory_space=pltpu.VMEM)
    return pl.pallas_call(
        gram_kernel,
        out_shape=jax.ShapeDtypeStruct((count, total, 2 * total), F32),
        in_specs=[smem] * 3 + [vmem] * 4,
        out_specs=vmem,
        compiler_params=params(12),
        name="gram",
    )(ids, owner, order, keep, other, observed, variance[:, None, :])


def rotation(size):
    step = size**-0.5
    row = lax.broadcasted_iota(jnp.int32, (size, size), 0)
    col = lax.broadcasted_iota(jnp.int32, (size, size), 1)
    v_row = (row == size - 1).astype(F32) - step
    v_col = (col == size - 1).astype(F32) - step
    return (row == col).astype(F32) - v_row * v_col / (1.0 - step)


def split3(x):
    high = x.astype(BF16)
    rest = x - high.astype(F32)
    mid = rest.astype(BF16)
    return high, mid, (rest - mid.astype(F32)).astype(BF16)


def dot32(x, y, lhs, rhs):
    parts = split3(x)
    m = x.shape[1 - lhs]
    out = None
    for k, right in enumerate(split3(y)):
        left = jnp.concatenate(parts[: 3 - k], axis=1 - lhs)
        each = lax.dot_general(
            left, right, (((lhs,), (rhs,)), ((), ())), preferred_element_type=F32
        )
        for j in reversed(range(3 - k)):
            piece = each[j * m : (j + 1) * m]
            out = piece if out is None else out + piece
    return out


def total(terms):
    while len(terms) > 1:
        terms = [x + y for x, y in zip(terms[::2], terms[1::2])]
    return terms[0]


def eliminate(a, b, rows_a, rows_b):
    groups = a.shape[0] // SUB
    wide = (SUB, LANES)
    sub = lax.broadcasted_iota(jnp.int32, wide, 0)
    a = [a[g * SUB : (g + 1) * SUB] for g in range(groups)]
    b = [b[g * SUB : (g + 1) * SUB] for g in range(groups)]
    plain, scaled = [], []

    def column(x, k):
        return jnp.broadcast_to(x[:, k : k + 1], wide)

    def row(x, k):
        return jnp.broadcast_to(x[k : k + 1, :], wide)

    for p in range(groups):
        cols = {
            g: [column(a[g], p * SUB + k) for k in range(SUB)] for g in range(p, groups)
        }
        c = [(x, x) for x in cols[p]]
        pa, pb = (a[p], a[p]), (b[p], b[p])
        plain.append(b[p])
        after = p + 1 if p + 1 < groups else None
        e = cols[after] if after else []
        for k in range(0, SUB, 2):
            (fk, ck), (fl, cl) = c[k], c[k + 1]
            kk, kl, lk, ll = row(fk, k), row(fl, k), row(fk, k + 1), row(fl, k + 1)
            scale = pl.reciprocal(kk * ll - kl * lk, approx=True)

            def pivot_rows(x, k=k, kk=kk, kl=kl, lk=lk, ll=ll):
                u, w = row(x[0], k), row(x[0], k + 1)
                return ll * u - kl * w, kk * w - lk * u

            def inside(x, n0, n1, k=k, ck=ck, cl=cl, scale=scale):
                rest = x[1] - scale * (ck * n0 + cl * n1)
                done = jnp.where(sub == k, scale * n0, jnp.where(sub == k + 1, scale * n1, rest))
                return rest, done

            def outside(x, n0, n1, k=k, scale=scale):
                return x - scale * (e[k] * n0 + e[k + 1] * n1)

            for j in range(k + 2, SUB):
                n = pivot_rows(c[j])
                c[j] = inside(c[j], *n)
                if after:
                    e[j] = outside(e[j], *n)
            if after:
                n = pivot_rows(pa)
                pa = inside(pa, *n)
                a[after] = outside(a[after], *n)
            n = pivot_rows(pb)
            pb = inside(pb, *n)
            if after:
                b[after] = outside(b[after], *n)
        pa, pb = pa[1], pb[1]
        scaled.append(pb)
        if p + 2 < groups:
            here = p % 2
            rows_a[here] = pa
            rows_b[here] = pb
            ra = [rows_a[here, pl.ds(k, SUB, stride=0), :] for k in range(SUB)]
            rb = [rows_b[here, pl.ds(k, SUB, stride=0), :] for k in range(SUB)]
            for g in range(p + 2, groups):
                a[g] = a[g] - total([cols[g][k] * ra[k] for k in range(SUB)])
                b[g] = b[g] - total([cols[g][k] * rb[k] for k in range(SUB)])
    return jnp.concatenate(plain, axis=0), jnp.concatenate(scaled, axis=0)


def chain_kernel(ids, mine, other, out, rows_a, rows_b):
    member = ids[1]
    count, size, width = mine.shape
    row = lax.broadcasted_iota(jnp.int32, (size, width), 0)
    lane = lax.broadcasted_iota(jnp.int32, (size, width), 1)
    diagonal = jnp.where(row == lane, size - 1.0, 0.0)

    def step(position, vt):
        k = lax.div(position, 2)
        gh = jnp.where(lax.rem(position, 2) == member, mine[k], other[k])
        zt = jnp.where(row == size - 1, 0.0, vt)
        s = dot32(zt[:, :size], gh, 1, 0)
        v = vt[:, :size]
        t = dot32(s[:, :size], jnp.concatenate([v, v], axis=0), 1, 1)
        a = jnp.where(lane == size - 1, 0.0, t) + diagonal
        b = jnp.where(lane < size, zt, s - t)
        plain, scaled = eliminate(a, b, rows_a, rows_b)
        return vt + dot32(plain, scaled, 0, 0)[size:]

    unit = rotation(size)
    start = jnp.concatenate([unit, jnp.zeros_like(unit)], axis=1)
    vt = lax.fori_loop(0, 2 * count, step, start)
    w = dot32(unit, vt[:, :size], 1, 0)
    half = size // 2
    first, second = w[:, :half], w[:, half:]
    w = jnp.concatenate(
        [jnp.where(member == 0, first, second), jnp.where(member == 0, second, first)], axis=1
    )
    high = w.astype(BF16).astype(F32)
    low = w - high
    out[...] = jnp.concatenate(
        [jnp.concatenate([high, high], axis=1), jnp.concatenate([low, jnp.zeros_like(low)], axis=1)],
        axis=0,
    )


def chain(ids, mine, other):
    size = mine.shape[1]
    rows = pltpu.VMEM((2, SUB, LANES), F32)
    return pl.pallas_call(
        chain_kernel,
        out_shape=jax.ShapeDtypeStruct((2 * size, 2 * size), F32),
        in_specs=[SMEM] + [VMEM] * 2,
        out_specs=VMEM,
        scratch_shapes=[rows, rows],
        compiler_params=params(12),
        name="chain",
    )(ids, mine, other)


def apply_kernel(ids, w_ref, own0, other0, own1, other1, out, held, sems):
    size = w_ref.shape[0] // 2
    rows, nct = own0.shape[:2]
    half = nct // 2
    first_tile = ids[1] * half
    weights = w_ref[...].astype(BF16)
    flat = held.reshape(held.size // LANES, LANES)

    for field, sources in enumerate(((own0, other0), (own1, other1))):

        def copy(block, slot, field=field):
            return pltpu.make_async_copy(held.at[slot], out.at[:, field, block], sems.at[slot])

        def step(block, carry, field=field, sources=sources, copy=copy):
            slot = lax.rem(block, 2)

            @pl.when((block >= 2) if field == 0 else (block >= 0))
            def _():
                copy(block, slot).wait()

            base = slot * size * half * SUB
            for r in range(SUB):
                parts = [
                    jnp.concatenate(
                        [src[block * SUB + r, first_tile + ct] for ct in range(half)], axis=1
                    )
                    for src in sources
                ]
                high = [x.astype(BF16) for x in parts]
                low = [(x - y.astype(F32)).astype(BF16) for x, y in zip(parts, high)]
                stacked = jnp.concatenate([*high, *low], axis=0)
                result = jnp.dot(weights, stacked, preferred_element_type=F32)
                result = result[:size] + result[size:]
                for ct in range(half):
                    flat[pl.ds(base + ct * SUB + r, size, stride=half * SUB), :] = result[
                        :, ct * LANES : (ct + 1) * LANES
                    ]
            copy(block, slot).start()
            return carry

        lax.fori_loop(0, rows // SUB, step, 0)
    for slot in range(2):
        copy(0, slot).wait()


def apply(ids, weights, own0, other0, own1, other1):
    rows, nct, members, _ = own0.shape
    size = 2 * members
    half = nct // 2
    r8 = rows // SUB
    return pl.pallas_call(
        apply_kernel,
        out_shape=jax.ShapeDtypeStruct((size, 2, r8, half, SUB, LANES), F32),
        in_specs=[SMEM] + [VMEM] * 5,
        out_specs=pl.BlockSpec(memory_space=pl.ANY),
        scratch_shapes=[
            pltpu.VMEM((2, size, half, SUB, LANES), F32),
            pltpu.SemaphoreType.DMA((2,)),
        ],
        compiler_params=params(12),
        name="apply",
    )(ids, weights, own0, other0, own1, other1)


def body(state, courant, diffusion, obs_cells, obs_owner, batch_order, obs_values, obs_error):
    slab = lax.axis_index("space")
    member = lax.axis_index("member")
    space = lax.axis_size("space")
    ids = jnp.stack([slab, member]).astype(jnp.int32)
    up = [(i, i + 1) for i in range(space - 1)]
    down = [(i + 1, i) for i in range(space - 1)]
    swap = [(0, 1), (1, 0)]

    state6, flow5, nu5 = tiled(state), tiled(courant), tiled(diffusion)
    up_edge, down_edge = pack_edges(state6, flow5, nu5)
    before = lax.ppermute(up_edge, "space", up)
    after = lax.ppermute(down_edge, "space", down)
    full0, held0, held1 = forecast_inner(state6, flow5, nu5)
    full0, _, held1, keep, away = forecast_edges(
        ids, obs_cells, obs_owner, batch_order, flow5, nu5, before, after, full0, held0, held1
    )
    other = lax.ppermute(away, "member", swap)
    gh = gram(ids, obs_owner, batch_order, keep, other, obs_values, obs_error)

    groups = list(range(held1.shape[0]))
    field1 = ()
    bit = 1
    while bit < space:
        received = lax.ppermute(gh, "space", [(i, i ^ bit) for i in range(space)])
        if groups:
            held1, gh = lax.optimization_barrier((held1, gh))
            field1 = forecast_piece(groups.pop(0), flow5, nu5, before, after, held1, field1)
            received, field1 = lax.optimization_barrier((received, (field1,)))
        gh = gh + received
        bit *= 2
    for group in groups:
        field1 = (forecast_piece(group, flow5, nu5, before, after, held1, field1),)
    (full1,) = field1
    theirs = lax.ppermute(gh, "member", swap)
    full0, full1, gh, theirs = lax.optimization_barrier((full0, full1, gh, theirs))
    other0 = lax.ppermute(full0, "member", swap)
    other1 = lax.ppermute(full1, "member", swap)
    weights = chain(ids, gh, theirs)
    return untiled(apply(ids, weights, full0, other0, full1, other1))


def solution(mesh):
    placed = (
        P("member", None, "space", None),
        P(None, "space", None),
        P(None, "space", None),
        P(),
        P(),
        P(),
        P(),
        P(),
    )
    return jax.shard_map(
        body,
        mesh=mesh,
        in_specs=placed,
        out_specs=P(None, None, "space", "member"),
        check_vma=False,
    )
```

```python
import functools

import jax
import jax.numpy as jnp
from jax import lax
from jax.experimental import pallas as pl
from jax.experimental.pallas import tpu as pltpu
from jax.sharding import PartitionSpec as P

HIGH = lax.Precision.HIGHEST
F32 = jnp.float32
BF16 = jnp.bfloat16
LANES = 128
SUB = 8
AHEAD = 2
PACK = 8


def params(mib):
    return pltpu.CompilerParams(vmem_limit_bytes=mib * 1024 * 1024)


def unrolled(count, most):
    return max(d for d in range(1, most + 1) if count % d == 0)


def rows_loop(count, most, fn):
    step = unrolled(count, most)

    def run(i, carry):
        for u in range(step):
            fn(i * step + u)
        return carry

    lax.fori_loop(0, count // step, run, 0)


def tiled(array):
    *lead, rows, cols = array.shape
    n = len(lead)
    split = array.reshape(*lead, rows // SUB, SUB, cols // LANES, LANES)
    return jnp.transpose(split, (*range(n), n, n + 2, n + 1, n + 3))


def untiled(array):
    *lead, r8, ct, sub, lanes = array.shape
    n = len(lead)
    back = jnp.transpose(array, (*range(n), n, n + 2, n + 1, n + 3))
    return back.reshape(*lead, r8 * sub, ct * lanes)


def pack_kernel(state, flow, nu, up, down, edge_flow, edge_nu, sems):
    members, fields, r8, nct = state.shape[:4]
    sides = ((up, r8 - 1, (SUB - 2, SUB - 1)), (down, 0, (0, 1)))
    copies = []

    def copy(src, dst):
        copies.append(pltpu.make_async_copy(src, dst, sems.at[len(copies)]))

    for side, (msg, block, rows) in enumerate(sides):
        copy(flow.at[:, block], edge_flow.at[side])
        copy(nu.at[:, block], edge_nu.at[side])
    for msg, block, rows in sides:
        for field in range(fields):
            for ct in range(nct):
                for at, row in enumerate(rows):
                    copy(
                        state.at[:, field, block, ct, row, :],
                        msg.at[ct, pl.ds((field * 2 + at) * members, members), :],
                    )
    for one in copies:
        one.start()
    for one in copies[:4]:
        one.wait()
    for side, (msg, block, rows) in enumerate(sides):
        edge = (SUB - 1, 0)[side]
        for ct in range(nct):
            numbers = [edge_flow[side, k, ct, edge : edge + 1, :] for k in range(2)]
            numbers += [edge_nu[side, k, ct, edge : edge + 1, :] for k in range(fields)]
            numbers.append(jnp.zeros((PACK - 2 - fields, LANES), F32))
            msg[ct, pl.ds(2 * fields * members, PACK), :] = jnp.concatenate(numbers, axis=0)
    for one in copies[4:]:
        one.wait()


def pack_edges(state6, flow5, nu5):
    members, fields, r8, nct = state6.shape[:4]
    msg = jax.ShapeDtypeStruct((nct, 2 * fields * members + PACK, LANES), F32)
    edge = pltpu.VMEM((2, 2, nct, SUB, LANES), F32)
    return pl.pallas_call(
        pack_kernel,
        out_shape=[msg] * 2,
        in_specs=[pl.BlockSpec(memory_space=pl.ANY)] * 3,
        out_specs=[pl.BlockSpec(memory_space=pltpu.VMEM)] * 2,
        scratch_shapes=[edge, edge, pltpu.SemaphoreType.DMA((4 + 4 * fields * nct,))],
        compiler_params=params(56),
        name="pack_edges",
    )(state6, flow5, nu5)


PAD = SUB


def stencil_coefs(flow_x, flow_y, nu, col, width):
    east = nu - jnp.minimum(flow_x, 0.0)
    west = nu + jnp.maximum(flow_x, 0.0)
    north = nu - jnp.minimum(flow_y, 0.0)
    south = nu + jnp.maximum(flow_y, 0.0)
    centre = 1.0 - (east + west + north + south)
    south = jnp.where(col == 0, 0.0, south)
    north = jnp.where(col == width - 1, 0.0, north)
    return centre, west, east, south, north


def fill_coefs(coef, field, flow, nu, blocks, before=None, after=None):
    _, r8, nct = flow.shape[:3]
    width = nct * LANES
    for ct in range(nct):
        for first, count in blocks:
            shape = (count * SUB, LANES)
            col = lax.broadcasted_iota(jnp.int32, shape, 1) + ct * LANES
            part = pl.ds(first, count)
            numbers = (flow[0, part, ct], flow[1, part, ct], nu[field, part, ct])
            numbers = [x.reshape(shape) for x in numbers]
            for k, value in enumerate(stencil_coefs(*numbers, col, width)):
                coef[k, ct, pl.ds(PAD + first * SUB, count * SUB), :] = value
        for msg, row in ((before, PAD - 1), (after, PAD + r8 * SUB)):
            if msg is not None:
                col = lax.broadcasted_iota(jnp.int32, (1, LANES), 1) + ct * LANES
                base = msg.shape[1] - PACK
                numbers = [msg[ct, pl.ds(base + k, 1), :] for k in (0, 1, 2 + field)]
                for k, value in enumerate(stencil_coefs(*numbers, col, width)):
                    coef[k, ct, pl.ds(row, 1), :] = value


def stencil(mid, west, east, weights):
    nct = len(mid)
    lane = lax.broadcasted_iota(jnp.int32, (SUB, LANES), 1)
    right = [pltpu.roll(x, 1, 1) for x in mid]
    left = [pltpu.roll(x, LANES - 1, 1) for x in mid]
    out = []
    for ct in range(nct):
        south = jnp.where(lane == 0, right[(ct - 1) % nct], right[ct])
        north = jnp.where(lane == LANES - 1, left[(ct + 1) % nct], left[ct])
        centre, w_w, w_e, w_s, w_n = weights[ct]
        out.append(
            (centre * mid[ct] + w_w * west[ct]) + (w_e * east[ct] + (w_s * south + w_n * north))
        )
    return out


class Rows:
    def __init__(self, held, coef):
        self.nct, _, blocks = held.shape[-5:-2]
        self.room = blocks * SUB
        self.flat = held.reshape(held.size // LANES, LANES)
        self.coef = coef.reshape(coef.size // LANES, LANES)

    def at(self, group, ct, row):
        start = (group * self.nct + ct) * SUB * self.room + PAD + row
        return pl.ds(start, SUB, stride=self.room)

    def load(self, group, row):
        return [self.flat[self.at(group, ct, row), :] for ct in range(self.nct)]

    def weights(self, row):
        return [
            [
                self.coef[pl.ds((k * self.nct + ct) * self.room + PAD + row, SUB, stride=0), :]
                for k in range(5)
            ]
            for ct in range(self.nct)
        ]


def group_steps(group, held, between, coef, put, edges):
    groups, nct, _, blocks = held.shape[:4]
    room = blocks * SUB
    source = held.reshape(groups, nct, SUB, room, LANES)
    middle = between.reshape(nct, SUB, room, LANES)

    def block_step(block, load, store):
        at = PAD + block * SUB
        weights = [[coef[k, ct, pl.ds(at, SUB), :] for k in range(5)] for ct in range(nct)]
        for m in range(SUB):
            mid, west, east = [
                [load(ct, m, pl.ds(at + off, SUB)) for ct in range(nct)] for off in (0, -1, 1)
            ]
            for ct, value in enumerate(stencil(mid, west, east, weights)):
                store(block, ct, m, value)

    def keep(block, ct, m, value):
        middle[ct, m, pl.ds(PAD + block * SUB, SUB), :] = value

    for block in range(blocks - 2):
        block_step(block, lambda ct, m, rows: source[group, ct, m, rows, :], keep)
    if edges:
        field, inner = Rows(held, coef), Rows(between, coef)
        for row in (-1, (blocks - 2) * SUB):
            around = [field.load(group, row + off) for off in (0, -1, 1)]
            for ct, value in enumerate(stencil(*around, field.weights(row))):
                inner.flat[inner.at(0, ct, row), :] = value
    for block in range(blocks - 2):
        block_step(block, lambda ct, m, rows: middle[ct, m, rows, :], put)


def held_shape(members, nct, r8):
    return (members // SUB, nct, SUB, r8 + 2, SUB, LANES)


def cost(cells):
    return pl.CostEstimate(flops=40 * cells, bytes_accessed=8 * cells, transcendentals=0)


SMEM = pl.BlockSpec(memory_space=pltpu.SMEM)
VMEM = pl.BlockSpec(memory_space=pltpu.VMEM)


def inner_kernel(state, flow, nu, full, turned, held0, held1, between, coef, sems):
    groups, nct, _, blocks = held0.shape[:4]
    members = groups * SUB
    r8 = blocks - 2

    def copies(field, held, group):
        return [
            pltpu.make_async_copy(
                state.at[pl.ds(group * SUB, SUB), field, :, ct],
                held.at[group, ct, :, pl.ds(1, r8)],
                sems.at[field, group, ct],
            )
            for ct in range(nct)
        ]

    for group in range(groups):
        for one in copies(0, held0, group):
            one.start()
    fill_coefs(coef, 0, flow, nu, [(0, r8)])
    flat, turned_flat = (x.reshape(x.size // LANES, LANES) for x in (full, turned))

    def run(group, carry):
        for one in copies(0, held0, group):
            one.wait()
        for one in copies(1, held1, group):
            one.start()

        def put(block, ct, m, value):
            start = (block * SUB * nct + ct) * members + group * SUB + m
            rows = pl.ds(start, SUB, stride=nct * members)
            flat[rows, :] = value
            turned_flat[rows, :] = pltpu.roll(value, group * (LANES // groups), 1)

        group_steps(group, held0, between, coef, put, False)
        return carry

    lax.fori_loop(0, groups, run, 0)
    for group in range(groups):
        for one in copies(1, held1, group):
            one.wait()


def forecast_inner(state6, flow5, nu5):
    members, _, r8, nct = state6.shape[:4]
    held = held_shape(members, nct, r8)
    full = jax.ShapeDtypeStruct((r8 * SUB, nct, members, LANES), F32)
    return pl.pallas_call(
        inner_kernel,
        out_shape=[
            full,
            full,
            jax.ShapeDtypeStruct(held, F32),
            jax.ShapeDtypeStruct(held, F32),
        ],
        in_specs=[pl.BlockSpec(memory_space=pl.ANY)] + [VMEM] * 2,
        out_specs=[VMEM] * 4,
        scratch_shapes=[
            pltpu.VMEM(held[1:], F32),
            pltpu.VMEM((5, nct, (r8 + 2) * SUB, LANES), F32),
            pltpu.SemaphoreType.DMA((2, held[0], nct)),
        ],
        compiler_params=params(34),
        cost_estimate=cost(members * r8 * SUB * nct * LANES),
        name="forecast_inner",
    )(state6, flow5, nu5)


def edge_kernel(
    ids, cells, owner, order, flow, nu, before, after, full_in, turned_in, held0_in, held1_in,
    full, turned, held0, held1, keep, away, coef
):
    groups, nct, _, blocks = held0.shape[:4]
    members = groups * SUB
    r8 = blocks - 2
    rows = r8 * SUB
    slab, member = ids[0], ids[1]

    for field, held in ((0, held0), (1, held1)):
        view = Rows(held, coef)
        for ct in range(nct):
            for group in range(groups):
                for k in range(2):
                    part = pl.ds((2 * field + k) * members + group * SUB, SUB)
                    view.flat[view.at(group, ct, k - 2), :] = before[ct, part, :]
                    view.flat[view.at(group, ct, rows + k), :] = after[ct, part, :]

    fill_coefs(coef, 0, flow, nu, [(0, 1), (r8 - 1, 1)], before, after)
    view = Rows(held0, coef)
    for first in (0, rows - 2):
        for group in range(groups):
            old = {r: view.load(group, r) for r in range(first - 2, first + 4)}
            one = {
                r: stencil(old[r], old[r - 1], old[r + 1], view.weights(r))
                for r in range(first - 1, first + 3)
            }
            for r in range(first, first + 2):
                new = stencil(one[r], one[r - 1], one[r + 1], view.weights(r))
                for ct, value in enumerate(new):
                    part = pl.ds(group * SUB, SUB)
                    full[r, ct, part, :] = value
                    turned[r, ct, part, :] = pltpu.roll(value, group * (LANES // groups), 1)

    share = LANES // groups
    tiles = turned.reshape(rows * nct, members, LANES)
    lane = lax.broadcasted_iota(jnp.int32, (SUB, LANES), 1)

    def merged(choices, which):
        out = choices[0]
        for k, x in enumerate(choices[1:]):
            out = jnp.where(which >= (k + 1) * share, x, out)
        return out

    def gather_tile(batch, tile):
        packed = []
        for first in range(0, LANES, share):
            acc = jnp.zeros((SUB, LANES), F32)
            for u in range(share):
                cell = cells[batch, tile * LANES + first + u]
                source = tiles[lax.shift_right_logical(cell, LANES.bit_length() - 1)]
                which = (lane - cell) & (LANES - 1)
                value = merged([source[g * SUB : (g + 1) * SUB] for g in range(groups)], which)
                moved = pltpu.roll(value, (u - cell) & (LANES - 1), 1)
                acc = jnp.where((lane & (share - 1)) == u, moved, acc)
            packed.append(acc)
        parts = [
            merged(
                [pltpu.roll(x, (k - g) * share % LANES, 1) if k != g else x
                 for k, x in enumerate(packed)],
                lane,
            )
            for g in range(groups)
        ]
        return jnp.concatenate(parts, axis=0)

    def gather_batch(position, carry):
        batch = order[position]
        mine = owner[batch] == slab
        kept = lax.rem(position, 2) == member
        at = lax.div(position, 2)

        for out, wanted in ((keep, kept), (away, jnp.logical_not(kept))):

            @pl.when(jnp.logical_and(wanted, jnp.logical_not(mine)))
            def _(out=out):
                out[at] = jnp.zeros(out.shape[1:], F32)

        @pl.when(mine)
        def _():
            def one(tile, carry):
                values = gather_tile(batch, tile)

                @pl.when(kept)
                def _():
                    keep[at, tile] = values

                @pl.when(jnp.logical_not(kept))
                def _():
                    away[at, tile] = values

                return carry

            lax.fori_loop(0, cells.shape[1] // LANES, one, 0)

        return carry

    lax.fori_loop(0, order.shape[0], gather_batch, 0)


def forecast_edges(
    ids, cells, owner, order, flow5, nu5, before, after, full, turned, held0, held1
):
    members = full.shape[2]
    nct, _, blocks = held0.shape[1:4]
    nb, nobs = cells.shape
    picks = jax.ShapeDtypeStruct((nb // 2, nobs // LANES, members, LANES), F32)
    same = [jax.ShapeDtypeStruct(x.shape, F32) for x in (full, turned, held0, held1)]
    return pl.pallas_call(
        edge_kernel,
        out_shape=[*same, picks, picks],
        in_specs=[SMEM] * 4 + [VMEM] * 8,
        out_specs=[VMEM] * 6,
        input_output_aliases={8: 0, 9: 1, 10: 2, 11: 3},
        scratch_shapes=[pltpu.VMEM((5, nct, blocks * SUB, LANES), F32)],
        compiler_params=params(6),
        cost_estimate=cost(members * SUB * nct * LANES),
        name="forecast_edges",
    )(ids, cells, owner, order, flow5, nu5, before, after, full, turned, held0, held1)


def piece_kernel(group, flow, nu, before, after, held, *rest):
    full, between, coef = rest[-3:]
    rows, nct, members = full.shape[:3]
    flat = full.reshape(full.size // LANES, LANES)
    fill_coefs(coef, 1, flow, nu, [(0, rows // SUB)], before, after)

    def put(block, ct, m, value):
        start = (block * SUB * nct + ct) * members + group * SUB + m
        flat[pl.ds(start, SUB, stride=nct * members), :] = value

    group_steps(group, held, between, coef, put, True)


def forecast_piece(group, flow5, nu5, before, after, held, done):
    groups, nct, _, blocks = held.shape[:4]
    rows = (blocks - 2) * SUB
    return pl.pallas_call(
        functools.partial(piece_kernel, group),
        out_shape=jax.ShapeDtypeStruct((rows, nct, groups * SUB, LANES), F32),
        in_specs=[VMEM] * (5 + len(done)),
        out_specs=VMEM,
        input_output_aliases={5: 0} if done else {},
        scratch_shapes=[
            pltpu.VMEM(held.shape[1:], F32),
            pltpu.VMEM((5, nct, blocks * SUB, LANES), F32),
        ],
        compiler_params=params(6),
        cost_estimate=cost(SUB * rows * nct * LANES),
        name=f"forecast_members_{group}",
    )(flow5, nu5, before, after, held, *done)


def gram_kernel(ids, owner, order, keep, other, observed, variance, gh):
    slab, member = ids[0], ids[1]
    count, tiles, members = keep.shape[:3]
    for k in range(count):
        batch = order[2 * k + member]
        mine = owner[batch] == slab
        out = gh.at[k]

        @pl.when(jnp.logical_not(mine))
        def _():
            out[...] = jnp.zeros(out.shape, F32)

        @pl.when(mine)
        def _():
            pair = jnp.zeros(out.shape, F32)
            for t in range(tiles):
                a, b = keep[k, t], other[k, t]
                prior = jnp.concatenate(
                    [jnp.where(member == 0, a, b), jnp.where(member == 0, b, a)], axis=0
                )
                mean = jnp.sum(prior, axis=0, keepdims=True) / (2 * members)
                anomaly = prior - mean
                scaled = anomaly / variance[batch, :, pl.ds(t * LANES, LANES)]
                misfit = observed[batch, :, pl.ds(t * LANES, LANES)] - mean
                pair += lax.dot_general(
                    scaled,
                    jnp.concatenate([anomaly, misfit], axis=0),
                    (((1,), (1,)), ((), ())),
                    precision=HIGH,
                    preferred_element_type=F32,
                )
            h = lax.dot_general(
                pair[:, 2 * members :], rotation(2 * members), (((1,), (0,)), ((), ())),
                precision=HIGH, preferred_element_type=F32,
            )
            out[...] = jnp.concatenate([pair[:, : 2 * members], h], axis=1)


def gram(ids, owner, order, keep, other, observed, variance):
    count, _, members, _ = keep.shape
    total = 2 * members
    smem = pl.BlockSpec(memory_space=pltpu.SMEM)
    vmem = pl.BlockSpec(memory_space=pltpu.VMEM)
    return pl.pallas_call(
        gram_kernel,
        out_shape=jax.ShapeDtypeStruct((count, total, 2 * total), F32),
        in_specs=[smem] * 3 + [vmem] * 4,
        out_specs=vmem,
        compiler_params=params(12),
        name="gram",
    )(ids, owner, order, keep, other, observed, variance[:, None, :])


def rotation(size):
    step = size**-0.5
    row = lax.broadcasted_iota(jnp.int32, (size, size), 0)
    col = lax.broadcasted_iota(jnp.int32, (size, size), 1)
    v_row = (row == size - 1).astype(F32) - step
    v_col = (col == size - 1).astype(F32) - step
    return (row == col).astype(F32) - v_row * v_col / (1.0 - step)


def split3(x):
    high = x.astype(BF16)
    rest = x - high.astype(F32)
    mid = rest.astype(BF16)
    return high, mid, (rest - mid.astype(F32)).astype(BF16)


def dot32(x, y, lhs, rhs):
    parts = split3(x)
    m = x.shape[1 - lhs]
    out = None
    for k, right in enumerate(split3(y)):
        left = jnp.concatenate(parts[: 3 - k], axis=1 - lhs)
        each = lax.dot_general(
            left, right, (((lhs,), (rhs,)), ((), ())), preferred_element_type=F32
        )
        for j in reversed(range(3 - k)):
            piece = each[j * m : (j + 1) * m]
            out = piece if out is None else out + piece
    return out


def total(terms):
    while len(terms) > 1:
        terms = [x + y for x, y in zip(terms[::2], terms[1::2])]
    return terms[0]


def eliminate(a, b, rows_a, rows_b):
    groups = a.shape[0] // SUB
    wide = (SUB, LANES)
    sub = lax.broadcasted_iota(jnp.int32, wide, 0)
    a = [a[g * SUB : (g + 1) * SUB] for g in range(groups)]
    b = [b[g * SUB : (g + 1) * SUB] for g in range(groups)]
    plain, scaled = [], []

    def column(x, k):
        return jnp.broadcast_to(x[:, k : k + 1], wide)

    def row(x, k):
        return jnp.broadcast_to(x[k : k + 1, :], wide)

    def less(x, scale, first, second, n):
        return x - scale * (first * n[0] + second * n[1])

    c = [column(a[0], k) for k in range(SUB)]
    kk, kl, ll = row(c[0], 0), row(c[1], 0), row(c[1], 1)
    for p in range(groups):
        c = [(x, x) for x in c]
        pa, pb = (a[p], a[p]), (b[p], b[p])
        plain.append(b[p])
        after = p + 1 if p + 1 < groups else None
        cols = {g: [column(a[g], p * SUB + k) for k in range(SUB)] for g in range(p + 1, groups)}
        e = cols.get(after)
        ahead = None
        for k in range(0, SUB, 2):
            (fk, ck), (fl, cl) = c[k], c[k + 1]
            scale = pl.reciprocal(kk * ll - kl * kl, approx=True)

            def pivot_rows(x, k=k, kk=kk, kl=kl, ll=ll):
                u, w = row(x, k), row(x, k + 1)
                return ll * u - kl * w, kk * w - kl * u

            def inside(x, n, k=k, ck=ck, cl=cl, scale=scale):
                rest = less(x[1], scale, ck, cl, n)
                done = jnp.where(
                    sub == k, scale * n[0], jnp.where(sub == k + 1, scale * n[1], rest)
                )
                return rest, done

            n = {j: pivot_rows(c[j][0]) for j in range(k + 2, SUB)}
            if k + 2 < SUB:
                here = (k + 2, k + 3)
                left, right = ([row(x, i) for i in here] for x in (fk, fl))
                first, second = c[k + 2][0], c[k + 3][0]
                blocks = (
                    less(row(first, k + 2), scale, left[0], right[0], n[k + 2]),
                    less(row(second, k + 2), scale, left[0], right[0], n[k + 3]),
                    less(row(second, k + 3), scale, left[1], right[1], n[k + 3]),
                )
            if ahead:
                upper, lower = ahead
                m = [pivot_rows(x) for x in upper]
                if k + 2 == SUB:
                    left, right = ([row(x, i) for i in (0, 1)] for x in (e[k], e[k + 1]))
                    blocks = (
                        less(row(lower[0], 0), scale, left[0], right[0], m[0]),
                        less(row(lower[1], 0), scale, left[0], right[0], m[1]),
                        less(row(lower[1], 1), scale, left[1], right[1], m[1]),
                    )
                upper = [less(x, scale, fk, fl, y) for x, y in zip(upper, m)]
                lower = [less(x, scale, e[k], e[k + 1], y) for x, y in zip(lower, m)]
                ahead = upper, lower
            for j in range(k + 2, SUB):
                c[j] = inside(c[j], n[j])
                if after:
                    e[j] = less(e[j], scale, e[k], e[k + 1], n[j])
            if after:
                m = pivot_rows(pa[0])
                pa = inside(pa, m)
                a[after] = less(a[after], scale, e[k], e[k + 1], m)
            m = pivot_rows(pb[0])
            pb = inside(pb, m)
            if after:
                b[after] = less(b[after], scale, e[k], e[k + 1], m)
                if k + 2 == SUB - 2 * AHEAD:
                    ahead = [
                        [column(x, (p + 1) * SUB + j) for j in range(SUB)] for x in (pa[0], a[after])
                    ]
            kk, kl, ll = blocks
        pa, pb = pa[1], pb[1]
        scaled.append(pb)
        if after:
            c = ahead[1]
        if p + 2 < groups:
            here = p % 2
            rows_a[here] = pa
            rows_b[here] = pb
            ra = [rows_a[here, pl.ds(k, SUB, stride=0), :] for k in range(SUB)]
            rb = [rows_b[here, pl.ds(k, SUB, stride=0), :] for k in range(SUB)]
            for g in range(p + 2, groups):
                a[g] = a[g] - total([cols[g][k] * ra[k] for k in range(SUB)])
                b[g] = b[g] - total([cols[g][k] * rb[k] for k in range(SUB)])
    return jnp.concatenate(plain, axis=0), jnp.concatenate(scaled, axis=0)


def chain_kernel(ids, mine, other, out, rows_a, rows_b):
    member = ids[1]
    count, size, width = mine.shape
    row = lax.broadcasted_iota(jnp.int32, (size, width), 0)
    lane = lax.broadcasted_iota(jnp.int32, (size, width), 1)
    diagonal = jnp.where(row == lane, size - 1.0, 0.0)

    def step(position, vt):
        k = lax.div(position, 2)
        gh = jnp.where(lax.rem(position, 2) == member, mine[k], other[k])
        zt = jnp.where(row == size - 1, 0.0, vt)
        s = dot32(zt[:, :size], gh, 1, 0)
        v = vt[:, :size]
        t = dot32(s[:, :size], jnp.concatenate([v, v], axis=0), 1, 1)
        a = jnp.where(lane == size - 1, 0.0, t) + diagonal
        b = jnp.where(lane < size, zt, s - t)
        plain, scaled = eliminate(a, b, rows_a, rows_b)
        return vt + dot32(plain, scaled, 0, 0)[size:]

    unit = rotation(size)
    start = jnp.concatenate([unit, jnp.zeros_like(unit)], axis=1)
    vt = lax.fori_loop(0, 2 * count, step, start)
    w = dot32(unit, vt[:, :size], 1, 0)
    half = size // 2
    first, second = w[:, :half], w[:, half:]
    w = jnp.concatenate(
        [jnp.where(member == 0, first, second), jnp.where(member == 0, second, first)], axis=1
    )
    high = w.astype(BF16).astype(F32)
    low = w - high
    out[...] = jnp.concatenate(
        [jnp.concatenate([high, high], axis=1), jnp.concatenate([low, jnp.zeros_like(low)], axis=1)],
        axis=0,
    )


def chain(ids, mine, other):
    size = mine.shape[1]
    rows = pltpu.VMEM((2, SUB, LANES), F32)
    return pl.pallas_call(
        chain_kernel,
        out_shape=jax.ShapeDtypeStruct((2 * size, 2 * size), F32),
        in_specs=[SMEM] + [VMEM] * 2,
        out_specs=VMEM,
        scratch_shapes=[rows, rows],
        compiler_params=params(12),
        name="chain",
    )(ids, mine, other)


def apply_kernel(ids, w_ref, own0, other0, own1, other1, out, held, sems):
    size = w_ref.shape[0] // 2
    rows, nct = own0.shape[:2]
    half = nct // 2
    first_tile = ids[1] * half
    weights = w_ref[...].astype(BF16)
    flat = held.reshape(held.size // LANES, LANES)

    for field, sources in enumerate(((own0, other0), (own1, other1))):

        def copy(block, slot, field=field):
            return pltpu.make_async_copy(held.at[slot], out.at[:, field, block], sems.at[slot])

        def step(block, carry, field=field, sources=sources, copy=copy):
            slot = lax.rem(block, 2)

            @pl.when((block >= 2) if field == 0 else (block >= 0))
            def _():
                copy(block, slot).wait()

            base = slot * size * half * SUB
            for r in range(SUB):
                parts = [
                    jnp.concatenate(
                        [src[block * SUB + r, first_tile + ct] for ct in range(half)], axis=1
                    )
                    for src in sources
                ]
                high = [x.astype(BF16) for x in parts]
                low = [(x - y.astype(F32)).astype(BF16) for x, y in zip(parts, high)]
                stacked = jnp.concatenate([*high, *low], axis=0)
                result = jnp.dot(weights, stacked, preferred_element_type=F32)
                result = result[:size] + result[size:]
                for ct in range(half):
                    flat[pl.ds(base + ct * SUB + r, size, stride=half * SUB), :] = result[
                        :, ct * LANES : (ct + 1) * LANES
                    ]
            copy(block, slot).start()
            return carry

        lax.fori_loop(0, rows // SUB, step, 0)
    for slot in range(2):
        copy(0, slot).wait()


def apply(ids, weights, own0, other0, own1, other1):
    rows, nct, members, _ = own0.shape
    size = 2 * members
    half = nct // 2
    r8 = rows // SUB
    return pl.pallas_call(
        apply_kernel,
        out_shape=jax.ShapeDtypeStruct((size, 2, r8, half, SUB, LANES), F32),
        in_specs=[SMEM] + [VMEM] * 5,
        out_specs=pl.BlockSpec(memory_space=pl.ANY),
        scratch_shapes=[
            pltpu.VMEM((2, size, half, SUB, LANES), F32),
            pltpu.SemaphoreType.DMA((2,)),
        ],
        compiler_params=params(12),
        name="apply",
    )(ids, weights, own0, other0, own1, other1)


def body(state, courant, diffusion, obs_cells, obs_owner, batch_order, obs_values, obs_error):
    slab = lax.axis_index("space")
    member = lax.axis_index("member")
    space = lax.axis_size("space")
    ids = jnp.stack([slab, member]).astype(jnp.int32)
    up = [(i, i + 1) for i in range(space - 1)]
    down = [(i + 1, i) for i in range(space - 1)]
    swap = [(0, 1), (1, 0)]

    state6, flow5, nu5 = tiled(state), tiled(courant), tiled(diffusion)
    up_edge, down_edge = pack_edges(state6, flow5, nu5)
    before = lax.ppermute(up_edge, "space", up)
    after = lax.ppermute(down_edge, "space", down)
    full0, turned0, held0, held1 = forecast_inner(state6, flow5, nu5)
    full0, _, _, held1, keep, away = forecast_edges(
        ids, obs_cells, obs_owner, batch_order, flow5, nu5, before, after,
        full0, turned0, held0, held1,
    )
    other = lax.ppermute(away, "member", swap)
    gh = gram(ids, obs_owner, batch_order, keep, other, obs_values, obs_error)

    groups = list(range(held1.shape[0]))
    field1 = ()
    bit = 1
    while bit < space:
        received = lax.ppermute(gh, "space", [(i, i ^ bit) for i in range(space)])
        if groups:
            held1, gh = lax.optimization_barrier((held1, gh))
            field1 = forecast_piece(groups.pop(0), flow5, nu5, before, after, held1, field1)
            received, field1 = lax.optimization_barrier((received, (field1,)))
        gh = gh + received
        bit *= 2
    for group in groups:
        field1 = (forecast_piece(group, flow5, nu5, before, after, held1, field1),)
    (full1,) = field1
    theirs = lax.ppermute(gh, "member", swap)
    full0, full1, gh, theirs = lax.optimization_barrier((full0, full1, gh, theirs))
    other0 = lax.ppermute(full0, "member", swap)
    other1 = lax.ppermute(full1, "member", swap)
    weights = chain(ids, gh, theirs)
    return untiled(apply(ids, weights, full0, other0, full1, other1))


def solution(mesh):
    placed = (
        P("member", None, "space", None),
        P(None, "space", None),
        P(None, "space", None),
        P(),
        P(),
        P(),
        P(),
        P(),
    )
    return jax.shard_map(
        body,
        mesh=mesh,
        in_specs=placed,
        out_specs=P(None, None, "space", "member"),
        check_vma=False,
    )
```

```python
import functools

import jax
import jax.numpy as jnp
from jax import lax
from jax.experimental import pallas as pl
from jax.experimental.pallas import tpu as pltpu
from jax.sharding import PartitionSpec as P

HIGH = lax.Precision.HIGHEST
F32 = jnp.float32
BF16 = jnp.bfloat16
LANES = 128
SUB = 8
GATHER = 32
AHEAD = 1
PACK = 8


def params(mib):
    return pltpu.CompilerParams(vmem_limit_bytes=mib * 1024 * 1024)


def unrolled(count, most):
    return max(d for d in range(1, most + 1) if count % d == 0)


def rows_loop(count, most, fn):
    step = unrolled(count, most)

    def run(i, carry):
        for u in range(step):
            fn(i * step + u)
        return carry

    lax.fori_loop(0, count // step, run, 0)


def tiled(array):
    *lead, rows, cols = array.shape
    n = len(lead)
    split = array.reshape(*lead, rows // SUB, SUB, cols // LANES, LANES)
    return jnp.transpose(split, (*range(n), n, n + 2, n + 1, n + 3))


def untiled(array):
    *lead, r8, ct, sub, lanes = array.shape
    n = len(lead)
    back = jnp.transpose(array, (*range(n), n, n + 2, n + 1, n + 3))
    return back.reshape(*lead, r8 * sub, ct * lanes)


def pack_kernel(state, flow, nu, up, down, edge_flow, edge_nu, sems):
    members, fields, r8, nct = state.shape[:4]
    sides = ((up, r8 - 1, (SUB - 2, SUB - 1)), (down, 0, (0, 1)))
    copies = []

    def copy(src, dst):
        copies.append(pltpu.make_async_copy(src, dst, sems.at[len(copies)]))

    for side, (msg, block, rows) in enumerate(sides):
        copy(flow.at[:, block], edge_flow.at[side])
        copy(nu.at[:, block], edge_nu.at[side])
    for msg, block, rows in sides:
        for field in range(fields):
            for ct in range(nct):
                for at, row in enumerate(rows):
                    copy(
                        state.at[:, field, block, ct, row, :],
                        msg.at[ct, pl.ds((field * 2 + at) * members, members), :],
                    )
    for one in copies:
        one.start()
    for one in copies[:4]:
        one.wait()
    for side, (msg, block, rows) in enumerate(sides):
        edge = (SUB - 1, 0)[side]
        for ct in range(nct):
            numbers = [edge_flow[side, k, ct, edge : edge + 1, :] for k in range(2)]
            numbers += [edge_nu[side, k, ct, edge : edge + 1, :] for k in range(fields)]
            numbers.append(jnp.zeros((PACK - 2 - fields, LANES), F32))
            msg[ct, pl.ds(2 * fields * members, PACK), :] = jnp.concatenate(numbers, axis=0)
    for one in copies[4:]:
        one.wait()


def pack_edges(state6, flow5, nu5):
    members, fields, r8, nct = state6.shape[:4]
    msg = jax.ShapeDtypeStruct((nct, 2 * fields * members + PACK, LANES), F32)
    edge = pltpu.VMEM((2, 2, nct, SUB, LANES), F32)
    return pl.pallas_call(
        pack_kernel,
        out_shape=[msg] * 2,
        in_specs=[pl.BlockSpec(memory_space=pl.ANY)] * 3,
        out_specs=[pl.BlockSpec(memory_space=pltpu.VMEM)] * 2,
        scratch_shapes=[edge, edge, pltpu.SemaphoreType.DMA((4 + 4 * fields * nct,))],
        compiler_params=params(56),
        name="pack_edges",
    )(state6, flow5, nu5)


PAD = SUB


def stencil_coefs(flow_x, flow_y, nu, col, width):
    east = nu - jnp.minimum(flow_x, 0.0)
    west = nu + jnp.maximum(flow_x, 0.0)
    north = nu - jnp.minimum(flow_y, 0.0)
    south = nu + jnp.maximum(flow_y, 0.0)
    centre = 1.0 - (east + west + north + south)
    south = jnp.where(col == 0, 0.0, south)
    north = jnp.where(col == width - 1, 0.0, north)
    return centre, west, east, south, north


def fill_coefs(coef, field, flow, nu, blocks, before=None, after=None):
    _, r8, nct = flow.shape[:3]
    width = nct * LANES
    for ct in range(nct):
        for first, count in blocks:
            shape = (count * SUB, LANES)
            col = lax.broadcasted_iota(jnp.int32, shape, 1) + ct * LANES
            part = pl.ds(first, count)
            numbers = (flow[0, part, ct], flow[1, part, ct], nu[field, part, ct])
            numbers = [x.reshape(shape) for x in numbers]
            for k, value in enumerate(stencil_coefs(*numbers, col, width)):
                coef[k, ct, pl.ds(PAD + first * SUB, count * SUB), :] = value
        for msg, row in ((before, PAD - 1), (after, PAD + r8 * SUB)):
            if msg is not None:
                col = lax.broadcasted_iota(jnp.int32, (1, LANES), 1) + ct * LANES
                base = msg.shape[1] - PACK
                numbers = [msg[ct, pl.ds(base + k, 1), :] for k in (0, 1, 2 + field)]
                for k, value in enumerate(stencil_coefs(*numbers, col, width)):
                    coef[k, ct, pl.ds(row, 1), :] = value


def stencil(mid, west, east, weights):
    nct = len(mid)
    lane = lax.broadcasted_iota(jnp.int32, (SUB, LANES), 1)
    right = [pltpu.roll(x, 1, 1) for x in mid]
    left = [pltpu.roll(x, LANES - 1, 1) for x in mid]
    out = []
    for ct in range(nct):
        south = jnp.where(lane == 0, right[(ct - 1) % nct], right[ct])
        north = jnp.where(lane == LANES - 1, left[(ct + 1) % nct], left[ct])
        centre, w_w, w_e, w_s, w_n = weights[ct]
        out.append(
            (centre * mid[ct] + w_w * west[ct]) + (w_e * east[ct] + (w_s * south + w_n * north))
        )
    return out


class Rows:
    def __init__(self, held, coef):
        self.nct, _, blocks = held.shape[-5:-2]
        self.room = blocks * SUB
        self.flat = held.reshape(held.size // LANES, LANES)
        self.coef = coef.reshape(coef.size // LANES, LANES)

    def at(self, group, ct, row):
        start = (group * self.nct + ct) * SUB * self.room + PAD + row
        return pl.ds(start, SUB, stride=self.room)

    def load(self, group, row):
        return [self.flat[self.at(group, ct, row), :] for ct in range(self.nct)]

    def weights(self, row):
        return [
            [
                self.coef[pl.ds((k * self.nct + ct) * self.room + PAD + row, SUB, stride=0), :]
                for k in range(5)
            ]
            for ct in range(self.nct)
        ]


def group_steps(group, held, between, coef, put, edges):
    groups, nct, _, blocks = held.shape[:4]
    room = blocks * SUB
    source = held.reshape(groups, nct, SUB, room, LANES)
    middle = between.reshape(nct, SUB, room, LANES)

    def block_step(block, load, store):
        at = PAD + block * SUB
        weights = [[coef[k, ct, pl.ds(at, SUB), :] for k in range(5)] for ct in range(nct)]
        for m in range(SUB):
            mid, west, east = [
                [load(ct, m, pl.ds(at + off, SUB)) for ct in range(nct)] for off in (0, -1, 1)
            ]
            for ct, value in enumerate(stencil(mid, west, east, weights)):
                store(block, ct, m, value)

    def keep(block, ct, m, value):
        middle[ct, m, pl.ds(PAD + block * SUB, SUB), :] = value

    for block in range(blocks - 2):
        block_step(block, lambda ct, m, rows: source[group, ct, m, rows, :], keep)
    if edges:
        field, inner = Rows(held, coef), Rows(between, coef)
        for row in (-1, (blocks - 2) * SUB):
            around = [field.load(group, row + off) for off in (0, -1, 1)]
            for ct, value in enumerate(stencil(*around, field.weights(row))):
                inner.flat[inner.at(0, ct, row), :] = value
    for block in range(blocks - 2):
        block_step(block, lambda ct, m, rows: middle[ct, m, rows, :], put)


def held_shape(members, nct, r8):
    return (members // SUB, nct, SUB, r8 + 2, SUB, LANES)


def cost(cells):
    return pl.CostEstimate(flops=40 * cells, bytes_accessed=8 * cells, transcendentals=0)


SMEM = pl.BlockSpec(memory_space=pltpu.SMEM)
VMEM = pl.BlockSpec(memory_space=pltpu.VMEM)


def inner_kernel(state, flow, nu, full, held0, held1, between, coef, sems):
    groups, nct, _, blocks = held0.shape[:4]
    members = groups * SUB
    r8 = blocks - 2

    def copies(field, held, group):
        return [
            pltpu.make_async_copy(
                state.at[pl.ds(group * SUB, SUB), field, :, ct],
                held.at[group, ct, :, pl.ds(1, r8)],
                sems.at[field, group, ct],
            )
            for ct in range(nct)
        ]

    for group in range(groups):
        for one in copies(0, held0, group):
            one.start()
    fill_coefs(coef, 0, flow, nu, [(0, r8)])
    flat = full.reshape(full.size // LANES, LANES)

    def run(group, carry):
        for one in copies(0, held0, group):
            one.wait()
        for one in copies(1, held1, group):
            one.start()

        def put(block, ct, m, value):
            start = (block * SUB * nct + ct) * members + group * SUB + m
            flat[pl.ds(start, SUB, stride=nct * members), :] = value

        group_steps(group, held0, between, coef, put, False)
        return carry

    lax.fori_loop(0, groups, run, 0)
    for group in range(groups):
        for one in copies(1, held1, group):
            one.wait()


def forecast_inner(state6, flow5, nu5):
    members, _, r8, nct = state6.shape[:4]
    held = held_shape(members, nct, r8)
    return pl.pallas_call(
        inner_kernel,
        out_shape=[
            jax.ShapeDtypeStruct((r8 * SUB, nct, members, LANES), F32),
            jax.ShapeDtypeStruct(held, F32),
            jax.ShapeDtypeStruct(held, F32),
        ],
        in_specs=[pl.BlockSpec(memory_space=pl.ANY)] + [VMEM] * 2,
        out_specs=[VMEM] * 3,
        scratch_shapes=[
            pltpu.VMEM(held[1:], F32),
            pltpu.VMEM((5, nct, (r8 + 2) * SUB, LANES), F32),
            pltpu.SemaphoreType.DMA((2, held[0], nct)),
        ],
        compiler_params=params(34),
        cost_estimate=cost(members * r8 * SUB * nct * LANES),
        name="forecast_inner",
    )(state6, flow5, nu5)


def edge_kernel(
    ids, cells, owner, order, flow, nu, before, after, full_in, held0_in, held1_in,
    full, held0, held1, keep, away, coef
):
    groups, nct, _, blocks = held0.shape[:4]
    members = groups * SUB
    r8 = blocks - 2
    rows = r8 * SUB
    slab, member = ids[0], ids[1]

    for field, held in ((0, held0), (1, held1)):
        view = Rows(held, coef)
        for ct in range(nct):
            for group in range(groups):
                for k in range(2):
                    part = pl.ds((2 * field + k) * members + group * SUB, SUB)
                    view.flat[view.at(group, ct, k - 2), :] = before[ct, part, :]
                    view.flat[view.at(group, ct, rows + k), :] = after[ct, part, :]

    fill_coefs(coef, 0, flow, nu, [(0, 1), (r8 - 1, 1)], before, after)
    view = Rows(held0, coef)
    for first in (0, rows - 2):
        for group in range(groups):
            old = {r: view.load(group, r) for r in range(first - 2, first + 4)}
            one = {
                r: stencil(old[r], old[r - 1], old[r + 1], view.weights(r))
                for r in range(first - 1, first + 3)
            }
            for r in range(first, first + 2):
                new = stencil(one[r], one[r - 1], one[r + 1], view.weights(r))
                for ct, value in enumerate(new):
                    full[r, ct, pl.ds(group * SUB, SUB), :] = value

    nobs = cells.shape[1]
    tiles = full.reshape(rows * nct, members, LANES)
    lane = lax.broadcasted_iota(jnp.int32, (members, LANES), 1)
    for position in range(order.shape[0]):
        batch = order[position]
        mine = owner[batch] == slab
        kept = lax.rem(position, 2) == member

        def pick(tile, carry, batch=batch, mine=mine, kept=kept, position=position):
            def some(group, acc):
                for u in range(GATHER):
                    o = group * GATHER + u
                    cell = cells[batch, tile * LANES + o]
                    tile_at = lax.shift_right_logical(cell, LANES.bit_length() - 1)
                    moved = pltpu.roll(tiles[tile_at], (o - cell) & (LANES - 1), 1)
                    acc = jnp.where(lane == o, moved, acc)
                return acc

            acc = lax.fori_loop(
                0, jnp.where(mine, LANES // GATHER, 0), some, jnp.zeros((members, LANES), F32)
            )

            @pl.when(kept)
            def _():
                keep[position // 2, tile] = acc

            @pl.when(jnp.logical_not(kept))
            def _():
                away[position // 2, tile] = acc

            return carry

        lax.fori_loop(0, nobs // LANES, pick, 0)


def forecast_edges(ids, cells, owner, order, flow5, nu5, before, after, full, held0, held1):
    members = full.shape[2]
    nct, _, blocks = held0.shape[1:4]
    nb, nobs = cells.shape
    picks = jax.ShapeDtypeStruct((nb // 2, nobs // LANES, members, LANES), F32)
    same = [jax.ShapeDtypeStruct(x.shape, F32) for x in (full, held0, held1)]
    return pl.pallas_call(
        edge_kernel,
        out_shape=[*same, picks, picks],
        in_specs=[SMEM] * 4 + [VMEM] * 7,
        out_specs=[VMEM] * 5,
        input_output_aliases={8: 0, 9: 1, 10: 2},
        scratch_shapes=[pltpu.VMEM((5, nct, blocks * SUB, LANES), F32)],
        compiler_params=params(6),
        cost_estimate=cost(members * SUB * nct * LANES),
        name="forecast_edges",
    )(ids, cells, owner, order, flow5, nu5, before, after, full, held0, held1)


def piece_kernel(group, flow, nu, before, after, held, *rest):
    full, between, coef = rest[-3:]
    rows, nct, members = full.shape[:3]
    flat = full.reshape(full.size // LANES, LANES)
    fill_coefs(coef, 1, flow, nu, [(0, rows // SUB)], before, after)

    def put(block, ct, m, value):
        start = (block * SUB * nct + ct) * members + group * SUB + m
        flat[pl.ds(start, SUB, stride=nct * members), :] = value

    group_steps(group, held, between, coef, put, True)


def forecast_piece(group, flow5, nu5, before, after, held, done):
    groups, nct, _, blocks = held.shape[:4]
    rows = (blocks - 2) * SUB
    return pl.pallas_call(
        functools.partial(piece_kernel, group),
        out_shape=jax.ShapeDtypeStruct((rows, nct, groups * SUB, LANES), F32),
        in_specs=[VMEM] * (5 + len(done)),
        out_specs=VMEM,
        input_output_aliases={5: 0} if done else {},
        scratch_shapes=[
            pltpu.VMEM(held.shape[1:], F32),
            pltpu.VMEM((5, nct, blocks * SUB, LANES), F32),
        ],
        compiler_params=params(6),
        cost_estimate=cost(SUB * rows * nct * LANES),
        name=f"forecast_members_{group}",
    )(flow5, nu5, before, after, held, *done)


def gram_kernel(ids, owner, order, keep, other, observed, variance, gh):
    slab, member = ids[0], ids[1]
    count, tiles, members = keep.shape[:3]
    for k in range(count):
        batch = order[2 * k + member]
        mine = owner[batch] == slab
        out = gh.at[k]

        @pl.when(jnp.logical_not(mine))
        def _():
            out[...] = jnp.zeros(out.shape, F32)

        @pl.when(mine)
        def _():
            pair = jnp.zeros(out.shape, F32)
            for t in range(tiles):
                a, b = keep[k, t], other[k, t]
                prior = jnp.concatenate(
                    [jnp.where(member == 0, a, b), jnp.where(member == 0, b, a)], axis=0
                )
                mean = jnp.sum(prior, axis=0, keepdims=True) / (2 * members)
                anomaly = prior - mean
                scaled = anomaly / variance[batch, :, pl.ds(t * LANES, LANES)]
                misfit = observed[batch, :, pl.ds(t * LANES, LANES)] - mean
                pair += lax.dot_general(
                    scaled,
                    jnp.concatenate([anomaly, misfit], axis=0),
                    (((1,), (1,)), ((), ())),
                    precision=HIGH,
                    preferred_element_type=F32,
                )
            h = lax.dot_general(
                pair[:, 2 * members :], rotation(2 * members), (((1,), (0,)), ((), ())),
                precision=HIGH, preferred_element_type=F32,
            )
            out[...] = jnp.concatenate([pair[:, : 2 * members], h], axis=1)


def gram(ids, owner, order, keep, other, observed, variance):
    count, _, members, _ = keep.shape
    total = 2 * members
    smem = pl.BlockSpec(memory_space=pltpu.SMEM)
    vmem = pl.BlockSpec(memory_space=pltpu.VMEM)
    return pl.pallas_call(
        gram_kernel,
        out_shape=jax.ShapeDtypeStruct((count, total, 2 * total), F32),
        in_specs=[smem] * 3 + [vmem] * 4,
        out_specs=vmem,
        compiler_params=params(12),
        name="gram",
    )(ids, owner, order, keep, other, observed, variance[:, None, :])


def rotation(size):
    step = size**-0.5
    row = lax.broadcasted_iota(jnp.int32, (size, size), 0)
    col = lax.broadcasted_iota(jnp.int32, (size, size), 1)
    v_row = (row == size - 1).astype(F32) - step
    v_col = (col == size - 1).astype(F32) - step
    return (row == col).astype(F32) - v_row * v_col / (1.0 - step)


def split3(x):
    high = x.astype(BF16)
    rest = x - high.astype(F32)
    mid = rest.astype(BF16)
    return high, mid, (rest - mid.astype(F32)).astype(BF16)


def dot32(x, y, lhs, rhs):
    parts = split3(x)
    m = x.shape[1 - lhs]
    out = None
    for k, right in enumerate(split3(y)):
        left = jnp.concatenate(parts[: 3 - k], axis=1 - lhs)
        each = lax.dot_general(
            left, right, (((lhs,), (rhs,)), ((), ())), preferred_element_type=F32
        )
        for j in reversed(range(3 - k)):
            piece = each[j * m : (j + 1) * m]
            out = piece if out is None else out + piece
    return out


def total(terms):
    while len(terms) > 1:
        terms = [x + y for x, y in zip(terms[::2], terms[1::2])]
    return terms[0]


def eliminate(a_ref, b_ref, scaled, rows_a, rows_b):
    groups = a_ref.shape[0] // SUB
    wide = (SUB, LANES)
    sub = lax.broadcasted_iota(jnp.int32, wide, 0)
    part = [pl.ds(g * SUB, SUB) for g in range(groups)]

    def column(x, k):
        return jnp.broadcast_to(x[:, k : k + 1], wide)

    def row(x, k):
        return jnp.broadcast_to(x[k : k + 1, :], wide)

    def less(x, scale, first, second, n):
        return x - scale * (first * n[0] + second * n[1])

    a_next, b_next = a_ref[part[0], :], b_ref[part[0], :]
    c = [column(a_next, k) for k in range(SUB)]
    kk, kl, ll = row(c[0], 0), row(c[1], 0), row(c[1], 1)
    for p in range(groups):
        c = [(x, x) for x in c]
        pa, pb = (a_next, a_next), (b_next, b_next)
        after = p + 1 if p + 1 < groups else None
        if after:
            a_next, b_next = a_ref[part[after], :], b_ref[part[after], :]
            e = [column(a_next, p * SUB + k) for k in range(SUB)]
        ahead = None
        for k in range(0, SUB, 2):
            (fk, ck), (fl, cl) = c[k], c[k + 1]
            scale = pl.reciprocal(kk * ll - kl * kl, approx=True)

            def pivot_rows(x, k=k, kk=kk, kl=kl, ll=ll):
                u, w = row(x, k), row(x, k + 1)
                return ll * u - kl * w, kk * w - kl * u

            def inside(x, n, k=k, ck=ck, cl=cl, scale=scale):
                rest = less(x[1], scale, ck, cl, n)
                done = jnp.where(
                    sub == k, scale * n[0], jnp.where(sub == k + 1, scale * n[1], rest)
                )
                return rest, done

            n = {j: pivot_rows(c[j][0]) for j in range(k + 2, SUB)}
            if k + 2 < SUB:
                here = (k + 2, k + 3)
                left, right = ([row(x, i) for i in here] for x in (fk, fl))
                first, second = c[k + 2][0], c[k + 3][0]
                blocks = (
                    less(row(first, k + 2), scale, left[0], right[0], n[k + 2]),
                    less(row(second, k + 2), scale, left[0], right[0], n[k + 3]),
                    less(row(second, k + 3), scale, left[1], right[1], n[k + 3]),
                )
            if ahead:
                upper, lower = ahead
                m = [pivot_rows(x) for x in upper]
                if k + 2 == SUB:
                    left, right = ([row(x, i) for i in (0, 1)] for x in (e[k], e[k + 1]))
                    blocks = (
                        less(row(lower[0], 0), scale, left[0], right[0], m[0]),
                        less(row(lower[1], 0), scale, left[0], right[0], m[1]),
                        less(row(lower[1], 1), scale, left[1], right[1], m[1]),
                    )
                upper = [less(x, scale, fk, fl, y) for x, y in zip(upper, m)]
                lower = [less(x, scale, e[k], e[k + 1], y) for x, y in zip(lower, m)]
                ahead = upper, lower
            for j in range(k + 2, SUB):
                c[j] = inside(c[j], n[j])
                if after:
                    e[j] = less(e[j], scale, e[k], e[k + 1], n[j])
            if after:
                m = pivot_rows(pa[0])
                pa = inside(pa, m)
                a_next = less(a_next, scale, e[k], e[k + 1], m)
            m = pivot_rows(pb[0])
            pb = inside(pb, m)
            if after:
                b_next = less(b_next, scale, e[k], e[k + 1], m)
                if k + 2 == SUB - 2 * AHEAD:
                    ahead = [
                        [column(x, (p + 1) * SUB + j) for j in range(SUB)] for x in (pa[0], a_next)
                    ]
            kk, kl, ll = blocks
        pa, pb = pa[1], pb[1]
        scaled[part[p], :] = pb
        if after:
            c = ahead[1]
            b_ref[part[after], :] = b_next
        if p + 2 < groups:
            here = p % 2
            rows_a[here] = pa
            rows_b[here] = pb
            ra = [rows_a[here, pl.ds(k, SUB, stride=0), :] for k in range(SUB)]
            rb = [rows_b[here, pl.ds(k, SUB, stride=0), :] for k in range(SUB)]
            for g in range(p + 2, groups):
                old = a_ref[part[g], :]
                cols = [column(old, p * SUB + k) for k in range(SUB)]
                a_ref[part[g], :] = old - total([x * y for x, y in zip(cols, ra)])
                b_ref[part[g], :] = b_ref[part[g], :] - total([x * y for x, y in zip(cols, rb)])


def chain_kernel(ids, mine, other, out, a, b, scaled, rows_a, rows_b):
    member = ids[1]
    count, size, width = mine.shape
    row = lax.broadcasted_iota(jnp.int32, (size, width), 0)
    lane = lax.broadcasted_iota(jnp.int32, (size, width), 1)
    diagonal = jnp.where(row == lane, size - 1.0, 0.0)

    def step(position, vt):
        k = lax.div(position, 2)
        gh = jnp.where(lax.rem(position, 2) == member, mine[k], other[k])
        zt = jnp.where(row == size - 1, 0.0, vt)
        s = dot32(zt[:, :size], gh, 1, 0)
        v = vt[:, :size]
        t = dot32(s[:, :size], jnp.concatenate([v, v], axis=0), 1, 1)
        a[...] = jnp.where(lane == size - 1, 0.0, t) + diagonal
        b[...] = jnp.where(lane < size, zt, s - t)
        eliminate(a, b, scaled, rows_a, rows_b)
        return vt + dot32(b[...], scaled[...], 0, 0)[size:]

    unit = rotation(size)
    start = jnp.concatenate([unit, jnp.zeros_like(unit)], axis=1)
    vt = lax.fori_loop(0, 2 * count, step, start)
    w = dot32(unit, vt[:, :size], 1, 0)
    half = size // 2
    first, second = w[:, :half], w[:, half:]
    w = jnp.concatenate(
        [jnp.where(member == 0, first, second), jnp.where(member == 0, second, first)], axis=1
    )
    high = w.astype(BF16).astype(F32)
    low = w - high
    out[...] = jnp.concatenate(
        [jnp.concatenate([high, high], axis=1), jnp.concatenate([low, jnp.zeros_like(low)], axis=1)],
        axis=0,
    )


def chain(ids, mine, other):
    size = mine.shape[1]
    rows = pltpu.VMEM((2, SUB, LANES), F32)
    square = pltpu.VMEM((size, 2 * size), F32)
    return pl.pallas_call(
        chain_kernel,
        out_shape=jax.ShapeDtypeStruct((2 * size, 2 * size), F32),
        in_specs=[SMEM] + [VMEM] * 2,
        out_specs=VMEM,
        scratch_shapes=[square, square, square, rows, rows],
        compiler_params=params(12),
        name="chain",
    )(ids, mine, other)


def apply_kernel(ids, w_ref, own0, other0, own1, other1, out, held, sems):
    size = w_ref.shape[0] // 2
    rows, nct = own0.shape[:2]
    half = nct // 2
    first_tile = ids[1] * half
    weights = w_ref[...].astype(BF16)
    flat = held.reshape(held.size // LANES, LANES)

    for field, sources in enumerate(((own0, other0), (own1, other1))):

        def copy(block, slot, field=field):
            return pltpu.make_async_copy(held.at[slot], out.at[:, field, block], sems.at[slot])

        def step(block, carry, field=field, sources=sources, copy=copy):
            slot = lax.rem(block, 2)

            @pl.when((block >= 2) if field == 0 else (block >= 0))
            def _():
                copy(block, slot).wait()

            base = slot * size * half * SUB
            for r in range(SUB):
                parts = [
                    jnp.concatenate(
                        [src[block * SUB + r, first_tile + ct] for ct in range(half)], axis=1
                    )
                    for src in sources
                ]
                high = [x.astype(BF16) for x in parts]
                low = [(x - y.astype(F32)).astype(BF16) for x, y in zip(parts, high)]
                stacked = jnp.concatenate([*high, *low], axis=0)
                result = jnp.dot(weights, stacked, preferred_element_type=F32)
                result = result[:size] + result[size:]
                for ct in range(half):
                    flat[pl.ds(base + ct * SUB + r, size, stride=half * SUB), :] = result[
                        :, ct * LANES : (ct + 1) * LANES
                    ]
            copy(block, slot).start()
            return carry

        lax.fori_loop(0, rows // SUB, step, 0)
    for slot in range(2):
        copy(0, slot).wait()


def apply(ids, weights, own0, other0, own1, other1):
    rows, nct, members, _ = own0.shape
    size = 2 * members
    half = nct // 2
    r8 = rows // SUB
    return pl.pallas_call(
        apply_kernel,
        out_shape=jax.ShapeDtypeStruct((size, 2, r8, half, SUB, LANES), F32),
        in_specs=[SMEM] + [VMEM] * 5,
        out_specs=pl.BlockSpec(memory_space=pl.ANY),
        scratch_shapes=[
            pltpu.VMEM((2, size, half, SUB, LANES), F32),
            pltpu.SemaphoreType.DMA((2,)),
        ],
        compiler_params=params(12),
        name="apply",
    )(ids, weights, own0, other0, own1, other1)


def body(state, courant, diffusion, obs_cells, obs_owner, batch_order, obs_values, obs_error):
    slab = lax.axis_index("space")
    member = lax.axis_index("member")
    space = lax.axis_size("space")
    ids = jnp.stack([slab, member]).astype(jnp.int32)
    up = [(i, i + 1) for i in range(space - 1)]
    down = [(i + 1, i) for i in range(space - 1)]
    swap = [(0, 1), (1, 0)]

    state6, flow5, nu5 = tiled(state), tiled(courant), tiled(diffusion)
    up_edge, down_edge = pack_edges(state6, flow5, nu5)
    before = lax.ppermute(up_edge, "space", up)
    after = lax.ppermute(down_edge, "space", down)
    full0, held0, held1 = forecast_inner(state6, flow5, nu5)
    full0, _, held1, keep, away = forecast_edges(
        ids, obs_cells, obs_owner, batch_order, flow5, nu5, before, after, full0, held0, held1
    )
    other = lax.ppermute(away, "member", swap)
    gh = gram(ids, obs_owner, batch_order, keep, other, obs_values, obs_error)

    groups = list(range(held1.shape[0]))
    field1 = ()
    bit = 1
    while bit < space:
        received = lax.ppermute(gh, "space", [(i, i ^ bit) for i in range(space)])
        if groups:
            held1, gh = lax.optimization_barrier((held1, gh))
            field1 = forecast_piece(groups.pop(0), flow5, nu5, before, after, held1, field1)
            received, field1 = lax.optimization_barrier((received, (field1,)))
        gh = gh + received
        bit *= 2
    for group in groups:
        field1 = (forecast_piece(group, flow5, nu5, before, after, held1, field1),)
    (full1,) = field1
    theirs = lax.ppermute(gh, "member", swap)
    full0, full1, gh, theirs = lax.optimization_barrier((full0, full1, gh, theirs))
    other0 = lax.ppermute(full0, "member", swap)
    other1 = lax.ppermute(full1, "member", swap)
    weights = chain(ids, gh, theirs)
    return untiled(apply(ids, weights, full0, other0, full1, other1))


def solution(mesh):
    placed = (
        P("member", None, "space", None),
        P(None, "space", None),
        P(None, "space", None),
        P(),
        P(),
        P(),
        P(),
        P(),
    )
    return jax.shard_map(
        body,
        mesh=mesh,
        in_specs=placed,
        out_specs=P(None, None, "space", "member"),
        check_vma=False,
    )
```

```python
import functools

import jax
import jax.numpy as jnp
from jax import lax
from jax.experimental import pallas as pl
from jax.experimental.pallas import tpu as pltpu
from jax.sharding import PartitionSpec as P

HIGH = lax.Precision.HIGHEST
F32 = jnp.float32
BF16 = jnp.bfloat16
LANES = 128
SUB = 8
GATHER = 32
AHEAD = 1
PACK = 8


def params(mib):
    return pltpu.CompilerParams(vmem_limit_bytes=mib * 1024 * 1024)


def unrolled(count, most):
    return max(d for d in range(1, most + 1) if count % d == 0)


def rows_loop(count, most, fn):
    step = unrolled(count, most)

    def run(i, carry):
        for u in range(step):
            fn(i * step + u)
        return carry

    lax.fori_loop(0, count // step, run, 0)


def tiled(array):
    *lead, rows, cols = array.shape
    n = len(lead)
    split = array.reshape(*lead, rows // SUB, SUB, cols // LANES, LANES)
    return jnp.transpose(split, (*range(n), n, n + 2, n + 1, n + 3))


def untiled(array):
    *lead, r8, ct, sub, lanes = array.shape
    n = len(lead)
    back = jnp.transpose(array, (*range(n), n, n + 2, n + 1, n + 3))
    return back.reshape(*lead, r8 * sub, ct * lanes)


def pack_kernel(state, flow, nu, up, down, edge_flow, edge_nu, sems):
    members, fields, r8, nct = state.shape[:4]
    sides = ((up, r8 - 1, (SUB - 2, SUB - 1)), (down, 0, (0, 1)))
    copies = []

    def copy(src, dst):
        copies.append(pltpu.make_async_copy(src, dst, sems.at[len(copies)]))

    for side, (msg, block, rows) in enumerate(sides):
        copy(flow.at[:, block], edge_flow.at[side])
        copy(nu.at[:, block], edge_nu.at[side])
    for msg, block, rows in sides:
        for field in range(fields):
            for ct in range(nct):
                for at, row in enumerate(rows):
                    copy(
                        state.at[:, field, block, ct, row, :],
                        msg.at[ct, pl.ds((field * 2 + at) * members, members), :],
                    )
    for one in copies:
        one.start()
    for one in copies[:4]:
        one.wait()
    for side, (msg, block, rows) in enumerate(sides):
        edge = (SUB - 1, 0)[side]
        for ct in range(nct):
            numbers = [edge_flow[side, k, ct, edge : edge + 1, :] for k in range(2)]
            numbers += [edge_nu[side, k, ct, edge : edge + 1, :] for k in range(fields)]
            numbers.append(jnp.zeros((PACK - 2 - fields, LANES), F32))
            msg[ct, pl.ds(2 * fields * members, PACK), :] = jnp.concatenate(numbers, axis=0)
    for one in copies[4:]:
        one.wait()


def pack_edges(state6, flow5, nu5):
    members, fields, r8, nct = state6.shape[:4]
    msg = jax.ShapeDtypeStruct((nct, 2 * fields * members + PACK, LANES), F32)
    edge = pltpu.VMEM((2, 2, nct, SUB, LANES), F32)
    return pl.pallas_call(
        pack_kernel,
        out_shape=[msg] * 2,
        in_specs=[pl.BlockSpec(memory_space=pl.ANY)] * 3,
        out_specs=[pl.BlockSpec(memory_space=pltpu.VMEM)] * 2,
        scratch_shapes=[edge, edge, pltpu.SemaphoreType.DMA((4 + 4 * fields * nct,))],
        compiler_params=params(56),
        name="pack_edges",
    )(state6, flow5, nu5)


PAD = SUB


def stencil_coefs(flow_x, flow_y, nu, col, width):
    east = nu - jnp.minimum(flow_x, 0.0)
    west = nu + jnp.maximum(flow_x, 0.0)
    north = nu - jnp.minimum(flow_y, 0.0)
    south = nu + jnp.maximum(flow_y, 0.0)
    centre = 1.0 - (east + west + north + south)
    south = jnp.where(col == 0, 0.0, south)
    north = jnp.where(col == width - 1, 0.0, north)
    return centre, west, east, south, north


def fill_coefs(coef, field, flow, nu, blocks, before=None, after=None):
    _, r8, nct = flow.shape[:3]
    width = nct * LANES
    for ct in range(nct):
        for first, count in blocks:
            shape = (count * SUB, LANES)
            col = lax.broadcasted_iota(jnp.int32, shape, 1) + ct * LANES
            part = pl.ds(first, count)
            numbers = (flow[0, part, ct], flow[1, part, ct], nu[field, part, ct])
            numbers = [x.reshape(shape) for x in numbers]
            for k, value in enumerate(stencil_coefs(*numbers, col, width)):
                coef[k, ct, pl.ds(PAD + first * SUB, count * SUB), :] = value
        for msg, row in ((before, PAD - 1), (after, PAD + r8 * SUB)):
            if msg is not None:
                col = lax.broadcasted_iota(jnp.int32, (1, LANES), 1) + ct * LANES
                base = msg.shape[1] - PACK
                numbers = [msg[ct, pl.ds(base + k, 1), :] for k in (0, 1, 2 + field)]
                for k, value in enumerate(stencil_coefs(*numbers, col, width)):
                    coef[k, ct, pl.ds(row, 1), :] = value


def stencil(mid, west, east, weights):
    nct = len(mid)
    lane = lax.broadcasted_iota(jnp.int32, (SUB, LANES), 1)
    right = [pltpu.roll(x, 1, 1) for x in mid]
    left = [pltpu.roll(x, LANES - 1, 1) for x in mid]
    out = []
    for ct in range(nct):
        south = jnp.where(lane == 0, right[(ct - 1) % nct], right[ct])
        north = jnp.where(lane == LANES - 1, left[(ct + 1) % nct], left[ct])
        centre, w_w, w_e, w_s, w_n = weights[ct]
        out.append(
            (centre * mid[ct] + w_w * west[ct]) + (w_e * east[ct] + (w_s * south + w_n * north))
        )
    return out


class Rows:
    def __init__(self, held, coef):
        self.nct, _, blocks = held.shape[-5:-2]
        self.room = blocks * SUB
        self.flat = held.reshape(held.size // LANES, LANES)
        self.coef = coef.reshape(coef.size // LANES, LANES)

    def at(self, group, ct, row):
        start = (group * self.nct + ct) * SUB * self.room + PAD + row
        return pl.ds(start, SUB, stride=self.room)

    def load(self, group, row):
        return [self.flat[self.at(group, ct, row), :] for ct in range(self.nct)]

    def weights(self, row):
        return [
            [
                self.coef[pl.ds((k * self.nct + ct) * self.room + PAD + row, SUB, stride=0), :]
                for k in range(5)
            ]
            for ct in range(self.nct)
        ]


def group_steps(group, held, between, coef, put, edges):
    groups, nct, _, blocks = held.shape[:4]
    room = blocks * SUB
    source = held.reshape(groups, nct, SUB, room, LANES)
    middle = between.reshape(nct, SUB, room, LANES)

    def block_step(block, load, store):
        at = PAD + block * SUB
        weights = [[coef[k, ct, pl.ds(at, SUB), :] for k in range(5)] for ct in range(nct)]
        for m in range(SUB):
            mid, west, east = [
                [load(ct, m, pl.ds(at + off, SUB)) for ct in range(nct)] for off in (0, -1, 1)
            ]
            for ct, value in enumerate(stencil(mid, west, east, weights)):
                store(block, ct, m, value)

    def keep(block, ct, m, value):
        middle[ct, m, pl.ds(PAD + block * SUB, SUB), :] = value

    for block in range(blocks - 2):
        block_step(block, lambda ct, m, rows: source[group, ct, m, rows, :], keep)
    if edges:
        field, inner = Rows(held, coef), Rows(between, coef)
        for row in (-1, (blocks - 2) * SUB):
            around = [field.load(group, row + off) for off in (0, -1, 1)]
            for ct, value in enumerate(stencil(*around, field.weights(row))):
                inner.flat[inner.at(0, ct, row), :] = value
    for block in range(blocks - 2):
        block_step(block, lambda ct, m, rows: middle[ct, m, rows, :], put)


def held_shape(members, nct, r8):
    return (members // SUB, nct, SUB, r8 + 2, SUB, LANES)


def cost(cells):
    return pl.CostEstimate(flops=40 * cells, bytes_accessed=8 * cells, transcendentals=0)


SMEM = pl.BlockSpec(memory_space=pltpu.SMEM)
VMEM = pl.BlockSpec(memory_space=pltpu.VMEM)


def inner_kernel(state, flow, nu, full, held0, held1, between, coef, sems):
    groups, nct, _, blocks = held0.shape[:4]
    members = groups * SUB
    r8 = blocks - 2

    def copies(field, held, group):
        return [
            pltpu.make_async_copy(
                state.at[pl.ds(group * SUB, SUB), field, :, ct],
                held.at[group, ct, :, pl.ds(1, r8)],
                sems.at[field, group, ct],
            )
            for ct in range(nct)
        ]

    for group in range(groups):
        for one in copies(0, held0, group):
            one.start()
    fill_coefs(coef, 0, flow, nu, [(0, r8)])
    flat = full.reshape(full.size // LANES, LANES)

    def run(group, carry):
        for one in copies(0, held0, group):
            one.wait()
        for one in copies(1, held1, group):
            one.start()

        def put(block, ct, m, value):
            start = (block * SUB * nct + ct) * members + group * SUB + m
            flat[pl.ds(start, SUB, stride=nct * members), :] = value

        group_steps(group, held0, between, coef, put, False)
        return carry

    lax.fori_loop(0, groups, run, 0)
    for group in range(groups):
        for one in copies(1, held1, group):
            one.wait()


def forecast_inner(state6, flow5, nu5):
    members, _, r8, nct = state6.shape[:4]
    held = held_shape(members, nct, r8)
    return pl.pallas_call(
        inner_kernel,
        out_shape=[
            jax.ShapeDtypeStruct((r8 * SUB, nct, members, LANES), F32),
            jax.ShapeDtypeStruct(held, F32),
            jax.ShapeDtypeStruct(held, F32),
        ],
        in_specs=[pl.BlockSpec(memory_space=pl.ANY)] + [VMEM] * 2,
        out_specs=[VMEM] * 3,
        scratch_shapes=[
            pltpu.VMEM(held[1:], F32),
            pltpu.VMEM((5, nct, (r8 + 2) * SUB, LANES), F32),
            pltpu.SemaphoreType.DMA((2, held[0], nct)),
        ],
        compiler_params=params(34),
        cost_estimate=cost(members * r8 * SUB * nct * LANES),
        name="forecast_inner",
    )(state6, flow5, nu5)


def edge_kernel(
    ids, cells, owner, order, flow, nu, before, after, full_in, held0_in, held1_in,
    full, held0, held1, keep, away, coef
):
    groups, nct, _, blocks = held0.shape[:4]
    members = groups * SUB
    r8 = blocks - 2
    rows = r8 * SUB
    slab, member = ids[0], ids[1]

    for field, held in ((0, held0), (1, held1)):
        view = Rows(held, coef)
        for ct in range(nct):
            for group in range(groups):
                for k in range(2):
                    part = pl.ds((2 * field + k) * members + group * SUB, SUB)
                    view.flat[view.at(group, ct, k - 2), :] = before[ct, part, :]
                    view.flat[view.at(group, ct, rows + k), :] = after[ct, part, :]

    fill_coefs(coef, 0, flow, nu, [(0, 1), (r8 - 1, 1)], before, after)
    view = Rows(held0, coef)
    for first in (0, rows - 2):
        for group in range(groups):
            old = {r: view.load(group, r) for r in range(first - 2, first + 4)}
            one = {
                r: stencil(old[r], old[r - 1], old[r + 1], view.weights(r))
                for r in range(first - 1, first + 3)
            }
            for r in range(first, first + 2):
                new = stencil(one[r], one[r - 1], one[r + 1], view.weights(r))
                for ct, value in enumerate(new):
                    full[r, ct, pl.ds(group * SUB, SUB), :] = value

    nobs = cells.shape[1]
    tiles = full.reshape(rows * nct, members, LANES)
    lane = lax.broadcasted_iota(jnp.int32, (members, LANES), 1)
    for position in range(order.shape[0]):
        batch = order[position]
        mine = owner[batch] == slab
        kept = lax.rem(position, 2) == member

        def pick(tile, carry, batch=batch, mine=mine, kept=kept, position=position):
            def some(group, acc):
                for u in range(GATHER):
                    o = group * GATHER + u
                    cell = cells[batch, tile * LANES + o]
                    tile_at = lax.shift_right_logical(cell, LANES.bit_length() - 1)
                    moved = pltpu.roll(tiles[tile_at], (o - cell) & (LANES - 1), 1)
                    acc = jnp.where(lane == o, moved, acc)
                return acc

            acc = lax.fori_loop(
                0, jnp.where(mine, LANES // GATHER, 0), some, jnp.zeros((members, LANES), F32)
            )

            @pl.when(kept)
            def _():
                keep[position // 2, tile] = acc

            @pl.when(jnp.logical_not(kept))
            def _():
                away[position // 2, tile] = acc

            return carry

        lax.fori_loop(0, nobs // LANES, pick, 0)


def forecast_edges(ids, cells, owner, order, flow5, nu5, before, after, full, held0, held1):
    members = full.shape[2]
    nct, _, blocks = held0.shape[1:4]
    nb, nobs = cells.shape
    picks = jax.ShapeDtypeStruct((nb // 2, nobs // LANES, members, LANES), F32)
    same = [jax.ShapeDtypeStruct(x.shape, F32) for x in (full, held0, held1)]
    return pl.pallas_call(
        edge_kernel,
        out_shape=[*same, picks, picks],
        in_specs=[SMEM] * 4 + [VMEM] * 7,
        out_specs=[VMEM] * 5,
        input_output_aliases={8: 0, 9: 1, 10: 2},
        scratch_shapes=[pltpu.VMEM((5, nct, blocks * SUB, LANES), F32)],
        compiler_params=params(6),
        cost_estimate=cost(members * SUB * nct * LANES),
        name="forecast_edges",
    )(ids, cells, owner, order, flow5, nu5, before, after, full, held0, held1)


def piece_kernel(group, flow, nu, before, after, held, *rest):
    full, between, coef = rest[-3:]
    rows, nct, members = full.shape[:3]
    flat = full.reshape(full.size // LANES, LANES)
    fill_coefs(coef, 1, flow, nu, [(0, rows // SUB)], before, after)

    def put(block, ct, m, value):
        start = (block * SUB * nct + ct) * members + group * SUB + m
        flat[pl.ds(start, SUB, stride=nct * members), :] = value

    group_steps(group, held, between, coef, put, True)


def forecast_piece(group, flow5, nu5, before, after, held, done):
    groups, nct, _, blocks = held.shape[:4]
    rows = (blocks - 2) * SUB
    return pl.pallas_call(
        functools.partial(piece_kernel, group),
        out_shape=jax.ShapeDtypeStruct((rows, nct, groups * SUB, LANES), F32),
        in_specs=[VMEM] * (5 + len(done)),
        out_specs=VMEM,
        input_output_aliases={5: 0} if done else {},
        scratch_shapes=[
            pltpu.VMEM(held.shape[1:], F32),
            pltpu.VMEM((5, nct, blocks * SUB, LANES), F32),
        ],
        compiler_params=params(6),
        cost_estimate=cost(SUB * rows * nct * LANES),
        name=f"forecast_members_{group}",
    )(flow5, nu5, before, after, held, *done)


def gram_kernel(ids, owner, order, keep, other, observed, variance, *outs):
    slab, member = ids[0], ids[1]
    count, tiles, members = keep.shape[:3]
    for k in range(count):
        batch = order[2 * k + member]
        mine = owner[batch] == slab
        part = count // len(outs)
        out = outs[k // part].at[k % part]

        @pl.when(jnp.logical_not(mine))
        def _():
            out[...] = jnp.zeros(out.shape, F32)

        @pl.when(mine)
        def _():
            pair = jnp.zeros(out.shape, F32)
            for t in range(tiles):
                a, b = keep[k, t], other[k, t]
                prior = jnp.concatenate(
                    [jnp.where(member == 0, a, b), jnp.where(member == 0, b, a)], axis=0
                )
                mean = jnp.sum(prior, axis=0, keepdims=True) / (2 * members)
                anomaly = prior - mean
                scaled = anomaly / variance[batch, :, pl.ds(t * LANES, LANES)]
                misfit = observed[batch, :, pl.ds(t * LANES, LANES)] - mean
                pair += lax.dot_general(
                    scaled,
                    jnp.concatenate([anomaly, misfit], axis=0),
                    (((1,), (1,)), ((), ())),
                    precision=HIGH,
                    preferred_element_type=F32,
                )
            h = lax.dot_general(
                pair[:, 2 * members :], rotation(2 * members), (((1,), (0,)), ((), ())),
                precision=HIGH, preferred_element_type=F32,
            )
            out[...] = jnp.concatenate([pair[:, : 2 * members], h], axis=1)


def gram(ids, owner, order, keep, other, observed, variance):
    count, _, members, _ = keep.shape
    total = 2 * members
    smem = pl.BlockSpec(memory_space=pltpu.SMEM)
    vmem = pl.BlockSpec(memory_space=pltpu.VMEM)
    return pl.pallas_call(
        gram_kernel,
        out_shape=[jax.ShapeDtypeStruct((count // 2, total, 2 * total), F32)] * 2,
        in_specs=[smem] * 3 + [vmem] * 4,
        out_specs=[vmem] * 2,
        compiler_params=params(12),
        name="gram",
    )(ids, owner, order, keep, other, observed, variance[:, None, :])


def rotation(size):
    step = size**-0.5
    row = lax.broadcasted_iota(jnp.int32, (size, size), 0)
    col = lax.broadcasted_iota(jnp.int32, (size, size), 1)
    v_row = (row == size - 1).astype(F32) - step
    v_col = (col == size - 1).astype(F32) - step
    return (row == col).astype(F32) - v_row * v_col / (1.0 - step)


def split3(x):
    high = x.astype(BF16)
    rest = x - high.astype(F32)
    mid = rest.astype(BF16)
    return high, mid, (rest - mid.astype(F32)).astype(BF16)


def dot32(x, y, lhs, rhs):
    parts = split3(x)
    m = x.shape[1 - lhs]
    out = None
    for k, right in enumerate(split3(y)):
        left = jnp.concatenate(parts[: 3 - k], axis=1 - lhs)
        each = lax.dot_general(
            left, right, (((lhs,), (rhs,)), ((), ())), preferred_element_type=F32
        )
        for j in reversed(range(3 - k)):
            piece = each[j * m : (j + 1) * m]
            out = piece if out is None else out + piece
    return out


def total(terms):
    while len(terms) > 1:
        terms = [x + y for x, y in zip(terms[::2], terms[1::2])]
    return terms[0]


def eliminate(a_ref, b_ref, scaled, rows_a, rows_b):
    groups = a_ref.shape[0] // SUB
    wide = (SUB, LANES)
    sub = lax.broadcasted_iota(jnp.int32, wide, 0)
    part = [pl.ds(g * SUB, SUB) for g in range(groups)]

    def column(x, k):
        return jnp.broadcast_to(x[:, k : k + 1], wide)

    def row(x, k):
        return jnp.broadcast_to(x[k : k + 1, :], wide)

    def less(x, scale, first, second, n):
        return x - scale * (first * n[0] + second * n[1])

    a_next, b_next = a_ref[part[0], :], b_ref[part[0], :]
    c = [column(a_next, k) for k in range(SUB)]
    kk, kl, ll = row(c[0], 0), row(c[1], 0), row(c[1], 1)
    for p in range(groups):
        c = [(x, x) for x in c]
        pa, pb = (a_next, a_next), (b_next, b_next)
        after = p + 1 if p + 1 < groups else None
        if after:
            a_next, b_next = a_ref[part[after], :], b_ref[part[after], :]
            e = [column(a_next, p * SUB + k) for k in range(SUB)]
        ahead = None
        for k in range(0, SUB, 2):
            (fk, ck), (fl, cl) = c[k], c[k + 1]
            scale = pl.reciprocal(kk * ll - kl * kl, approx=True)

            def pivot_rows(x, k=k, kk=kk, kl=kl, ll=ll):
                u, w = row(x, k), row(x, k + 1)
                return ll * u - kl * w, kk * w - kl * u

            def inside(x, n, k=k, ck=ck, cl=cl, scale=scale):
                rest = less(x[1], scale, ck, cl, n)
                done = jnp.where(
                    sub == k, scale * n[0], jnp.where(sub == k + 1, scale * n[1], rest)
                )
                return rest, done

            n = {j: pivot_rows(c[j][0]) for j in range(k + 2, SUB)}
            if k + 2 < SUB:
                here = (k + 2, k + 3)
                left, right = ([row(x, i) for i in here] for x in (fk, fl))
                first, second = c[k + 2][0], c[k + 3][0]
                blocks = (
                    less(row(first, k + 2), scale, left[0], right[0], n[k + 2]),
                    less(row(second, k + 2), scale, left[0], right[0], n[k + 3]),
                    less(row(second, k + 3), scale, left[1], right[1], n[k + 3]),
                )
            if ahead:
                upper, lower = ahead
                m = [pivot_rows(x) for x in upper]
                if k + 2 == SUB:
                    left, right = ([row(x, i) for i in (0, 1)] for x in (e[k], e[k + 1]))
                    blocks = (
                        less(row(lower[0], 0), scale, left[0], right[0], m[0]),
                        less(row(lower[1], 0), scale, left[0], right[0], m[1]),
                        less(row(lower[1], 1), scale, left[1], right[1], m[1]),
                    )
                upper = [less(x, scale, fk, fl, y) for x, y in zip(upper, m)]
                lower = [less(x, scale, e[k], e[k + 1], y) for x, y in zip(lower, m)]
                ahead = upper, lower
            for j in range(k + 2, SUB):
                c[j] = inside(c[j], n[j])
                if after:
                    e[j] = less(e[j], scale, e[k], e[k + 1], n[j])
            if after:
                m = pivot_rows(pa[0])
                pa = inside(pa, m)
                a_next = less(a_next, scale, e[k], e[k + 1], m)
            m = pivot_rows(pb[0])
            pb = inside(pb, m)
            if after:
                b_next = less(b_next, scale, e[k], e[k + 1], m)
                if k + 2 == SUB - 2 * AHEAD:
                    ahead = [
                        [column(x, (p + 1) * SUB + j) for j in range(SUB)] for x in (pa[0], a_next)
                    ]
            kk, kl, ll = blocks
        pa, pb = pa[1], pb[1]
        scaled[part[p], :] = pb
        if after:
            c = ahead[1]
            b_ref[part[after], :] = b_next
        if p + 2 < groups:
            here = p % 2
            rows_a[here] = pa
            rows_b[here] = pb
            ra = [rows_a[here, pl.ds(k, SUB, stride=0), :] for k in range(SUB)]
            rb = [rows_b[here, pl.ds(k, SUB, stride=0), :] for k in range(SUB)]
            for g in range(p + 2, groups):
                old = a_ref[part[g], :]
                cols = [column(old, p * SUB + k) for k in range(SUB)]
                a_ref[part[g], :] = old - total([x * y for x, y in zip(cols, ra)])
                b_ref[part[g], :] = b_ref[part[g], :] - total([x * y for x, y in zip(cols, rb)])


def chain_kernel(ids, mine0, mine1, other0, other1, out, a, b, scaled, rows_a, rows_b):
    member = ids[1]
    count, size, width = mine0.shape
    row = lax.broadcasted_iota(jnp.int32, (size, width), 0)
    lane = lax.broadcasted_iota(jnp.int32, (size, width), 1)
    diagonal = jnp.where(row == lane, size - 1.0, 0.0)

    def step(position, vt):
        k = lax.rem(lax.div(position, 2), count)
        early = position < 2 * count
        gh = jnp.where(
            lax.rem(position, 2) == member,
            jnp.where(early, mine0[k], mine1[k]),
            jnp.where(early, other0[k], other1[k]),
        )
        zt = jnp.where(row == size - 1, 0.0, vt)
        s = dot32(zt[:, :size], gh, 1, 0)
        v = vt[:, :size]
        t = dot32(s[:, :size], jnp.concatenate([v, v], axis=0), 1, 1)
        a[...] = jnp.where(lane == size - 1, 0.0, t) + diagonal
        b[...] = jnp.where(lane < size, zt, s - t)
        eliminate(a, b, scaled, rows_a, rows_b)
        return vt + dot32(b[...], scaled[...], 0, 0)[size:]

    unit = rotation(size)
    start = jnp.concatenate([unit, jnp.zeros_like(unit)], axis=1)
    vt = lax.fori_loop(0, 4 * count, step, start)
    w = dot32(unit, vt[:, :size], 1, 0)
    half = size // 2
    first, second = w[:, :half], w[:, half:]
    w = jnp.concatenate(
        [jnp.where(member == 0, first, second), jnp.where(member == 0, second, first)], axis=1
    )
    high = w.astype(BF16).astype(F32)
    low = w - high
    out[...] = jnp.concatenate(
        [jnp.concatenate([high, high], axis=1), jnp.concatenate([low, jnp.zeros_like(low)], axis=1)],
        axis=0,
    )


def chain(ids, *pairs):
    size = pairs[0].shape[1]
    rows = pltpu.VMEM((2, SUB, LANES), F32)
    square = pltpu.VMEM((size, 2 * size), F32)
    return pl.pallas_call(
        chain_kernel,
        out_shape=jax.ShapeDtypeStruct((2 * size, 2 * size), F32),
        in_specs=[SMEM] + [VMEM] * len(pairs),
        out_specs=VMEM,
        scratch_shapes=[square, square, square, rows, rows],
        compiler_params=params(12),
        name="chain",
    )(ids, *pairs)


def apply_kernel(ids, w_ref, own0, other0, own1, other1, out, held, sems):
    size = w_ref.shape[0] // 2
    rows, nct = own0.shape[:2]
    half = nct // 2
    first_tile = ids[1] * half
    weights = w_ref[...].astype(BF16)
    flat = held.reshape(held.size // LANES, LANES)

    for field, sources in enumerate(((own0, other0), (own1, other1))):

        def copy(block, slot, field=field):
            return pltpu.make_async_copy(held.at[slot], out.at[:, field, block], sems.at[slot])

        def step(block, carry, field=field, sources=sources, copy=copy):
            slot = lax.rem(block, 2)

            @pl.when((block >= 2) if field == 0 else (block >= 0))
            def _():
                copy(block, slot).wait()

            base = slot * size * half * SUB
            for r in range(SUB):
                parts = [
                    jnp.concatenate(
                        [src[block * SUB + r, first_tile + ct] for ct in range(half)], axis=1
                    )
                    for src in sources
                ]
                high = [x.astype(BF16) for x in parts]
                low = [(x - y.astype(F32)).astype(BF16) for x, y in zip(parts, high)]
                stacked = jnp.concatenate([*high, *low], axis=0)
                result = jnp.dot(weights, stacked, preferred_element_type=F32)
                result = result[:size] + result[size:]
                for ct in range(half):
                    flat[pl.ds(base + ct * SUB + r, size, stride=half * SUB), :] = result[
                        :, ct * LANES : (ct + 1) * LANES
                    ]
            copy(block, slot).start()
            return carry

        lax.fori_loop(0, rows // SUB, step, 0)
    for slot in range(2):
        copy(0, slot).wait()


def apply(ids, weights, own0, other0, own1, other1):
    rows, nct, members, _ = own0.shape
    size = 2 * members
    half = nct // 2
    r8 = rows // SUB
    return pl.pallas_call(
        apply_kernel,
        out_shape=jax.ShapeDtypeStruct((size, 2, r8, half, SUB, LANES), F32),
        in_specs=[SMEM] + [VMEM] * 5,
        out_specs=pl.BlockSpec(memory_space=pl.ANY),
        scratch_shapes=[
            pltpu.VMEM((2, size, half, SUB, LANES), F32),
            pltpu.SemaphoreType.DMA((2,)),
        ],
        compiler_params=params(12),
        name="apply",
    )(ids, weights, own0, other0, own1, other1)


def body(state, courant, diffusion, obs_cells, obs_owner, batch_order, obs_values, obs_error):
    slab = lax.axis_index("space")
    member = lax.axis_index("member")
    space = lax.axis_size("space")
    ids = jnp.stack([slab, member]).astype(jnp.int32)
    up = [(i, i + 1) for i in range(space - 1)]
    down = [(i + 1, i) for i in range(space - 1)]
    swap = [(0, 1), (1, 0)]

    state6, flow5, nu5 = tiled(state), tiled(courant), tiled(diffusion)
    up_edge, down_edge = pack_edges(state6, flow5, nu5)
    before = lax.ppermute(up_edge, "space", up)
    after = lax.ppermute(down_edge, "space", down)
    full0, held0, held1 = forecast_inner(state6, flow5, nu5)
    full0, _, held1, keep, away = forecast_edges(
        ids, obs_cells, obs_owner, batch_order, flow5, nu5, before, after, full0, held0, held1
    )
    other = lax.ppermute(away, "member", swap)
    halves = gram(ids, obs_owner, batch_order, keep, other, obs_values, obs_error)

    groups = list(range(held1.shape[0]))
    field1 = ()
    bits = [1 << i for i in range(space.bit_length() - 1)]
    turned = bits[len(bits) // 2 :] + bits[: len(bits) // 2]
    for pair in zip(bits, turned):
        received = [
            lax.ppermute(half, "space", [(i, i ^ bit) for i in range(space)])
            for half, bit in zip(halves, pair)
        ]
        if groups:
            held1, halves = lax.optimization_barrier((held1, halves))
            field1 = forecast_piece(groups.pop(0), flow5, nu5, before, after, held1, field1)
            received, field1 = lax.optimization_barrier((received, (field1,)))
        halves = [half + more for half, more in zip(halves, received)]
    for group in groups:
        field1 = (forecast_piece(group, flow5, nu5, before, after, held1, field1),)
    (full1,) = field1
    theirs = [lax.ppermute(half, "member", swap) for half in halves]
    full0, full1, halves, theirs = lax.optimization_barrier((full0, full1, halves, theirs))
    other0 = lax.ppermute(full0, "member", swap)
    other1 = lax.ppermute(full1, "member", swap)
    weights = chain(ids, *halves, *theirs)
    return untiled(apply(ids, weights, full0, other0, full1, other1))


def solution(mesh):
    placed = (
        P("member", None, "space", None),
        P(None, "space", None),
        P(None, "space", None),
        P(),
        P(),
        P(),
        P(),
        P(),
    )
    return jax.shard_map(
        body,
        mesh=mesh,
        in_specs=placed,
        out_specs=P(None, None, "space", "member"),
        check_vma=False,
    )
```

```python
import functools

import jax
import jax.numpy as jnp
from jax import lax
from jax.experimental import pallas as pl
from jax.experimental.pallas import tpu as pltpu
from jax.sharding import PartitionSpec as P

HIGH = lax.Precision.HIGHEST
F32 = jnp.float32
BF16 = jnp.bfloat16
LANES = 128
SUB = 8
GATHER = 32
AHEAD = 1
PACK = 8


def params(mib):
    return pltpu.CompilerParams(vmem_limit_bytes=mib * 1024 * 1024)


def unrolled(count, most):
    return max(d for d in range(1, most + 1) if count % d == 0)


def rows_loop(count, most, fn):
    step = unrolled(count, most)

    def run(i, carry):
        for u in range(step):
            fn(i * step + u)
        return carry

    lax.fori_loop(0, count // step, run, 0)


def tiled(array):
    *lead, rows, cols = array.shape
    n = len(lead)
    split = array.reshape(*lead, rows // SUB, SUB, cols // LANES, LANES)
    return jnp.transpose(split, (*range(n), n, n + 2, n + 1, n + 3))


def untiled(array):
    *lead, r8, ct, sub, lanes = array.shape
    n = len(lead)
    back = jnp.transpose(array, (*range(n), n, n + 2, n + 1, n + 3))
    return back.reshape(*lead, r8 * sub, ct * lanes)


def pack_kernel(state, flow, nu, first, second, edge_flow, edge_nu, sems):
    members, fields, r8, nct = state.shape[:4]
    even = lax.rem(lax.axis_index("space"), 2) == 0

    def pack(above, below):
        sides = ((above, r8 - 1, (SUB - 2, SUB - 1)), (below, 0, (0, 1)))
        copies = []

        def copy(src, dst):
            copies.append(pltpu.make_async_copy(src, dst, sems.at[len(copies)]))

        for side, (msg, block, rows) in enumerate(sides):
            copy(flow.at[:, block], edge_flow.at[side])
            copy(nu.at[:, block], edge_nu.at[side])
        for msg, block, rows in sides:
            for field in range(fields):
                for ct in range(nct):
                    for at, row in enumerate(rows):
                        copy(
                            state.at[:, field, block, ct, row, :],
                            msg.at[ct, pl.ds((field * 2 + at) * members, members), :],
                        )
        for one in copies:
            one.start()
        for one in copies[:4]:
            one.wait()
        for side, (msg, block, rows) in enumerate(sides):
            edge = (SUB - 1, 0)[side]
            for ct in range(nct):
                numbers = [edge_flow[side, k, ct, edge : edge + 1, :] for k in range(2)]
                numbers += [edge_nu[side, k, ct, edge : edge + 1, :] for k in range(fields)]
                numbers.append(jnp.zeros((PACK - 2 - fields, LANES), F32))
                msg[ct, pl.ds(2 * fields * members, PACK), :] = jnp.concatenate(numbers, axis=0)
        for one in copies[4:]:
            one.wait()

    @pl.when(even)
    def _():
        pack(first, second)

    @pl.when(jnp.logical_not(even))
    def _():
        pack(second, first)


class Chosen:
    def __init__(self, flag, yes, no):
        self.flag, self.yes, self.no, self.shape = flag, yes, no, yes.shape

    def __getitem__(self, at):
        return jnp.where(self.flag, self.yes[at], self.no[at])


def neighbours(slab, first, second):
    even = lax.rem(slab, 2) == 0
    return Chosen(even, second, first), Chosen(even, first, second)


def pack_edges(state6, flow5, nu5):
    members, fields, r8, nct = state6.shape[:4]
    msg = jax.ShapeDtypeStruct((nct, 2 * fields * members + PACK, LANES), F32)
    edge = pltpu.VMEM((2, 2, nct, SUB, LANES), F32)
    return pl.pallas_call(
        pack_kernel,
        out_shape=[msg] * 2,
        in_specs=[pl.BlockSpec(memory_space=pl.ANY)] * 3,
        out_specs=[pl.BlockSpec(memory_space=pltpu.VMEM)] * 2,
        scratch_shapes=[edge, edge, pltpu.SemaphoreType.DMA((4 + 4 * fields * nct,))],
        compiler_params=params(56),
        name="pack_edges",
    )(state6, flow5, nu5)


PAD = SUB


def stencil_coefs(flow_x, flow_y, nu, col, width):
    east = nu - jnp.minimum(flow_x, 0.0)
    west = nu + jnp.maximum(flow_x, 0.0)
    north = nu - jnp.minimum(flow_y, 0.0)
    south = nu + jnp.maximum(flow_y, 0.0)
    centre = 1.0 - (east + west + north + south)
    south = jnp.where(col == 0, 0.0, south)
    north = jnp.where(col == width - 1, 0.0, north)
    return centre, west, east, south, north


def fill_coefs(coef, field, flow, nu, blocks, before=None, after=None):
    _, r8, nct = flow.shape[:3]
    width = nct * LANES
    for ct in range(nct):
        for first, count in blocks:
            shape = (count * SUB, LANES)
            col = lax.broadcasted_iota(jnp.int32, shape, 1) + ct * LANES
            part = pl.ds(first, count)
            numbers = (flow[0, part, ct], flow[1, part, ct], nu[field, part, ct])
            numbers = [x.reshape(shape) for x in numbers]
            for k, value in enumerate(stencil_coefs(*numbers, col, width)):
                coef[k, ct, pl.ds(PAD + first * SUB, count * SUB), :] = value
        for msg, row in ((before, PAD - 1), (after, PAD + r8 * SUB)):
            if msg is not None:
                col = lax.broadcasted_iota(jnp.int32, (1, LANES), 1) + ct * LANES
                base = msg.shape[1] - PACK
                numbers = [msg[ct, pl.ds(base + k, 1), :] for k in (0, 1, 2 + field)]
                for k, value in enumerate(stencil_coefs(*numbers, col, width)):
                    coef[k, ct, pl.ds(row, 1), :] = value


def stencil(mid, west, east, weights):
    nct = len(mid)
    lane = lax.broadcasted_iota(jnp.int32, (SUB, LANES), 1)
    right = [pltpu.roll(x, 1, 1) for x in mid]
    left = [pltpu.roll(x, LANES - 1, 1) for x in mid]
    out = []
    for ct in range(nct):
        south = jnp.where(lane == 0, right[(ct - 1) % nct], right[ct])
        north = jnp.where(lane == LANES - 1, left[(ct + 1) % nct], left[ct])
        centre, w_w, w_e, w_s, w_n = weights[ct]
        out.append(
            (centre * mid[ct] + w_w * west[ct]) + (w_e * east[ct] + (w_s * south + w_n * north))
        )
    return out


class Rows:
    def __init__(self, held, coef):
        self.nct, _, blocks = held.shape[-5:-2]
        self.room = blocks * SUB
        self.flat = held.reshape(held.size // LANES, LANES)
        self.coef = coef.reshape(coef.size // LANES, LANES)

    def at(self, group, ct, row):
        start = (group * self.nct + ct) * SUB * self.room + PAD + row
        return pl.ds(start, SUB, stride=self.room)

    def load(self, group, row):
        return [self.flat[self.at(group, ct, row), :] for ct in range(self.nct)]

    def weights(self, row):
        return [
            [
                self.coef[pl.ds((k * self.nct + ct) * self.room + PAD + row, SUB, stride=0), :]
                for k in range(5)
            ]
            for ct in range(self.nct)
        ]


def group_steps(group, held, between, coef, put, edges):
    groups, nct, _, blocks = held.shape[:4]
    room = blocks * SUB
    source = held.reshape(groups, nct, SUB, room, LANES)
    middle = between.reshape(nct, SUB, room, LANES)

    def block_step(block, load, store):
        at = PAD + block * SUB
        weights = [[coef[k, ct, pl.ds(at, SUB), :] for k in range(5)] for ct in range(nct)]
        for m in range(SUB):
            mid, west, east = [
                [load(ct, m, pl.ds(at + off, SUB)) for ct in range(nct)] for off in (0, -1, 1)
            ]
            for ct, value in enumerate(stencil(mid, west, east, weights)):
                store(block, ct, m, value)

    def keep(block, ct, m, value):
        middle[ct, m, pl.ds(PAD + block * SUB, SUB), :] = value

    for block in range(blocks - 2):
        block_step(block, lambda ct, m, rows: source[group, ct, m, rows, :], keep)
    if edges:
        field, inner = Rows(held, coef), Rows(between, coef)
        for row in (-1, (blocks - 2) * SUB):
            around = [field.load(group, row + off) for off in (0, -1, 1)]
            for ct, value in enumerate(stencil(*around, field.weights(row))):
                inner.flat[inner.at(0, ct, row), :] = value
    for block in range(blocks - 2):
        block_step(block, lambda ct, m, rows: middle[ct, m, rows, :], put)


def held_shape(members, nct, r8):
    return (members // SUB, nct, SUB, r8 + 2, SUB, LANES)


def cost(cells):
    return pl.CostEstimate(flops=40 * cells, bytes_accessed=8 * cells, transcendentals=0)


SMEM = pl.BlockSpec(memory_space=pltpu.SMEM)
VMEM = pl.BlockSpec(memory_space=pltpu.VMEM)


def inner_kernel(state, flow, nu, full, held0, held1, between, coef, sems):
    groups, nct, _, blocks = held0.shape[:4]
    members = groups * SUB
    r8 = blocks - 2

    def copies(field, held, group):
        return [
            pltpu.make_async_copy(
                state.at[pl.ds(group * SUB, SUB), field, :, ct],
                held.at[group, ct, :, pl.ds(1, r8)],
                sems.at[field, group, ct],
            )
            for ct in range(nct)
        ]

    for group in range(groups):
        for one in copies(0, held0, group):
            one.start()
    fill_coefs(coef, 0, flow, nu, [(0, r8)])
    flat = full.reshape(full.size // LANES, LANES)

    def run(group, carry):
        for one in copies(0, held0, group):
            one.wait()
        for one in copies(1, held1, group):
            one.start()

        def put(block, ct, m, value):
            start = (block * SUB * nct + ct) * members + group * SUB + m
            flat[pl.ds(start, SUB, stride=nct * members), :] = value

        group_steps(group, held0, between, coef, put, False)
        return carry

    lax.fori_loop(0, groups, run, 0)
    for group in range(groups):
        for one in copies(1, held1, group):
            one.wait()


def forecast_inner(state6, flow5, nu5):
    members, _, r8, nct = state6.shape[:4]
    held = held_shape(members, nct, r8)
    return pl.pallas_call(
        inner_kernel,
        out_shape=[
            jax.ShapeDtypeStruct((r8 * SUB, nct, members, LANES), F32),
            jax.ShapeDtypeStruct(held, F32),
            jax.ShapeDtypeStruct(held, F32),
        ],
        in_specs=[pl.BlockSpec(memory_space=pl.ANY)] + [VMEM] * 2,
        out_specs=[VMEM] * 3,
        scratch_shapes=[
            pltpu.VMEM(held[1:], F32),
            pltpu.VMEM((5, nct, (r8 + 2) * SUB, LANES), F32),
            pltpu.SemaphoreType.DMA((2, held[0], nct)),
        ],
        compiler_params=params(34),
        cost_estimate=cost(members * r8 * SUB * nct * LANES),
        name="forecast_inner",
    )(state6, flow5, nu5)


def edge_kernel(
    ids, cells, owner, order, flow, nu, before, after, full_in, held0_in, held1_in,
    full, held0, held1, keep, away, coef
):
    groups, nct, _, blocks = held0.shape[:4]
    members = groups * SUB
    r8 = blocks - 2
    rows = r8 * SUB
    slab, member = ids[0], ids[1]
    before, after = neighbours(slab, before, after)

    for field, held in ((0, held0), (1, held1)):
        view = Rows(held, coef)
        for ct in range(nct):
            for group in range(groups):
                for k in range(2):
                    part = pl.ds((2 * field + k) * members + group * SUB, SUB)
                    view.flat[view.at(group, ct, k - 2), :] = before[ct, part, :]
                    view.flat[view.at(group, ct, rows + k), :] = after[ct, part, :]

    fill_coefs(coef, 0, flow, nu, [(0, 1), (r8 - 1, 1)], before, after)
    view = Rows(held0, coef)
    for first in (0, rows - 2):
        for group in range(groups):
            old = {r: view.load(group, r) for r in range(first - 2, first + 4)}
            one = {
                r: stencil(old[r], old[r - 1], old[r + 1], view.weights(r))
                for r in range(first - 1, first + 3)
            }
            for r in range(first, first + 2):
                new = stencil(one[r], one[r - 1], one[r + 1], view.weights(r))
                for ct, value in enumerate(new):
                    full[r, ct, pl.ds(group * SUB, SUB), :] = value

    nobs = cells.shape[1]
    tiles = full.reshape(rows * nct, members, LANES)
    lane = lax.broadcasted_iota(jnp.int32, (members, LANES), 1)
    for position in range(order.shape[0]):
        batch = order[position]
        mine = owner[batch] == slab
        kept = lax.rem(position, 2) == member

        def pick(tile, carry, batch=batch, mine=mine, kept=kept, position=position):
            def some(group, acc):
                for u in range(GATHER):
                    o = group * GATHER + u
                    cell = cells[batch, tile * LANES + o]
                    tile_at = lax.shift_right_logical(cell, LANES.bit_length() - 1)
                    moved = pltpu.roll(tiles[tile_at], (o - cell) & (LANES - 1), 1)
                    acc = jnp.where(lane == o, moved, acc)
                return acc

            acc = lax.fori_loop(
                0, jnp.where(mine, LANES // GATHER, 0), some, jnp.zeros((members, LANES), F32)
            )

            @pl.when(kept)
            def _():
                keep[position // 2, tile] = acc

            @pl.when(jnp.logical_not(kept))
            def _():
                away[position // 2, tile] = acc

            return carry

        lax.fori_loop(0, nobs // LANES, pick, 0)


def forecast_edges(ids, cells, owner, order, flow5, nu5, before, after, full, held0, held1):
    members = full.shape[2]
    nct, _, blocks = held0.shape[1:4]
    nb, nobs = cells.shape
    picks = jax.ShapeDtypeStruct((nb // 2, nobs // LANES, members, LANES), F32)
    same = [jax.ShapeDtypeStruct(x.shape, F32) for x in (full, held0, held1)]
    return pl.pallas_call(
        edge_kernel,
        out_shape=[*same, picks, picks],
        in_specs=[SMEM] * 4 + [VMEM] * 7,
        out_specs=[VMEM] * 5,
        input_output_aliases={8: 0, 9: 1, 10: 2},
        scratch_shapes=[pltpu.VMEM((5, nct, blocks * SUB, LANES), F32)],
        compiler_params=params(6),
        cost_estimate=cost(members * SUB * nct * LANES),
        name="forecast_edges",
    )(ids, cells, owner, order, flow5, nu5, before, after, full, held0, held1)


def piece_kernel(group, ids, flow, nu, first, second, held, *rest):
    full, between, coef = rest[-3:]
    rows, nct, members = full.shape[:3]
    flat = full.reshape(full.size // LANES, LANES)
    before, after = neighbours(ids[0], first, second)
    fill_coefs(coef, 1, flow, nu, [(0, rows // SUB)], before, after)

    def put(block, ct, m, value):
        start = (block * SUB * nct + ct) * members + group * SUB + m
        flat[pl.ds(start, SUB, stride=nct * members), :] = value

    group_steps(group, held, between, coef, put, True)


def forecast_piece(group, ids, flow5, nu5, before, after, held, done):
    groups, nct, _, blocks = held.shape[:4]
    rows = (blocks - 2) * SUB
    return pl.pallas_call(
        functools.partial(piece_kernel, group),
        out_shape=jax.ShapeDtypeStruct((rows, nct, groups * SUB, LANES), F32),
        in_specs=[SMEM] + [VMEM] * (5 + len(done)),
        out_specs=VMEM,
        input_output_aliases={6: 0} if done else {},
        scratch_shapes=[
            pltpu.VMEM(held.shape[1:], F32),
            pltpu.VMEM((5, nct, blocks * SUB, LANES), F32),
        ],
        compiler_params=params(6),
        cost_estimate=cost(SUB * rows * nct * LANES),
        name=f"forecast_members_{group}",
    )(ids, flow5, nu5, before, after, held, *done)


def gram_kernel(ids, owner, order, keep, other, observed, variance, gh):
    slab, member = ids[0], ids[1]
    count, tiles, members = keep.shape[:3]
    for k in range(count):
        batch = order[2 * k + member]
        mine = owner[batch] == slab
        out = gh.at[k]

        @pl.when(jnp.logical_not(mine))
        def _():
            out[...] = jnp.zeros(out.shape, F32)

        @pl.when(mine)
        def _():
            pair = jnp.zeros(out.shape, F32)
            for t in range(tiles):
                a, b = keep[k, t], other[k, t]
                prior = jnp.concatenate(
                    [jnp.where(member == 0, a, b), jnp.where(member == 0, b, a)], axis=0
                )
                mean = jnp.sum(prior, axis=0, keepdims=True) / (2 * members)
                anomaly = prior - mean
                scaled = anomaly / variance[batch, :, pl.ds(t * LANES, LANES)]
                misfit = observed[batch, :, pl.ds(t * LANES, LANES)] - mean
                pair += lax.dot_general(
                    scaled,
                    jnp.concatenate([anomaly, misfit], axis=0),
                    (((1,), (1,)), ((), ())),
                    precision=HIGH,
                    preferred_element_type=F32,
                )
            h = lax.dot_general(
                pair[:, 2 * members :], rotation(2 * members), (((1,), (0,)), ((), ())),
                precision=HIGH, preferred_element_type=F32,
            )
            out[...] = jnp.concatenate([pair[:, : 2 * members], h], axis=1)


def gram(ids, owner, order, keep, other, observed, variance):
    count, _, members, _ = keep.shape
    total = 2 * members
    smem = pl.BlockSpec(memory_space=pltpu.SMEM)
    vmem = pl.BlockSpec(memory_space=pltpu.VMEM)
    return pl.pallas_call(
        gram_kernel,
        out_shape=jax.ShapeDtypeStruct((count, total, 2 * total), F32),
        in_specs=[smem] * 3 + [vmem] * 4,
        out_specs=vmem,
        compiler_params=params(12),
        name="gram",
    )(ids, owner, order, keep, other, observed, variance[:, None, :])


def rotation(size):
    step = size**-0.5
    row = lax.broadcasted_iota(jnp.int32, (size, size), 0)
    col = lax.broadcasted_iota(jnp.int32, (size, size), 1)
    v_row = (row == size - 1).astype(F32) - step
    v_col = (col == size - 1).astype(F32) - step
    return (row == col).astype(F32) - v_row * v_col / (1.0 - step)


def split3(x):
    high = x.astype(BF16)
    rest = x - high.astype(F32)
    mid = rest.astype(BF16)
    return high, mid, (rest - mid.astype(F32)).astype(BF16)


def dot32(x, y, lhs, rhs):
    parts = split3(x)
    m = x.shape[1 - lhs]
    out = None
    for k, right in enumerate(split3(y)):
        left = jnp.concatenate(parts[: 3 - k], axis=1 - lhs)
        each = lax.dot_general(
            left, right, (((lhs,), (rhs,)), ((), ())), preferred_element_type=F32
        )
        for j in reversed(range(3 - k)):
            piece = each[j * m : (j + 1) * m]
            out = piece if out is None else out + piece
    return out


def total(terms):
    while len(terms) > 1:
        terms = [x + y for x, y in zip(terms[::2], terms[1::2])]
    return terms[0]


def eliminate(a_ref, b_ref, scaled, rows_a, rows_b):
    groups = a_ref.shape[0] // SUB
    wide = (SUB, LANES)
    sub = lax.broadcasted_iota(jnp.int32, wide, 0)
    part = [pl.ds(g * SUB, SUB) for g in range(groups)]

    def column(x, k):
        return jnp.broadcast_to(x[:, k : k + 1], wide)

    def row(x, k):
        return jnp.broadcast_to(x[k : k + 1, :], wide)

    def less(x, scale, first, second, n):
        return x - scale * (first * n[0] + second * n[1])

    a_next, b_next = a_ref[part[0], :], b_ref[part[0], :]
    c = [column(a_next, k) for k in range(SUB)]
    kk, kl, ll = row(c[0], 0), row(c[1], 0), row(c[1], 1)
    for p in range(groups):
        c = [(x, x) for x in c]
        pa, pb = (a_next, a_next), (b_next, b_next)
        after = p + 1 if p + 1 < groups else None
        if after:
            a_next, b_next = a_ref[part[after], :], b_ref[part[after], :]
            e = [column(a_next, p * SUB + k) for k in range(SUB)]
        ahead = None
        for k in range(0, SUB, 2):
            (fk, ck), (fl, cl) = c[k], c[k + 1]
            scale = pl.reciprocal(kk * ll - kl * kl, approx=True)

            def pivot_rows(x, k=k, kk=kk, kl=kl, ll=ll):
                u, w = row(x, k), row(x, k + 1)
                return ll * u - kl * w, kk * w - kl * u

            def inside(x, n, k=k, ck=ck, cl=cl, scale=scale):
                rest = less(x[1], scale, ck, cl, n)
                done = jnp.where(
                    sub == k, scale * n[0], jnp.where(sub == k + 1, scale * n[1], rest)
                )
                return rest, done

            n = {j: pivot_rows(c[j][0]) for j in range(k + 2, SUB)}
            if k + 2 < SUB:
                here = (k + 2, k + 3)
                left, right = ([row(x, i) for i in here] for x in (fk, fl))
                first, second = c[k + 2][0], c[k + 3][0]
                blocks = (
                    less(row(first, k + 2), scale, left[0], right[0], n[k + 2]),
                    less(row(second, k + 2), scale, left[0], right[0], n[k + 3]),
                    less(row(second, k + 3), scale, left[1], right[1], n[k + 3]),
                )
            if ahead:
                upper, lower = ahead
                m = [pivot_rows(x) for x in upper]
                if k + 2 == SUB:
                    left, right = ([row(x, i) for i in (0, 1)] for x in (e[k], e[k + 1]))
                    blocks = (
                        less(row(lower[0], 0), scale, left[0], right[0], m[0]),
                        less(row(lower[1], 0), scale, left[0], right[0], m[1]),
                        less(row(lower[1], 1), scale, left[1], right[1], m[1]),
                    )
                upper = [less(x, scale, fk, fl, y) for x, y in zip(upper, m)]
                lower = [less(x, scale, e[k], e[k + 1], y) for x, y in zip(lower, m)]
                ahead = upper, lower
            for j in range(k + 2, SUB):
                c[j] = inside(c[j], n[j])
                if after:
                    e[j] = less(e[j], scale, e[k], e[k + 1], n[j])
            if after:
                m = pivot_rows(pa[0])
                pa = inside(pa, m)
                a_next = less(a_next, scale, e[k], e[k + 1], m)
            m = pivot_rows(pb[0])
            pb = inside(pb, m)
            if after:
                b_next = less(b_next, scale, e[k], e[k + 1], m)
                if k + 2 == SUB - 2 * AHEAD:
                    ahead = [
                        [column(x, (p + 1) * SUB + j) for j in range(SUB)] for x in (pa[0], a_next)
                    ]
            kk, kl, ll = blocks
        pa, pb = pa[1], pb[1]
        scaled[part[p], :] = pb
        if after:
            c = ahead[1]
            b_ref[part[after], :] = b_next
        if p + 2 < groups:
            here = p % 2
            rows_a[here] = pa
            rows_b[here] = pb
            ra = [rows_a[here, pl.ds(k, SUB, stride=0), :] for k in range(SUB)]
            rb = [rows_b[here, pl.ds(k, SUB, stride=0), :] for k in range(SUB)]
            for g in range(p + 2, groups):
                old = a_ref[part[g], :]
                cols = [column(old, p * SUB + k) for k in range(SUB)]
                a_ref[part[g], :] = old - total([x * y for x, y in zip(cols, ra)])
                b_ref[part[g], :] = b_ref[part[g], :] - total([x * y for x, y in zip(cols, rb)])


def chain_kernel(ids, mine, other, out, a, b, scaled, rows_a, rows_b):
    member = ids[1]
    count, size, width = mine.shape
    row = lax.broadcasted_iota(jnp.int32, (size, width), 0)
    lane = lax.broadcasted_iota(jnp.int32, (size, width), 1)
    diagonal = jnp.where(row == lane, size - 1.0, 0.0)

    def step(position, vt):
        k = lax.div(position, 2)
        gh = jnp.where(lax.rem(position, 2) == member, mine[k], other[k])
        zt = jnp.where(row == size - 1, 0.0, vt)
        s = dot32(zt[:, :size], gh, 1, 0)
        v = vt[:, :size]
        t = dot32(s[:, :size], jnp.concatenate([v, v], axis=0), 1, 1)
        a[...] = jnp.where(lane == size - 1, 0.0, t) + diagonal
        b[...] = jnp.where(lane < size, zt, s - t)
        eliminate(a, b, scaled, rows_a, rows_b)
        return vt + dot32(b[...], scaled[...], 0, 0)[size:]

    unit = rotation(size)
    start = jnp.concatenate([unit, jnp.zeros_like(unit)], axis=1)
    vt = lax.fori_loop(0, 2 * count, step, start)
    w = dot32(unit, vt[:, :size], 1, 0)
    half = size // 2
    first, second = w[:, :half], w[:, half:]
    w = jnp.concatenate(
        [jnp.where(member == 0, first, second), jnp.where(member == 0, second, first)], axis=1
    )
    high = w.astype(BF16).astype(F32)
    low = w - high
    out[...] = jnp.concatenate(
        [jnp.concatenate([high, high], axis=1), jnp.concatenate([low, jnp.zeros_like(low)], axis=1)],
        axis=0,
    )


def chain(ids, mine, other):
    size = mine.shape[1]
    rows = pltpu.VMEM((2, SUB, LANES), F32)
    square = pltpu.VMEM((size, 2 * size), F32)
    return pl.pallas_call(
        chain_kernel,
        out_shape=jax.ShapeDtypeStruct((2 * size, 2 * size), F32),
        in_specs=[SMEM] + [VMEM] * 2,
        out_specs=VMEM,
        scratch_shapes=[square, square, square, rows, rows],
        compiler_params=params(12),
        name="chain",
    )(ids, mine, other)


def apply_kernel(ids, w_ref, own0, other0, own1, other1, out, held, sems):
    size = w_ref.shape[0] // 2
    rows, nct = own0.shape[:2]
    half = nct // 2
    first_tile = ids[1] * half
    weights = w_ref[...].astype(BF16)
    flat = held.reshape(held.size // LANES, LANES)

    for field, sources in enumerate(((own0, other0), (own1, other1))):

        def copy(block, slot, field=field):
            return pltpu.make_async_copy(held.at[slot], out.at[:, field, block], sems.at[slot])

        def step(block, carry, field=field, sources=sources, copy=copy):
            slot = lax.rem(block, 2)

            @pl.when((block >= 2) if field == 0 else (block >= 0))
            def _():
                copy(block, slot).wait()

            base = slot * size * half * SUB
            for r in range(SUB):
                parts = [
                    jnp.concatenate(
                        [src[block * SUB + r, first_tile + ct] for ct in range(half)], axis=1
                    )
                    for src in sources
                ]
                high = [x.astype(BF16) for x in parts]
                low = [(x - y.astype(F32)).astype(BF16) for x, y in zip(parts, high)]
                stacked = jnp.concatenate([*high, *low], axis=0)
                result = jnp.dot(weights, stacked, preferred_element_type=F32)
                result = result[:size] + result[size:]
                for ct in range(half):
                    flat[pl.ds(base + ct * SUB + r, size, stride=half * SUB), :] = result[
                        :, ct * LANES : (ct + 1) * LANES
                    ]
            copy(block, slot).start()
            return carry

        lax.fori_loop(0, rows // SUB, step, 0)
    for slot in range(2):
        copy(0, slot).wait()


def apply(ids, weights, own0, other0, own1, other1):
    rows, nct, members, _ = own0.shape
    size = 2 * members
    half = nct // 2
    r8 = rows // SUB
    return pl.pallas_call(
        apply_kernel,
        out_shape=jax.ShapeDtypeStruct((size, 2, r8, half, SUB, LANES), F32),
        in_specs=[SMEM] + [VMEM] * 5,
        out_specs=pl.BlockSpec(memory_space=pl.ANY),
        scratch_shapes=[
            pltpu.VMEM((2, size, half, SUB, LANES), F32),
            pltpu.SemaphoreType.DMA((2,)),
        ],
        compiler_params=params(12),
        name="apply",
    )(ids, weights, own0, other0, own1, other1)


def body(state, courant, diffusion, obs_cells, obs_owner, batch_order, obs_values, obs_error):
    slab = lax.axis_index("space")
    member = lax.axis_index("member")
    space = lax.axis_size("space")
    ids = jnp.stack([slab, member]).astype(jnp.int32)
    pairs = [
        [(i + d, i + 1 - d) for i in range(start, space - 1, 2) for d in (0, 1)] for start in (0, 1)
    ]
    swap = [(0, 1), (1, 0)]

    state6, flow5, nu5 = tiled(state), tiled(courant), tiled(diffusion)
    edges = pack_edges(state6, flow5, nu5)
    before, after = (lax.ppermute(x, "space", pair) for x, pair in zip(edges, pairs))
    full0, held0, held1 = forecast_inner(state6, flow5, nu5)
    full0, _, held1, keep, away = forecast_edges(
        ids, obs_cells, obs_owner, batch_order, flow5, nu5, before, after, full0, held0, held1
    )
    other = lax.ppermute(away, "member", swap)
    gh = gram(ids, obs_owner, batch_order, keep, other, obs_values, obs_error)

    groups = list(range(held1.shape[0]))
    field1 = ()
    bit = 1
    while bit < space:
        received = lax.ppermute(gh, "space", [(i, i ^ bit) for i in range(space)])
        if groups:
            held1, gh = lax.optimization_barrier((held1, gh))
            field1 = forecast_piece(groups.pop(0), ids, flow5, nu5, before, after, held1, field1)
            received, field1 = lax.optimization_barrier((received, (field1,)))
        gh = gh + received
        bit *= 2
    for group in groups:
        field1 = (forecast_piece(group, ids, flow5, nu5, before, after, held1, field1),)
    (full1,) = field1
    theirs = lax.ppermute(gh, "member", swap)
    full0, full1, gh, theirs = lax.optimization_barrier((full0, full1, gh, theirs))
    other0 = lax.ppermute(full0, "member", swap)
    other1 = lax.ppermute(full1, "member", swap)
    weights = chain(ids, gh, theirs)
    return untiled(apply(ids, weights, full0, other0, full1, other1))


def solution(mesh):
    placed = (
        P("member", None, "space", None),
        P(None, "space", None),
        P(None, "space", None),
        P(),
        P(),
        P(),
        P(),
        P(),
    )
    return jax.shard_map(
        body,
        mesh=mesh,
        in_specs=placed,
        out_specs=P(None, None, "space", "member"),
        check_vma=False,
    )
```

```python
import functools

import jax
import jax.numpy as jnp
from jax import lax
from jax.experimental import pallas as pl
from jax.experimental.pallas import tpu as pltpu
from jax.sharding import PartitionSpec as P

HIGH = lax.Precision.HIGHEST
F32 = jnp.float32
BF16 = jnp.bfloat16
LANES = 128
SUB = 8
AHEAD = 1
PACK = 8


def params(mib):
    return pltpu.CompilerParams(vmem_limit_bytes=mib * 1024 * 1024)


def unrolled(count, most):
    return max(d for d in range(1, most + 1) if count % d == 0)


def rows_loop(count, most, fn):
    step = unrolled(count, most)

    def run(i, carry):
        for u in range(step):
            fn(i * step + u)
        return carry

    lax.fori_loop(0, count // step, run, 0)


def tiled(array):
    *lead, rows, cols = array.shape
    n = len(lead)
    split = array.reshape(*lead, rows // SUB, SUB, cols // LANES, LANES)
    return jnp.transpose(split, (*range(n), n, n + 2, n + 1, n + 3))


def untiled(array):
    *lead, r8, ct, sub, lanes = array.shape
    n = len(lead)
    back = jnp.transpose(array, (*range(n), n, n + 2, n + 1, n + 3))
    return back.reshape(*lead, r8 * sub, ct * lanes)


def pack_kernel(state, flow, nu, first, second, edge_flow, edge_nu, sems):
    members, fields, r8, nct = state.shape[:4]
    even = lax.rem(lax.axis_index("space"), 2) == 0

    def pack(above, below):
        sides = ((above, r8 - 1, (SUB - 2, SUB - 1)), (below, 0, (0, 1)))
        copies = []

        def copy(src, dst):
            copies.append(pltpu.make_async_copy(src, dst, sems.at[len(copies)]))

        for side, (msg, block, rows) in enumerate(sides):
            copy(flow.at[:, block], edge_flow.at[side])
            copy(nu.at[:, block], edge_nu.at[side])
        for msg, block, rows in sides:
            for field in range(fields):
                for ct in range(nct):
                    for at, row in enumerate(rows):
                        copy(
                            state.at[:, field, block, ct, row, :],
                            msg.at[ct, pl.ds((field * 2 + at) * members, members), :],
                        )
        for one in copies:
            one.start()
        for one in copies[:4]:
            one.wait()
        for side, (msg, block, rows) in enumerate(sides):
            edge = (SUB - 1, 0)[side]
            for ct in range(nct):
                numbers = [edge_flow[side, k, ct, edge : edge + 1, :] for k in range(2)]
                numbers += [edge_nu[side, k, ct, edge : edge + 1, :] for k in range(fields)]
                numbers.append(jnp.zeros((PACK - 2 - fields, LANES), F32))
                msg[ct, pl.ds(2 * fields * members, PACK), :] = jnp.concatenate(numbers, axis=0)
        for one in copies[4:]:
            one.wait()

    @pl.when(even)
    def _():
        pack(first, second)

    @pl.when(jnp.logical_not(even))
    def _():
        pack(second, first)


class Chosen:
    def __init__(self, flag, yes, no):
        self.flag, self.yes, self.no, self.shape = flag, yes, no, yes.shape

    def __getitem__(self, at):
        return jnp.where(self.flag, self.yes[at], self.no[at])


def neighbours(slab, first, second):
    even = lax.rem(slab, 2) == 0
    return Chosen(even, second, first), Chosen(even, first, second)


def pack_edges(state6, flow5, nu5):
    members, fields, r8, nct = state6.shape[:4]
    msg = jax.ShapeDtypeStruct((nct, 2 * fields * members + PACK, LANES), F32)
    edge = pltpu.VMEM((2, 2, nct, SUB, LANES), F32)
    return pl.pallas_call(
        pack_kernel,
        out_shape=[msg] * 2,
        in_specs=[pl.BlockSpec(memory_space=pl.ANY)] * 3,
        out_specs=[pl.BlockSpec(memory_space=pltpu.VMEM)] * 2,
        scratch_shapes=[edge, edge, pltpu.SemaphoreType.DMA((4 + 4 * fields * nct,))],
        compiler_params=params(56),
        name="pack_edges",
    )(state6, flow5, nu5)


PAD = SUB


def stencil_coefs(flow_x, flow_y, nu, col, width):
    east = nu - jnp.minimum(flow_x, 0.0)
    west = nu + jnp.maximum(flow_x, 0.0)
    north = nu - jnp.minimum(flow_y, 0.0)
    south = nu + jnp.maximum(flow_y, 0.0)
    centre = 1.0 - (east + west + north + south)
    south = jnp.where(col == 0, 0.0, south)
    north = jnp.where(col == width - 1, 0.0, north)
    return centre, west, east, south, north


def fill_coefs(coef, field, flow, nu, blocks, before=None, after=None):
    _, r8, nct = flow.shape[:3]
    width = nct * LANES
    for ct in range(nct):
        for first, count in blocks:
            shape = (count * SUB, LANES)
            col = lax.broadcasted_iota(jnp.int32, shape, 1) + ct * LANES
            part = pl.ds(first, count)
            numbers = (flow[0, part, ct], flow[1, part, ct], nu[field, part, ct])
            numbers = [x.reshape(shape) for x in numbers]
            for k, value in enumerate(stencil_coefs(*numbers, col, width)):
                coef[k, ct, pl.ds(PAD + first * SUB, count * SUB), :] = value
        for msg, row in ((before, PAD - 1), (after, PAD + r8 * SUB)):
            if msg is not None:
                col = lax.broadcasted_iota(jnp.int32, (1, LANES), 1) + ct * LANES
                base = msg.shape[1] - PACK
                numbers = [msg[ct, pl.ds(base + k, 1), :] for k in (0, 1, 2 + field)]
                for k, value in enumerate(stencil_coefs(*numbers, col, width)):
                    coef[k, ct, pl.ds(row, 1), :] = value


def stencil(mid, west, east, weights):
    nct = len(mid)
    lane = lax.broadcasted_iota(jnp.int32, (SUB, LANES), 1)
    right = [pltpu.roll(x, 1, 1) for x in mid]
    left = [pltpu.roll(x, LANES - 1, 1) for x in mid]
    out = []
    for ct in range(nct):
        south = jnp.where(lane == 0, right[(ct - 1) % nct], right[ct])
        north = jnp.where(lane == LANES - 1, left[(ct + 1) % nct], left[ct])
        centre, w_w, w_e, w_s, w_n = weights[ct]
        out.append(
            (centre * mid[ct] + w_w * west[ct]) + (w_e * east[ct] + (w_s * south + w_n * north))
        )
    return out


class Rows:
    def __init__(self, held, coef):
        self.nct, _, blocks = held.shape[-5:-2]
        self.room = blocks * SUB
        self.flat = held.reshape(held.size // LANES, LANES)
        self.coef = coef.reshape(coef.size // LANES, LANES)

    def at(self, group, ct, row):
        start = (group * self.nct + ct) * SUB * self.room + PAD + row
        return pl.ds(start, SUB, stride=self.room)

    def load(self, group, row):
        return [self.flat[self.at(group, ct, row), :] for ct in range(self.nct)]

    def weights(self, row):
        return [
            [
                self.coef[pl.ds((k * self.nct + ct) * self.room + PAD + row, SUB, stride=0), :]
                for k in range(5)
            ]
            for ct in range(self.nct)
        ]


def group_steps(group, held, between, coef, put, edges):
    groups, nct, _, blocks = held.shape[:4]
    room = blocks * SUB
    source = held.reshape(groups, nct, SUB, room, LANES)
    middle = between.reshape(nct, SUB, room, LANES)

    def block_step(block, load, store):
        at = PAD + block * SUB
        weights = [[coef[k, ct, pl.ds(at, SUB), :] for k in range(5)] for ct in range(nct)]
        for m in range(SUB):
            mid, west, east = [
                [load(ct, m, pl.ds(at + off, SUB)) for ct in range(nct)] for off in (0, -1, 1)
            ]
            for ct, value in enumerate(stencil(mid, west, east, weights)):
                store(block, ct, m, value)

    def keep(block, ct, m, value):
        middle[ct, m, pl.ds(PAD + block * SUB, SUB), :] = value

    for block in range(blocks - 2):
        block_step(block, lambda ct, m, rows: source[group, ct, m, rows, :], keep)
    if edges:
        field, inner = Rows(held, coef), Rows(between, coef)
        for row in (-1, (blocks - 2) * SUB):
            around = [field.load(group, row + off) for off in (0, -1, 1)]
            for ct, value in enumerate(stencil(*around, field.weights(row))):
                inner.flat[inner.at(0, ct, row), :] = value
    for block in range(blocks - 2):
        block_step(block, lambda ct, m, rows: middle[ct, m, rows, :], put)


def held_shape(members, nct, r8):
    return (members // SUB, nct, SUB, r8 + 2, SUB, LANES)


def cost(cells):
    return pl.CostEstimate(flops=40 * cells, bytes_accessed=8 * cells, transcendentals=0)


SMEM = pl.BlockSpec(memory_space=pltpu.SMEM)
VMEM = pl.BlockSpec(memory_space=pltpu.VMEM)


def inner_kernel(state, flow, nu, full, held0, held1, between, coef, sems):
    groups, nct, _, blocks = held0.shape[:4]
    members = groups * SUB
    r8 = blocks - 2

    def copies(field, held, group):
        return [
            pltpu.make_async_copy(
                state.at[pl.ds(group * SUB, SUB), field, :, ct],
                held.at[group, ct, :, pl.ds(1, r8)],
                sems.at[field, group, ct],
            )
            for ct in range(nct)
        ]

    for group in range(groups):
        for one in copies(0, held0, group):
            one.start()
    fill_coefs(coef, 0, flow, nu, [(0, r8)])
    flat = full.reshape(full.size // LANES, LANES)

    def run(group, carry):
        for one in copies(0, held0, group):
            one.wait()
        for one in copies(1, held1, group):
            one.start()

        def put(block, ct, m, value):
            start = (block * SUB * nct + ct) * members + group * SUB + m
            flat[pl.ds(start, SUB, stride=nct * members), :] = value

        group_steps(group, held0, between, coef, put, False)
        return carry

    lax.fori_loop(0, groups, run, 0)
    for group in range(groups):
        for one in copies(1, held1, group):
            one.wait()


def forecast_inner(state6, flow5, nu5):
    members, _, r8, nct = state6.shape[:4]
    held = held_shape(members, nct, r8)
    return pl.pallas_call(
        inner_kernel,
        out_shape=[
            jax.ShapeDtypeStruct((r8 * SUB, nct, members, LANES), F32),
            jax.ShapeDtypeStruct(held, F32),
            jax.ShapeDtypeStruct(held, F32),
        ],
        in_specs=[pl.BlockSpec(memory_space=pl.ANY)] + [VMEM] * 2,
        out_specs=[VMEM] * 3,
        scratch_shapes=[
            pltpu.VMEM(held[1:], F32),
            pltpu.VMEM((5, nct, (r8 + 2) * SUB, LANES), F32),
            pltpu.SemaphoreType.DMA((2, held[0], nct)),
        ],
        compiler_params=params(34),
        cost_estimate=cost(members * r8 * SUB * nct * LANES),
        name="forecast_inner",
    )(state6, flow5, nu5)


def edge_kernel(
    ids, cells, owner, order, flow, nu, before, after, full_in, held0_in, held1_in,
    full, held0, held1, keep, away, coef
):
    groups, nct, _, blocks = held0.shape[:4]
    members = groups * SUB
    r8 = blocks - 2
    rows = r8 * SUB
    slab, member = ids[0], ids[1]
    before, after = neighbours(slab, before, after)

    for field, held in ((0, held0), (1, held1)):
        view = Rows(held, coef)
        for ct in range(nct):
            for group in range(groups):
                for k in range(2):
                    part = pl.ds((2 * field + k) * members + group * SUB, SUB)
                    view.flat[view.at(group, ct, k - 2), :] = before[ct, part, :]
                    view.flat[view.at(group, ct, rows + k), :] = after[ct, part, :]

    fill_coefs(coef, 0, flow, nu, [(0, 1), (r8 - 1, 1)], before, after)
    view = Rows(held0, coef)
    for first in (0, rows - 2):
        for group in range(groups):
            old = {r: view.load(group, r) for r in range(first - 2, first + 4)}
            one = {
                r: stencil(old[r], old[r - 1], old[r + 1], view.weights(r))
                for r in range(first - 1, first + 3)
            }
            for r in range(first, first + 2):
                new = stencil(one[r], one[r - 1], one[r + 1], view.weights(r))
                for ct, value in enumerate(new):
                    full[r, ct, pl.ds(group * SUB, SUB), :] = value

    nobs = cells.shape[1]
    tiles = full.reshape(rows * nct, members, LANES)
    lane = lax.broadcasted_iota(jnp.int32, (members, LANES), 1)

    def gather_tile(batch, tile):
        acc = jnp.zeros((members, LANES), F32)
        for o in range(LANES):
            cell = cells[batch, tile * LANES + o]
            tile_at = lax.shift_right_logical(cell, LANES.bit_length() - 1)
            moved = pltpu.roll(tiles[tile_at], (o - cell) & (LANES - 1), 1)
            acc = jnp.where(lane == o, moved, acc)
        return acc

    def gather_batch(position, carry):
        batch = order[position]
        mine = owner[batch] == slab
        kept = lax.rem(position, 2) == member
        at = lax.div(position, 2)

        for out, wanted in ((keep, kept), (away, jnp.logical_not(kept))):

            @pl.when(jnp.logical_and(wanted, jnp.logical_not(mine)))
            def _(out=out):
                out[at] = jnp.zeros(out.shape[1:], F32)

        @pl.when(mine)
        def _():
            def one(tile, carry):
                values = gather_tile(batch, tile)

                @pl.when(kept)
                def _():
                    keep[at, tile] = values

                @pl.when(jnp.logical_not(kept))
                def _():
                    away[at, tile] = values

                return carry

            lax.fori_loop(0, nobs // LANES, one, 0)

        return carry

    lax.fori_loop(0, order.shape[0], gather_batch, 0)


def forecast_edges(ids, cells, owner, order, flow5, nu5, before, after, full, held0, held1):
    members = full.shape[2]
    nct, _, blocks = held0.shape[1:4]
    nb, nobs = cells.shape
    picks = jax.ShapeDtypeStruct((nb // 2, nobs // LANES, members, LANES), F32)
    same = [jax.ShapeDtypeStruct(x.shape, F32) for x in (full, held0, held1)]
    return pl.pallas_call(
        edge_kernel,
        out_shape=[*same, picks, picks],
        in_specs=[SMEM] * 4 + [VMEM] * 7,
        out_specs=[VMEM] * 5,
        input_output_aliases={8: 0, 9: 1, 10: 2},
        scratch_shapes=[pltpu.VMEM((5, nct, blocks * SUB, LANES), F32)],
        compiler_params=params(6),
        cost_estimate=cost(members * SUB * nct * LANES),
        name="forecast_edges",
    )(ids, cells, owner, order, flow5, nu5, before, after, full, held0, held1)


def piece_kernel(group, ids, flow, nu, first, second, held, *rest):
    full, between, coef = rest[-3:]
    rows, nct, members = full.shape[:3]
    flat = full.reshape(full.size // LANES, LANES)
    before, after = neighbours(ids[0], first, second)
    fill_coefs(coef, 1, flow, nu, [(0, rows // SUB)], before, after)

    def put(block, ct, m, value):
        start = (block * SUB * nct + ct) * members + group * SUB + m
        flat[pl.ds(start, SUB, stride=nct * members), :] = value

    group_steps(group, held, between, coef, put, True)


def forecast_piece(group, ids, flow5, nu5, before, after, held, done):
    groups, nct, _, blocks = held.shape[:4]
    rows = (blocks - 2) * SUB
    return pl.pallas_call(
        functools.partial(piece_kernel, group),
        out_shape=jax.ShapeDtypeStruct((rows, nct, groups * SUB, LANES), F32),
        in_specs=[SMEM] + [VMEM] * (5 + len(done)),
        out_specs=VMEM,
        input_output_aliases={6: 0} if done else {},
        scratch_shapes=[
            pltpu.VMEM(held.shape[1:], F32),
            pltpu.VMEM((5, nct, blocks * SUB, LANES), F32),
        ],
        compiler_params=params(6),
        cost_estimate=cost(SUB * rows * nct * LANES),
        name=f"forecast_members_{group}",
    )(ids, flow5, nu5, before, after, held, *done)


def gram_kernel(ids, owner, order, keep, other, observed, variance, gh):
    slab, member = ids[0], ids[1]
    count, tiles, members = keep.shape[:3]
    for k in range(count):
        batch = order[2 * k + member]
        mine = owner[batch] == slab
        out = gh.at[k]

        @pl.when(jnp.logical_not(mine))
        def _():
            out[...] = jnp.zeros(out.shape, F32)

        @pl.when(mine)
        def _():
            pair = jnp.zeros(out.shape, F32)
            for t in range(tiles):
                a, b = keep[k, t], other[k, t]
                prior = jnp.concatenate(
                    [jnp.where(member == 0, a, b), jnp.where(member == 0, b, a)], axis=0
                )
                mean = jnp.sum(prior, axis=0, keepdims=True) / (2 * members)
                anomaly = prior - mean
                scaled = anomaly / variance[batch, :, pl.ds(t * LANES, LANES)]
                misfit = observed[batch, :, pl.ds(t * LANES, LANES)] - mean
                pair += lax.dot_general(
                    scaled,
                    jnp.concatenate([anomaly, misfit], axis=0),
                    (((1,), (1,)), ((), ())),
                    precision=HIGH,
                    preferred_element_type=F32,
                )
            h = lax.dot_general(
                pair[:, 2 * members :], rotation(2 * members), (((1,), (0,)), ((), ())),
                precision=HIGH, preferred_element_type=F32,
            )
            out[...] = jnp.concatenate([pair[:, : 2 * members], h], axis=1)


def gram(ids, owner, order, keep, other, observed, variance):
    count, _, members, _ = keep.shape
    total = 2 * members
    smem = pl.BlockSpec(memory_space=pltpu.SMEM)
    vmem = pl.BlockSpec(memory_space=pltpu.VMEM)
    return pl.pallas_call(
        gram_kernel,
        out_shape=jax.ShapeDtypeStruct((count, total, 2 * total), F32),
        in_specs=[smem] * 3 + [vmem] * 4,
        out_specs=vmem,
        compiler_params=params(12),
        name="gram",
    )(ids, owner, order, keep, other, observed, variance[:, None, :])


def rotation(size):
    step = size**-0.5
    row = lax.broadcasted_iota(jnp.int32, (size, size), 0)
    col = lax.broadcasted_iota(jnp.int32, (size, size), 1)
    v_row = (row == size - 1).astype(F32) - step
    v_col = (col == size - 1).astype(F32) - step
    return (row == col).astype(F32) - v_row * v_col / (1.0 - step)


def split3(x):
    high = x.astype(BF16)
    rest = x - high.astype(F32)
    mid = rest.astype(BF16)
    return high, mid, (rest - mid.astype(F32)).astype(BF16)


def dot32(x, y, lhs, rhs):
    parts = split3(x)
    m = x.shape[1 - lhs]
    out = None
    for k, right in enumerate(split3(y)):
        left = jnp.concatenate(parts[: 3 - k], axis=1 - lhs)
        each = lax.dot_general(
            left, right, (((lhs,), (rhs,)), ((), ())), preferred_element_type=F32
        )
        for j in reversed(range(3 - k)):
            piece = each[j * m : (j + 1) * m]
            out = piece if out is None else out + piece
    return out


def total(terms):
    while len(terms) > 1:
        terms = [x + y for x, y in zip(terms[::2], terms[1::2])]
    return terms[0]


def eliminate(a_ref, b_ref, scaled, rows_a, rows_b):
    groups = a_ref.shape[0] // SUB
    wide = (SUB, LANES)
    sub = lax.broadcasted_iota(jnp.int32, wide, 0)
    part = [pl.ds(g * SUB, SUB) for g in range(groups)]

    def column(x, k):
        return jnp.broadcast_to(x[:, k : k + 1], wide)

    def row(x, k):
        return jnp.broadcast_to(x[k : k + 1, :], wide)

    def less(x, scale, first, second, n):
        return x - scale * (first * n[0] + second * n[1])

    a_next, b_next = a_ref[part[0], :], b_ref[part[0], :]
    c = [column(a_next, k) for k in range(SUB)]
    kk, kl, ll = row(c[0], 0), row(c[1], 0), row(c[1], 1)
    for p in range(groups):
        c = [(x, x) for x in c]
        pa, pb = (a_next, a_next), (b_next, b_next)
        after = p + 1 if p + 1 < groups else None
        if after:
            a_next, b_next = a_ref[part[after], :], b_ref[part[after], :]
            e = [column(a_next, p * SUB + k) for k in range(SUB)]
        ahead = None
        for k in range(0, SUB, 2):
            (fk, ck), (fl, cl) = c[k], c[k + 1]
            scale = pl.reciprocal(kk * ll - kl * kl, approx=True)

            def pivot_rows(x, k=k, kk=kk, kl=kl, ll=ll):
                u, w = row(x, k), row(x, k + 1)
                return ll * u - kl * w, kk * w - kl * u

            def inside(x, n, k=k, ck=ck, cl=cl, scale=scale):
                rest = less(x[1], scale, ck, cl, n)
                done = jnp.where(
                    sub == k, scale * n[0], jnp.where(sub == k + 1, scale * n[1], rest)
                )
                return rest, done

            n = {j: pivot_rows(c[j][0]) for j in range(k + 2, SUB)}
            if k + 2 < SUB:
                here = (k + 2, k + 3)
                left, right = ([row(x, i) for i in here] for x in (fk, fl))
                first, second = c[k + 2][0], c[k + 3][0]
                blocks = (
                    less(row(first, k + 2), scale, left[0], right[0], n[k + 2]),
                    less(row(second, k + 2), scale, left[0], right[0], n[k + 3]),
                    less(row(second, k + 3), scale, left[1], right[1], n[k + 3]),
                )
            if ahead:
                upper, lower = ahead
                m = [pivot_rows(x) for x in upper]
                if k + 2 == SUB:
                    left, right = ([row(x, i) for i in (0, 1)] for x in (e[k], e[k + 1]))
                    blocks = (
                        less(row(lower[0], 0), scale, left[0], right[0], m[0]),
                        less(row(lower[1], 0), scale, left[0], right[0], m[1]),
                        less(row(lower[1], 1), scale, left[1], right[1], m[1]),
                    )
                upper = [less(x, scale, fk, fl, y) for x, y in zip(upper, m)]
                lower = [less(x, scale, e[k], e[k + 1], y) for x, y in zip(lower, m)]
                ahead = upper, lower
            for j in range(k + 2, SUB):
                c[j] = inside(c[j], n[j])
                if after:
                    e[j] = less(e[j], scale, e[k], e[k + 1], n[j])
            if after:
                m = pivot_rows(pa[0])
                pa = inside(pa, m)
                a_next = less(a_next, scale, e[k], e[k + 1], m)
            m = pivot_rows(pb[0])
            pb = inside(pb, m)
            if after:
                b_next = less(b_next, scale, e[k], e[k + 1], m)
                if k + 2 == SUB - 2 * AHEAD:
                    ahead = [
                        [column(x, (p + 1) * SUB + j) for j in range(SUB)] for x in (pa[0], a_next)
                    ]
            kk, kl, ll = blocks
        pa, pb = pa[1], pb[1]
        scaled[part[p], :] = pb
        if after:
            c = ahead[1]
            b_ref[part[after], :] = b_next
        if p + 2 < groups:
            here = p % 2
            rows_a[here] = pa
            rows_b[here] = pb
            ra = [rows_a[here, pl.ds(k, SUB, stride=0), :] for k in range(SUB)]
            rb = [rows_b[here, pl.ds(k, SUB, stride=0), :] for k in range(SUB)]
            for g in range(p + 2, groups):
                old = a_ref[part[g], :]
                cols = [column(old, p * SUB + k) for k in range(SUB)]
                a_ref[part[g], :] = old - total([x * y for x, y in zip(cols, ra)])
                b_ref[part[g], :] = b_ref[part[g], :] - total([x * y for x, y in zip(cols, rb)])


def chain_kernel(ids, mine, other, out, a, b, scaled, rows_a, rows_b):
    member = ids[1]
    count, size, width = mine.shape
    row = lax.broadcasted_iota(jnp.int32, (size, width), 0)
    lane = lax.broadcasted_iota(jnp.int32, (size, width), 1)
    diagonal = jnp.where(row == lane, size - 1.0, 0.0)

    def step(position, vt):
        k = lax.div(position, 2)
        gh = jnp.where(lax.rem(position, 2) == member, mine[k], other[k])
        zt = jnp.where(row == size - 1, 0.0, vt)
        s = dot32(zt[:, :size], gh, 1, 0)
        v = vt[:, :size]
        t = dot32(s[:, :size], jnp.concatenate([v, v], axis=0), 1, 1)
        a[...] = jnp.where(lane == size - 1, 0.0, t) + diagonal
        b[...] = jnp.where(lane < size, zt, s - t)
        eliminate(a, b, scaled, rows_a, rows_b)
        return vt + dot32(b[...], scaled[...], 0, 0)[size:]

    unit = rotation(size)
    start = jnp.concatenate([unit, jnp.zeros_like(unit)], axis=1)
    vt = lax.fori_loop(0, 2 * count, step, start)
    w = dot32(unit, vt[:, :size], 1, 0)
    half = size // 2
    first, second = w[:, :half], w[:, half:]
    w = jnp.concatenate(
        [jnp.where(member == 0, first, second), jnp.where(member == 0, second, first)], axis=1
    )
    high = w.astype(BF16).astype(F32)
    low = w - high
    out[...] = jnp.concatenate(
        [jnp.concatenate([high, high], axis=1), jnp.concatenate([low, jnp.zeros_like(low)], axis=1)],
        axis=0,
    )


def chain(ids, mine, other):
    size = mine.shape[1]
    rows = pltpu.VMEM((2, SUB, LANES), F32)
    square = pltpu.VMEM((size, 2 * size), F32)
    return pl.pallas_call(
        chain_kernel,
        out_shape=jax.ShapeDtypeStruct((2 * size, 2 * size), F32),
        in_specs=[SMEM] + [VMEM] * 2,
        out_specs=VMEM,
        scratch_shapes=[square, square, square, rows, rows],
        compiler_params=params(12),
        name="chain",
    )(ids, mine, other)


def apply_kernel(ids, w_ref, own0, other0, own1, other1, out, held, sems):
    size = w_ref.shape[0] // 2
    rows, nct = own0.shape[:2]
    half = nct // 2
    first_tile = ids[1] * half
    weights = w_ref[...].astype(BF16)
    flat = held.reshape(held.size // LANES, LANES)

    for field, sources in enumerate(((own0, other0), (own1, other1))):

        def copy(block, slot, field=field):
            return pltpu.make_async_copy(held.at[slot], out.at[:, field, block], sems.at[slot])

        def step(block, carry, field=field, sources=sources, copy=copy):
            slot = lax.rem(block, 2)

            @pl.when((block >= 2) if field == 0 else (block >= 0))
            def _():
                copy(block, slot).wait()

            base = slot * size * half * SUB
            for r in range(SUB):
                parts = [
                    jnp.concatenate(
                        [src[block * SUB + r, first_tile + ct] for ct in range(half)], axis=1
                    )
                    for src in sources
                ]
                high = [x.astype(BF16) for x in parts]
                low = [(x - y.astype(F32)).astype(BF16) for x, y in zip(parts, high)]
                stacked = jnp.concatenate([*high, *low], axis=0)
                result = jnp.dot(weights, stacked, preferred_element_type=F32)
                result = result[:size] + result[size:]
                for ct in range(half):
                    flat[pl.ds(base + ct * SUB + r, size, stride=half * SUB), :] = result[
                        :, ct * LANES : (ct + 1) * LANES
                    ]
            copy(block, slot).start()
            return carry

        lax.fori_loop(0, rows // SUB, step, 0)
    for slot in range(2):
        copy(0, slot).wait()


def apply(ids, weights, own0, other0, own1, other1):
    rows, nct, members, _ = own0.shape
    size = 2 * members
    half = nct // 2
    r8 = rows // SUB
    return pl.pallas_call(
        apply_kernel,
        out_shape=jax.ShapeDtypeStruct((size, 2, r8, half, SUB, LANES), F32),
        in_specs=[SMEM] + [VMEM] * 5,
        out_specs=pl.BlockSpec(memory_space=pl.ANY),
        scratch_shapes=[
            pltpu.VMEM((2, size, half, SUB, LANES), F32),
            pltpu.SemaphoreType.DMA((2,)),
        ],
        compiler_params=params(12),
        name="apply",
    )(ids, weights, own0, other0, own1, other1)


def body(state, courant, diffusion, obs_cells, obs_owner, batch_order, obs_values, obs_error):
    slab = lax.axis_index("space")
    member = lax.axis_index("member")
    space = lax.axis_size("space")
    ids = jnp.stack([slab, member]).astype(jnp.int32)
    pairs = [
        [(i + d, i + 1 - d) for i in range(start, space - 1, 2) for d in (0, 1)] for start in (0, 1)
    ]
    swap = [(0, 1), (1, 0)]

    state6, flow5, nu5 = tiled(state), tiled(courant), tiled(diffusion)
    edges = pack_edges(state6, flow5, nu5)
    before, after = (lax.ppermute(x, "space", pair) for x, pair in zip(edges, pairs))
    full0, held0, held1 = forecast_inner(state6, flow5, nu5)
    full0, _, held1, keep, away = forecast_edges(
        ids, obs_cells, obs_owner, batch_order, flow5, nu5, before, after, full0, held0, held1
    )
    other = lax.ppermute(away, "member", swap)
    gh = gram(ids, obs_owner, batch_order, keep, other, obs_values, obs_error)

    groups = list(range(held1.shape[0]))
    field1 = ()
    bit = 1
    while bit < space:
        received = lax.ppermute(gh, "space", [(i, i ^ bit) for i in range(space)])
        if groups:
            held1, gh = lax.optimization_barrier((held1, gh))
            field1 = forecast_piece(groups.pop(0), ids, flow5, nu5, before, after, held1, field1)
            received, field1 = lax.optimization_barrier((received, (field1,)))
        gh = gh + received
        bit *= 2
    for group in groups:
        field1 = (forecast_piece(group, ids, flow5, nu5, before, after, held1, field1),)
    (full1,) = field1
    theirs = lax.ppermute(gh, "member", swap)
    full0, full1, gh, theirs = lax.optimization_barrier((full0, full1, gh, theirs))
    other0 = lax.ppermute(full0, "member", swap)
    other1 = lax.ppermute(full1, "member", swap)
    weights = chain(ids, gh, theirs)
    return untiled(apply(ids, weights, full0, other0, full1, other1))


def solution(mesh):
    placed = (
        P("member", None, "space", None),
        P(None, "space", None),
        P(None, "space", None),
        P(),
        P(),
        P(),
        P(),
        P(),
    )
    return jax.shard_map(
        body,
        mesh=mesh,
        in_specs=placed,
        out_specs=P(None, None, "space", "member"),
        check_vma=False,
    )
```
